128 devices in a mesh: seq: 8 (over z, core), dp: 16 (over x, y).
Axes of the slice: x: 4, y: 4, z: 4, core: 2. Of those that a mesh axis runs over, the one named last changes fastest.
Arguments:
- layer_input: bfloat16 [32768, 1024], P(('dp', 'seq')), may hold values from -6 to 6
- out_grad: bfloat16 [32768, 1024], P(('dp', 'seq')), may hold values from -6 to 6
- lengths: int32 [16, 3], P('dp'), may hold values from 1 to 1365, 2048 in all within a row
- item_owner: int32 [32768, 1], P(('dp', 'seq')), may hold values from 0 to 127; in each aligned block of 256 rows (0 to 255, 256 to 511, ...) at most 4 rows name the same one
- item_row: int32 [32768], P(('dp', 'seq')), may hold values from 0 to 511
- w_attn: bfloat16 [1024, 3072], replicated, may hold values from -0.1875 to 0.1875
- w_gate: bfloat16 [1024, 1024], replicated, may hold values from -0.1875 to 0.1875
- w_out: bfloat16 [1024, 1024], replicated, may hold values from -0.1875 to 0.1875
- emb_table: float32 [65536, 1024], P(('seq', 'dp')), may hold values from -6 to 6
- row_accum: float32 [65536], P(('seq', 'dp')), may hold values from 0.25 to 4
Outputs:
- grad_attn: float32 [1024, 3072], P('dp', 'seq')
- grad_gate: float32 [1024, 1024], P('dp', 'seq')
- grad_out: float32 [1024, 1024], P('dp', 'seq')
- new_table: float32 [65536, 1024], P(('seq', 'dp'))
- new_accum: float32 [65536], P(('seq', 'dp'))
The draws below stay inside these ranges and needn't reach their ends.
Inputs may be any that keep to these rules, and one draw needn't show every extreme that they name: Each group's 3 lengths sum to 2048; the largest is exactly 1365. `item_owner`: among the 256 events of one device at most 4 name one owner, a bound that some block reaches.
All inputs are finite; a program needn't handle non-finite values.
Results may differ from the reference program's by a relative error of at most 0.0092.
Values may be sent and summed in bfloat16 or wider, within the bound.
A program may use at most 128 MiB of HBM per device.

```python
import math
import jax
import jax.numpy as jnp
import numpy as np
from jax import lax

D = 1024
H = 16
DH = 64
TOK_DEV = 256
USERS = 3
ROWS_OWN = 512
PACK = 2048
MAXLEN = 1365
TOKENS = 32768
CAP = 4
N_DP = 16
DEVICES = 128


def place_ends(entries, own_key, smallest, top_value):
    extent = entries.shape
    spot = [jax.random.randint(jax.random.fold_in(own_key, axis), (), 0, extent[axis]) for axis in range(len(extent))]
    entries = entries.at[tuple(spot)].set(smallest)
    longest = extent.index(max(extent))
    spot[longest] = (spot[longest] + 1) % extent[longest]
    return entries.at[tuple(spot)].set(top_value)


def block_scale(own_key, extent, cuts, low, largest):
    gain = 1.0
    for axis_at, blocks in cuts:
        heights = jax.random.uniform(jax.random.fold_in(jax.random.fold_in(own_key, 6), axis_at), (blocks,), jnp.float32, low / len(cuts), largest / len(cuts))
        gain = gain * jnp.repeat(jnp.exp(heights), extent[axis_at] // blocks).reshape((-1,) + (1,) * (len(extent) - 1 - axis_at))
    return gain


def rank_bounds(number_of, lean):
    weights = [(1 << 20) // math.isqrt(rank ** lean) + 1 for rank in range(1, number_of + 1)]
    width = 1 + sum(weights) // (1 << 30)
    return np.cumsum(np.array([max(1, weight // width) for weight in weights]))


def ranked_ids(rng, dims, number_of, slope):
    grid = rank_bounds(number_of, slope)
    pick = jax.random.randint(jax.random.fold_in(rng, 1), dims, 0, int(grid[number_of - 1]))
    grade = jnp.searchsorted(jnp.asarray(grid, jnp.int32), pick, side="right")
    return jax.random.permutation(jax.random.fold_in(rng, 2), number_of)[grade].astype(jnp.int32)


def split_up(amount, total, most, slope):
    loads = [(1 << 20) // math.isqrt(rank ** slope) + 1 for rank in range(2, amount + 1)]
    spare, given = total - most - (amount - 1), [1] * (amount - 1)
    while spare > 0:
        movable = [i for i in range(amount - 1) if given[i] < most]
        mass, remaining = sum([loads[i] for i in movable]), spare
        for i in movable:
            extra = min(most - given[i], max(1, remaining * loads[i] // mass), spare)
            given[i] = given[i] + extra
            spare = spare - extra
    return np.array([most] + given)


def ragged(own_key, amount, total, limit, skew):
    if amount == 2:
        one = jax.random.randint(own_key, (), max(1, total - limit), min(limit, total - 1) + 1)
        return jnp.stack([one, total - one])
    sizes = jnp.asarray(split_up(amount, total, limit, skew), jnp.int32)
    couples = (amount - 1) // 2
    donor, receiver = sizes[1:1 + 2 * couples:2], sizes[2:2 + 2 * couples:2]
    slack = jnp.minimum(donor - 1, limit - receiver)
    shifted = jax.random.randint(jax.random.fold_in(own_key, 1), (couples,), 0, 1 << 20) % (slack + 1)
    sizes = sizes.at[1:1 + 2 * couples:2].set(donor - shifted).at[2:2 + 2 * couples:2].set(receiver + shifted)
    return sizes[jax.random.permutation(jax.random.fold_in(own_key, 2), amount)]


def shared_out(key, own, number, rows, count, top, bound, slope):
    ranking = jax.random.permutation(key, count)
    crowded, usual = shares(count, rows * top, bound, slope, True), shares(count, rows * top, bound, slope, False)
    places = jnp.arange(count)

    def named(sizes, offset_by):
        used = int((sizes > 0).sum())
        fixed = max(1, used // 4)
        shifted = fixed + (places - fixed + offset_by * (used - fixed)) % max(1, count - fixed)
        return jnp.zeros((count,), jnp.int32).at[ranking[jnp.where(places < fixed, places, shifted)]].set(jnp.asarray(sizes, jnp.int32))

    sizes = jnp.where(number % 4 == 0, named(crowded, number // 4), named(usual, number - number // 4 - 1))
    mixed = jax.random.permutation(jax.random.fold_in(own, 3), count)
    giver, sink = mixed[0:count // 2 * 2:2], mixed[1:count // 2 * 2:2]
    margin = jnp.minimum(sizes[giver] - 1, bound - sizes[sink]) // 2
    margin = jnp.where((giver == ranking[0]) | (sink == ranking[0]) | (sizes[sink] == 0), 0, jnp.maximum(margin, 0))
    shifted = jax.random.randint(jax.random.fold_in(own, 4), (count // 2,), 0, 1 << 20) % (margin + 1)
    sizes = sizes.at[giver].add(-shifted).at[sink].add(shifted)
    members = jnp.searchsorted(jnp.cumsum(sizes), jnp.arange(rows * top), side="right").astype(jnp.int32)
    table = members.reshape(top, rows).T
    table = table[jax.random.permutation(jax.random.fold_in(own, 1), rows)]
    offset_by = jax.random.randint(jax.random.fold_in(own, 2), (rows, 1), 0, top)
    return jnp.take_along_axis(table, (jnp.arange(top)[None, :] + offset_by) % top, axis=1)


def shares(amount, total, most, slope, full):
    portions = [(1 << 20) // math.isqrt(standing ** slope) + 1 for standing in range(1, amount + 1)]
    largest = most if full else min(most, max(-(-total // amount), total * portions[0] // sum(portions)))
    least = 1 if total - largest >= amount - 1 else 0
    holding, spare = [largest] + [least] * (amount - 1), total - largest - least * (amount - 1)
    while spare > 0:
        movable = [i for i in range(1, amount) if holding[i] < largest] or [i for i in range(1, amount) if holding[i] < most]
        mass, budget = sum([portions[i] for i in movable]), spare
        for i in movable:
            more = min(most - holding[i], max(1, budget * portions[i] // mass), spare)
            holding[i] = holding[i] + more
            spare = spare - more
    return np.array(holding)


def noise(rng, shape, spread, reach, split=(), kind=jnp.bfloat16):
    entries = jax.random.normal(rng, shape, jnp.float32) * spread
    if len(split) > 0:
        entries = block_scale(rng, shape, split, -0.22, 0.18) * entries
    return jnp.clip(entries, min=-reach, max=reach).astype(kind)


def setup_inputs(seed: int = 0) -> dict:
    keys = jax.random.split(jax.random.key(seed), 11)
    layer_input = noise(keys[0], (TOKENS, D), 1.0, 6.0, ((0, 128),))
    out_grad = noise(keys[1], (TOKENS, D), 1.0, 6.0, ((0, 128),))
    lengths = jax.vmap(lambda own: ragged(own, USERS, PACK, MAXLEN, 2))(jax.random.split(keys[2], N_DP)).reshape((N_DP, USERS)).astype(jnp.int32)
    item_owner_keys = jax.random.split(jax.random.fold_in(keys[3], 1), TOKENS // TOK_DEV)
    item_owner_turns = jax.random.permutation(jax.random.fold_in(keys[3], 3), TOKENS // TOK_DEV)
    item_owner = jax.vmap(lambda own, number: shared_out(jax.random.fold_in(keys[3], 2), own, number, TOK_DEV, DEVICES, 1, CAP, 2))(item_owner_keys, item_owner_turns).reshape((TOKENS, 1))
    item_row = place_ends(ranked_ids(keys[4], (TOKENS,), ROWS_OWN, 2), jax.random.fold_in(keys[4], 3), 0, ROWS_OWN - 1).astype(jnp.int32)
    w_attn = noise(keys[5], (D, 3 * D), D ** -0.5, 0.1875)
    w_gate = noise(keys[6], (D, D), D ** -0.5, 0.1875)
    w_out = noise(keys[7], (D, D), D ** -0.5, 0.1875)
    emb_table = noise(keys[8], (DEVICES * ROWS_OWN, D), 1.0, 6.0, ((0, 128),), jnp.float32)
    row_accum = jnp.clip(jnp.exp(math.log(4.0) - 2.7725887 * jax.random.uniform(keys[9], (DEVICES * ROWS_OWN,), jnp.float32) ** block_scale(keys[9], (DEVICES * ROWS_OWN,), ((0, 128),), -0.2, 0.2)), 0.25, 4.0)
    return {"layer_input": layer_input, "out_grad": out_grad, "lengths": lengths, "item_owner": item_owner, "item_row": item_row, "w_attn": w_attn, "w_gate": w_gate, "w_out": w_out, "emb_table": emb_table, "row_accum": row_accum}


NORM_EPS = 1e-05
LEARN_RATE = 0.1

def silu_grad(pre_act):
    sigmoid = jax.nn.sigmoid(pre_act)
    return sigmoid * (1.0 + pre_act * (1.0 - sigmoid))

def segment_ids(length_row, positions):
    seg_ends = jnp.cumsum(length_row.astype(jnp.int32))
    places = jnp.arange(positions, dtype=jnp.int32)
    return lax.optimization_barrier(jnp.sum((places[:, None] >= seg_ends[None, :]).astype(jnp.int32), axis=1))

def group_backward(layer_input, out_grad, length_row, w_attn, w_gate, w_out):
    positions = layer_input.shape[0]
    scale = DH ** (-0.5)
    attn_pre = jnp.dot(layer_input, w_attn, preferred_element_type=jnp.float32)
    gate_pre = jnp.dot(layer_input, w_gate, preferred_element_type=jnp.float32)
    acts = jax.nn.silu(attn_pre).astype(jnp.bfloat16).reshape(positions, H, 3, DH)
    gate_act = jax.nn.silu(gate_pre)
    segment = segment_ids(length_row, positions)
    places = jnp.arange(positions, dtype=jnp.int32)
    allowed = (segment[:, None] == segment[None, :]) & (places[None, :] <= places[:, None])
    per_head = jnp.transpose(acts, (1, 0, 2, 3))

    def head_forward(head_item):
        scores = jnp.dot(head_item[:, 1], head_item[:, 2].T, preferred_element_type=jnp.float32) * scale
        weights = jnp.where(allowed, jax.nn.silu(scores) / MAXLEN, 0.0).astype(jnp.bfloat16)
        return jnp.dot(weights, head_item[:, 0], preferred_element_type=jnp.float32).astype(jnp.bfloat16)
    heads_out = lax.map(head_forward, per_head)
    mixed_in = jnp.transpose(heads_out, (1, 0, 2)).reshape(positions, D).astype(jnp.float32)
    centred = mixed_in - lax.optimization_barrier(jnp.mean(mixed_in, axis=1, keepdims=True))
    inv_dev = lax.rsqrt(lax.optimization_barrier(jnp.mean(centred * centred, axis=1, keepdims=True)) + NORM_EPS)
    normed = centred * inv_dev
    mixed = (normed * gate_act).astype(jnp.bfloat16)
    mixed_grad = jnp.dot(out_grad, w_out.T, preferred_element_type=jnp.float32)
    grad_out_part = jnp.dot(mixed.T, out_grad, preferred_element_type=jnp.float32)
    normed_grad = mixed_grad * gate_act
    gate_act_grad = mixed_grad * normed
    heads_grad = inv_dev * (normed_grad - lax.optimization_barrier(jnp.mean(normed_grad, axis=1, keepdims=True)) - normed * lax.optimization_barrier(jnp.mean(normed_grad * normed, axis=1, keepdims=True)))
    heads_grad = heads_grad.astype(jnp.bfloat16).reshape(positions, H, DH)

    def head_backward(head_pair):
        head_item, grad_item = head_pair
        values = head_item[:, 0]
        queries = head_item[:, 1]
        keys_head = head_item[:, 2]
        scores = jnp.dot(queries, keys_head.T, preferred_element_type=jnp.float32) * scale
        weights = jnp.where(allowed, jax.nn.silu(scores) / MAXLEN, 0.0).astype(jnp.bfloat16)
        weight_grad = jnp.dot(grad_item, values.T, preferred_element_type=jnp.float32)
        score_grad = jnp.where(allowed, weight_grad * silu_grad(scores) * (scale / MAXLEN), 0.0).astype(jnp.bfloat16)
        values_grad = jnp.dot(weights.T, grad_item, preferred_element_type=jnp.float32)
        query_grad = jnp.dot(score_grad, keys_head, preferred_element_type=jnp.float32)
        keys_grad = jnp.dot(score_grad.T, queries, preferred_element_type=jnp.float32)
        return jnp.stack([values_grad.astype(jnp.bfloat16), query_grad.astype(jnp.bfloat16), keys_grad.astype(jnp.bfloat16)], axis=1)
    acts_grad = lax.map(head_backward, (per_head, jnp.transpose(heads_grad, (1, 0, 2))))
    acts_grad = jnp.transpose(acts_grad, (1, 0, 2, 3)).reshape(positions, 3 * D)
    attn_grad = (acts_grad.astype(jnp.float32) * silu_grad(attn_pre)).astype(jnp.bfloat16)
    gate_grad = (gate_act_grad * silu_grad(gate_pre)).astype(jnp.bfloat16)
    grad_attn_part = jnp.dot(layer_input.T, attn_grad, preferred_element_type=jnp.float32)
    grad_gate_part = jnp.dot(layer_input.T, gate_grad, preferred_element_type=jnp.float32)
    input_grad = jnp.dot(attn_grad, w_attn.T, preferred_element_type=jnp.float32) + jnp.dot(gate_grad, w_gate.T, preferred_element_type=jnp.float32) + out_grad.astype(jnp.float32)
    return (grad_attn_part, grad_gate_part, grad_out_part, input_grad)

def reference(layer_input, out_grad, lengths, item_owner, item_row, w_attn, w_gate, w_out, emb_table, row_accum):
    groups = lengths.shape[0]
    inputs_grp = layer_input.reshape(groups, -1, D)
    grads_grp = out_grad.reshape(groups, -1, D)

    def step(totals, pieces):
        parts = group_backward(pieces[0], pieces[1], pieces[2], w_attn, w_gate, w_out)
        return ((totals[0] + parts[0], totals[1] + parts[1], totals[2] + parts[2]), parts[3])
    init = (jnp.zeros((D, 3 * D), jnp.float32), jnp.zeros((D, D), jnp.float32), jnp.zeros((D, D), jnp.float32))
    totals, input_grads = lax.scan(step, init, (inputs_grp, grads_grp, lengths))
    input_grads = input_grads.reshape(-1, D)
    table_rows = (item_owner[:, 0] * ROWS_OWN + item_row).astype(jnp.int32)
    table_grad = jnp.zeros(emb_table.shape, jnp.float32).at[table_rows].add(input_grads)
    new_accum = row_accum + lax.optimization_barrier(jnp.mean(table_grad * table_grad, axis=1))
    new_table = emb_table - LEARN_RATE * table_grad * lax.rsqrt(new_accum)[:, None]
    return (totals[0], totals[1], totals[2], new_table, new_accum)
```

```python
import functools

import jax
import jax.numpy as jnp
from jax import lax
from jax.experimental import pallas as pl
from jax.experimental.pallas import tpu as pltpu
from jax.sharding import PartitionSpec as P

D = 1024
H = 16
DH = 64
NORM_EPS = 1e-05
LEARN_RATE = 0.1
TQ = 256
TK = 256
VMEM_BYTES = 56 * 1024 * 1024

BF = jnp.bfloat16
F32 = jnp.float32
NN = (((1,), (0,)), ((), ()))
NT = (((1,), (1,)), ((), ()))


def mm(a, b, dims=NN):
    return lax.dot_general(a, b, dims, preferred_element_type=F32)


def silu(z):
    t = 0.5 * z
    return t + t * jnp.tanh(t)


def silu_grad(z):
    t = 0.5 * z
    th = jnp.tanh(t)
    return 0.5 * ((1.0 + th) * (1.0 + t * (1.0 - th)))


def event_starts(len_ref, places):
    end0 = len_ref[0]
    end1 = end0 + len_ref[1]
    return jnp.where(places >= end1, end1, jnp.where(places >= end0, end0, 0))


def scalar_start(len_ref, place):
    end0 = len_ref[0]
    end1 = end0 + len_ref[1]
    return jnp.where(place >= end1, end1, jnp.where(place >= end0, end0, 0))


def tile_allowed(len_ref, j, i):
    keys = j * TK + lax.broadcasted_iota(jnp.int32, (TK, TQ), 0)
    places = i * TQ + lax.broadcasted_iota(jnp.int32, (1, TQ), 1)
    return (keys >= event_starts(len_ref, places)) & (keys <= places)


def fwd_kernel(pos, maxlen, len_ref, x_ref, og_ref, wt_ref, wo_ref, pre_ref, h_ref, mg_ref, st_ref, v_s, q_s, k_s):
    chunk = 512

    @pl.loop(0, pos // chunk)
    def _(c):
        at = pl.ds(pl.multiple_of(c * chunk, chunk), chunk)
        pre = mm(wt_ref[...], x_ref[at, :], NT)
        pre_ref[:, at] = pre
        act = silu(pre[: 6 * DH])
        for hd in range(2):
            base = hd * 3 * DH
            v_s[hd, :, at] = act[base : base + DH].astype(BF)
            q_s[hd, :, at] = (act[base + DH : base + 2 * DH].astype(BF) * 0.0625).astype(BF)
            k_s[hd, at, :] = act[base + 2 * DH : base + 3 * DH].astype(BF).T
        mg_ref[:, at] = mm(wo_ref[...], og_ref[at, :], NT)

    @pl.loop(0, pos // TQ)
    def _(i):
        at = pl.ds(pl.multiple_of(i * TQ, TQ), TQ)
        first = scalar_start(len_ref, i * TQ) // TK
        last = ((i + 1) * TQ - 1) // TK

        def step(j, accs):
            kat = pl.ds(pl.multiple_of(j * TK, TK), TK)
            allowed = tile_allowed(len_ref, j, i)
            outs = []
            for hd in range(2):
                t = mm(k_s[hd, kat, :], q_s[hd, :, at])
                w = jnp.where(allowed, t + t * jnp.tanh(t), 0.0).astype(BF)
                outs.append(accs[hd] + mm(v_s[hd, :, kat], w))
            return tuple(outs)

        zero = jnp.zeros((DH, TQ), F32)
        accs = lax.fori_loop(first, last + 1, step, (zero, zero))
        for hd in range(2):
            h_ref[hd * DH : (hd + 1) * DH, at] = (accs[hd] * (1.0 / maxlen)).astype(BF)

    @pl.loop(0, pos // chunk)
    def _(c):
        at = pl.ds(pl.multiple_of(c * chunk, chunk), chunk)
        h = h_ref[:, at].astype(F32)
        mean = jnp.sum(h, axis=0, keepdims=True) * (1.0 / (2 * DH))
        cen = h - mean
        ng = mg_ref[:, at] * silu(pre_ref[6 * DH :, at])
        st_ref[0:1, at] = mean
        st_ref[1:2, at] = jnp.sum(cen * cen, axis=0, keepdims=True)
        st_ref[2:3, at] = jnp.sum(ng, axis=0, keepdims=True)
        st_ref[3:4, at] = jnp.sum(ng * cen, axis=0, keepdims=True)
        st_ref[4:8, at] = jnp.zeros((4, chunk), F32)


def bwd_kernel(
    pos, maxlen, seq_count,
    len_ref, sta_ref, pre_ref, h_ref, mg_ref, wt_ref, x_hbm, og_hbm,
    ig_ref, gw_ref, go_ref,
    x_s, og_s, sems, q_s, kt_s, k_s, v_s, qn_s, ot_s, o_s, mix_s, g_s, gn_s, dv_s, dk_s, dq_s,
):
    x_copy = pltpu.make_async_copy(x_hbm, x_s, sems.at[0])
    og_copy = pltpu.make_async_copy(og_hbm, og_s, sems.at[1])
    x_copy.start()
    og_copy.start()
    chunk = 512

    @pl.loop(0, pos // chunk)
    def _(c):
        at = pl.ds(pl.multiple_of(c * chunk, chunk), chunk)
        act = silu(pre_ref[: 6 * DH, at]).astype(BF)
        means = [sta_ref[8 * d : 8 * d + 1, at] for d in range(seq_count)]
        mean = functools.reduce(jnp.add, means) * (1.0 / seq_count)
        var = jnp.zeros_like(mean)
        ng_mean = jnp.zeros_like(mean)
        ng_cov = jnp.zeros_like(mean)
        for d in range(seq_count):
            off = means[d] - mean
            ng_sum = sta_ref[8 * d + 2 : 8 * d + 3, at]
            var = var + sta_ref[8 * d + 1 : 8 * d + 2, at] + (2 * DH) * off * off
            ng_mean = ng_mean + ng_sum
            ng_cov = ng_cov + sta_ref[8 * d + 3 : 8 * d + 4, at] + off * ng_sum
        inv = lax.rsqrt(var * (1.0 / D) + NORM_EPS)
        ng_mean = ng_mean * (1.0 / D)
        proj = inv * ng_cov * (1.0 / D)
        gate_pre = pre_ref[6 * DH :, at]
        gate = silu(gate_pre)
        normed = (h_ref[:, at].astype(F32) - mean) * inv
        mix_s[:, at] = (normed * gate).astype(BF)
        mg = mg_ref[:, at]
        g_s[6 * DH :, at] = (mg * normed * silu_grad(gate_pre)).astype(BF)
        hg = (inv * (mg * gate - ng_mean - normed * proj)).astype(BF)
        for hd in range(2):
            base = hd * 3 * DH
            q16 = (act[base + DH : base + 2 * DH] * 0.0625).astype(BF)
            k = act[base + 2 * DH : base + 3 * DH]
            q_s[hd, :, at] = q16
            kt_s[hd, :, at] = k
            k_s[hd, at, :] = k.T
            v_s[hd, at, :] = act[base : base + DH].T
            qn_s[hd, at, :] = q16.T
            o = hg[hd * DH : (hd + 1) * DH]
            ot_s[hd, :, at] = o
            o_s[hd, at, :] = o.T
            dv_s[hd, at, :] = jnp.zeros((chunk, DH), F32)
            dk_s[hd, at, :] = jnp.zeros((chunk, DH), F32)

    @pl.loop(0, pos // TQ)
    def _(i):
        at = pl.ds(pl.multiple_of(i * TQ, TQ), TQ)
        first = scalar_start(len_ref, i * TQ) // TK
        last = ((i + 1) * TQ - 1) // TK

        def step(j, accs):
            kat = pl.ds(pl.multiple_of(j * TK, TK), TK)
            allowed = tile_allowed(len_ref, j, i)
            outs = []
            for hd in range(2):
                t = mm(k_s[hd, kat, :], q_s[hd, :, at])
                dw = mm(v_s[hd, kat, :], ot_s[hd, :, at])
                a = 1.0 + jnp.tanh(t)
                w = t * a
                ds = jnp.where(allowed, dw * (a + w * (2.0 - a)), 0.0).astype(BF)
                w = jnp.where(allowed, w, 0.0).astype(BF)
                dv_s[hd, kat, :] += mm(w, o_s[hd, at, :])
                dk_s[hd, kat, :] += mm(ds, qn_s[hd, at, :])
                outs.append(accs[hd] + mm(kt_s[hd, :, kat], ds))
            return tuple(outs)

        zero = jnp.zeros((DH, TQ), F32)
        accs = lax.fori_loop(first, last + 1, step, (zero, zero))
        for hd in range(2):
            dq_s[hd, :, at] = accs[hd]

    fac = 0.0625 / maxlen

    @pl.loop(0, pos // chunk)
    def _(c):
        at = pl.ds(pl.multiple_of(c * chunk, chunk), chunk)
        sg = silu_grad(pre_ref[: 6 * DH, at])
        for hd in range(2):
            base = hd * 3 * DH
            dv = (dv_s[hd, at, :] * (1.0 / maxlen)).astype(BF).T
            dk = (dk_s[hd, at, :] * (16.0 * fac)).astype(BF).T
            dq = (dq_s[hd, :, at] * fac).astype(BF)
            for part, grad in enumerate((dv, dq, dk)):
                rows = slice(base + part * DH, base + (part + 1) * DH)
                g_s[rows, at] = (grad.astype(F32) * sg[rows]).astype(BF)
        gn_s[at, :] = g_s[:, at].T
        ig_ref[at, :] = mm(gn_s[at, :], wt_ref[...]).astype(BF)

    x_copy.wait()
    gw_ref[...] = mm(g_s[...], x_s[...]).astype(BF).T
    og_copy.wait()
    go_ref[...] = mm(mix_s[...], og_s[...]).astype(BF)


def vmem(count):
    return [pl.BlockSpec(memory_space=pltpu.VMEM)] * count


def forward(lens, x_g, og_g, wt, wo, pos, maxlen):
    return pl.pallas_call(
        functools.partial(fwd_kernel, pos, maxlen),
        out_shape=(
            jax.ShapeDtypeStruct((8 * DH, pos), F32),
            jax.ShapeDtypeStruct((2 * DH, pos), BF),
            jax.ShapeDtypeStruct((2 * DH, pos), F32),
            jax.ShapeDtypeStruct((8, pos), F32),
        ),
        in_specs=[pl.BlockSpec(memory_space=pltpu.SMEM)] + vmem(4),
        out_specs=tuple(vmem(4)),
        scratch_shapes=[
            pltpu.VMEM((2, DH, pos), BF),
            pltpu.VMEM((2, DH, pos), BF),
            pltpu.VMEM((2, pos, DH), BF),
        ],
        compiler_params=pltpu.CompilerParams(vmem_limit_bytes=VMEM_BYTES),
        name="forward",
    )(lens, x_g, og_g, wt, wo)


def backward(lens, stats, pre, h, mg, wt, x_g, og_g, pos, maxlen, seq_count):
    heads_t = pltpu.VMEM((2, DH, pos), BF)
    heads_n = pltpu.VMEM((2, pos, DH), BF)
    sums_n = pltpu.VMEM((2, pos, DH), F32)
    return pl.pallas_call(
        functools.partial(bwd_kernel, pos, maxlen, seq_count),
        out_shape=(
            jax.ShapeDtypeStruct((pos, D), BF),
            jax.ShapeDtypeStruct((D, 8 * DH), BF),
            jax.ShapeDtypeStruct((2 * DH, D), BF),
        ),
        in_specs=[pl.BlockSpec(memory_space=pltpu.SMEM)] + vmem(5) + [pl.BlockSpec(memory_space=pl.ANY)] * 2,
        out_specs=tuple(vmem(3)),
        scratch_shapes=[
            pltpu.VMEM((pos, D), BF),
            pltpu.VMEM((pos, D), BF),
            pltpu.SemaphoreType.DMA((2,)),
            heads_t, heads_t, heads_n, heads_n, heads_n, heads_t, heads_n,
            pltpu.VMEM((2 * DH, pos), BF),
            pltpu.VMEM((8 * DH, pos), BF),
            pltpu.VMEM((pos, 8 * DH), BF),
            sums_n, sums_n,
            pltpu.VMEM((2, DH, pos), F32),
        ],
        compiler_params=pltpu.CompilerParams(vmem_limit_bytes=VMEM_BYTES),
        name="backward",
    )(lens, stats, pre, h, mg, wt, x_g, og_g)


def body(
    layer_input,
    out_grad,
    lengths,
    item_owner,
    item_row,
    w_attn,
    w_gate,
    w_out,
    emb_table,
    row_accum,
):
    seq_count = lax.axis_size("seq")
    dp_count = lax.axis_size("dp")
    devices = seq_count * dp_count
    me = lax.axis_index("seq")
    tokens_dev = layer_input.shape[0]
    pos = tokens_dev * seq_count
    maxlen = 2 * pos // 3
    wt = jnp.concatenate(
        [
            lax.dynamic_slice_in_dim(w_attn, me * 6 * DH, 6 * DH, 1).T,
            lax.dynamic_slice_in_dim(w_gate, me * 2 * DH, 2 * DH, 1).T,
        ],
        axis=0,
    )
    wo = lax.dynamic_slice_in_dim(w_out, me * 2 * DH, 2 * DH, 0)
    lens = lengths[0]
    x_g = lax.all_gather(layer_input, "seq", axis=0, tiled=True)
    og_g = lax.all_gather(out_grad, "seq", axis=0, tiled=True)
    pre, h, mg, stats = forward(lens, x_g, og_g, wt, wo, pos, maxlen)
    stats = lax.all_gather(stats, "seq", axis=0, tiled=True)
    ig, gw, go = backward(lens, stats, pre, h, mg, wt, x_g, og_g, pos, maxlen, seq_count)
    ig = lax.all_to_all(ig.reshape(seq_count, tokens_dev, D), "seq", 0, 0, tiled=True)
    input_grad = jnp.sum(ig.astype(F32), axis=0) + out_grad.astype(F32)
    gw = lax.all_to_all(gw.reshape(dp_count, D // dp_count, 8 * DH), "dp", 0, 0, tiled=True)
    gw = jnp.sum(gw.astype(F32), axis=0)
    go = lax.all_to_all(go, "seq", 1, 0, tiled=True)
    go = lax.all_to_all(go.reshape(dp_count, D // dp_count, 2 * DH), "dp", 0, 0, tiled=True)
    go = jnp.sum(go.astype(F32), axis=0)

    rows_own = emb_table.shape[0]
    capacity = max(2, 2 * tokens_dev // devices)
    owners = item_owner[:, 0]
    hits = (owners[:, None] == jnp.arange(devices, dtype=jnp.int32)[None, :]).astype(jnp.int32)
    slots = jnp.sum((jnp.cumsum(hits, axis=0) - hits) * hits, axis=1)
    flat_slot = owners * capacity + slots
    total = devices * capacity
    place = (jnp.arange(total, dtype=jnp.int32)[:, None] == flat_slot[None, :])
    send_rows = mm(place.astype(BF), input_grad.astype(BF)).astype(BF)
    send_ids = jnp.sum(jnp.where(place, item_row[None, :] + 1, 0), axis=1) - 1
    got_rows = lax.all_to_all(send_rows.reshape(devices, capacity, D), ("seq", "dp"), 0, 0, tiled=True)
    got_ids = lax.all_to_all(send_ids.reshape(devices, capacity), ("seq", "dp"), 0, 0, tiled=True)
    pick = (jnp.arange(rows_own, dtype=jnp.int32)[:, None] == got_ids.reshape(1, total)).astype(BF)
    table_grad = mm(pick, got_rows.reshape(total, D))
    new_accum = row_accum + jnp.mean(table_grad * table_grad, axis=1)
    new_table = emb_table - LEARN_RATE * table_grad * lax.rsqrt(new_accum)[:, None]
    return (gw[:, : 6 * DH], gw[:, 6 * DH :], go, new_table, new_accum)


def solution(mesh):
    placed = (
        P(("dp", "seq"), None),
        P(("dp", "seq"), None),
        P("dp", None),
        P(("dp", "seq"), None),
        P(("dp", "seq")),
        P(),
        P(),
        P(),
        P(("seq", "dp"), None),
        P(("seq", "dp")),
    )
    return jax.shard_map(
        body,
        mesh=mesh,
        in_specs=placed,
        out_specs=(
            P("dp", "seq"),
            P("dp", "seq"),
            P("dp", "seq"),
            P(("seq", "dp"), None),
            P(("seq", "dp")),
        ),
        check_vma=False,
    )
```

```python
import functools

import jax
import jax.numpy as jnp
from jax import lax
from jax.experimental import pallas as pl
from jax.experimental.pallas import tpu as pltpu
from jax.sharding import PartitionSpec as P

D = 1024
H = 16
DH = 64
NORM_EPS = 1e-05
LEARN_RATE = 0.1
TQ = 256
TK = 256
VMEM_BYTES = 56 * 1024 * 1024

BF = jnp.bfloat16
F32 = jnp.float32
NN = (((1,), (0,)), ((), ()))
NT = (((1,), (1,)), ((), ()))
MESH = pl.DeviceIdType.MESH


def mm(a, b, dims=NN):
    return lax.dot_general(a, b, dims, preferred_element_type=F32)


def silu(z):
    t = 0.5 * z
    return t + t * jnp.tanh(t)


def silu_grad(z):
    t = 0.5 * z
    th = jnp.tanh(t)
    return 0.5 * ((1.0 + th) * (1.0 + t * (1.0 - th)))


def event_starts(len_ref, places):
    end0 = len_ref[0]
    end1 = end0 + len_ref[1]
    return jnp.where(places >= end1, end1, jnp.where(places >= end0, end0, 0))


def scalar_start(len_ref, place):
    end0 = len_ref[0]
    end1 = end0 + len_ref[1]
    return jnp.where(place >= end1, end1, jnp.where(place >= end0, end0, 0))


def tile_allowed(len_ref, j, i):
    keys = j * TK + lax.broadcasted_iota(jnp.int32, (TK, TQ), 0)
    places = i * TQ + lax.broadcasted_iota(jnp.int32, (1, TQ), 1)
    return (keys >= event_starts(len_ref, places)) & (keys <= places)


def fwd_kernel(pos, maxlen, len_ref, pre_ref, mg_ref, h_ref, st_ref, v_s, q_s, k_s):
    chunk = 512

    @pl.loop(0, pos // chunk)
    def _(c):
        at = pl.ds(pl.multiple_of(c * chunk, chunk), chunk)
        act = silu(pre_ref[: 6 * DH, at])
        for hd in range(2):
            base = hd * 3 * DH
            v_s[hd, :, at] = act[base : base + DH].astype(BF)
            q_s[hd, :, at] = (act[base + DH : base + 2 * DH].astype(BF) * 0.0625).astype(BF)
            k_s[hd, at, :] = act[base + 2 * DH : base + 3 * DH].astype(BF).T

    @pl.loop(0, pos // TQ)
    def _(i):
        at = pl.ds(pl.multiple_of(i * TQ, TQ), TQ)
        first = scalar_start(len_ref, i * TQ) // TK
        last = ((i + 1) * TQ - 1) // TK

        def step(j, accs):
            kat = pl.ds(pl.multiple_of(j * TK, TK), TK)
            allowed = tile_allowed(len_ref, j, i)
            outs = []
            for hd in range(2):
                t = mm(k_s[hd, kat, :], q_s[hd, :, at])
                w = jnp.where(allowed, t + t * jnp.tanh(t), 0.0).astype(BF)
                outs.append(accs[hd] + mm(v_s[hd, :, kat], w))
            return tuple(outs)

        zero = jnp.zeros((DH, TQ), F32)
        accs = lax.fori_loop(first, last + 1, step, (zero, zero))
        for hd in range(2):
            h_ref[hd * DH : (hd + 1) * DH, at] = (accs[hd] * (1.0 / maxlen)).astype(BF)

    for c in range(pos // chunk):
        at = slice(c * chunk, (c + 1) * chunk)
        row, lane = stat_place(pos, chunk, c)
        h = h_ref[:, at].astype(F32)
        mean = jnp.sum(h, axis=0, keepdims=True) * (1.0 / (2 * DH))
        cen = h - mean
        ng = mg_ref[:, at].astype(F32) * silu(pre_ref[6 * DH :, at])
        st_ref[row : row + 1, lane] = mean
        st_ref[row + 1 : row + 2, lane] = jnp.sum(cen * cen, axis=0, keepdims=True)
        st_ref[row + 2 : row + 3, lane] = jnp.sum(ng, axis=0, keepdims=True)
        st_ref[row + 3 : row + 4, lane] = jnp.sum(ng * cen, axis=0, keepdims=True)


def stat_place(pos, chunk, c):
    first = c * chunk
    row = 4 * (first // (pos // 2))
    lane = first % (pos // 2)
    return row, slice(lane, lane + chunk)


def bwd_kernel(
    pos, maxlen, seq_count,
    len_ref, sta_ref, pre_ref, h_ref, mg_ref, wt_ref, x_hbm, og_hbm,
    ig_ref, gw_ref, go_ref,
    x_s, og_s, sems, q_s, kt_s, k_s, v_s, qn_s, ot_s, o_s, mix_s, g_s, gn_s, dv_s, dk_s, dq_s,
):
    x_copy = pltpu.make_async_copy(x_hbm, x_s, sems.at[0])
    og_copy = pltpu.make_async_copy(og_hbm, og_s, sems.at[1])
    x_copy.start()
    og_copy.start()
    chunk = 512

    for c in range(pos // chunk):
        at = slice(c * chunk, (c + 1) * chunk)
        row, lane = stat_place(pos, chunk, c)
        act = silu(pre_ref[: 6 * DH, at]).astype(BF)
        means = [sta_ref[d, row : row + 1, lane] for d in range(seq_count)]
        mean = functools.reduce(jnp.add, means) * (1.0 / seq_count)
        var = jnp.zeros_like(mean)
        ng_mean = jnp.zeros_like(mean)
        ng_cov = jnp.zeros_like(mean)
        for d in range(seq_count):
            off = means[d] - mean
            ng_sum = sta_ref[d, row + 2 : row + 3, lane]
            var = var + sta_ref[d, row + 1 : row + 2, lane] + (2 * DH) * off * off
            ng_mean = ng_mean + ng_sum
            ng_cov = ng_cov + sta_ref[d, row + 3 : row + 4, lane] + off * ng_sum
        inv = lax.rsqrt(var * (1.0 / D) + NORM_EPS)
        ng_mean = ng_mean * (1.0 / D)
        proj = inv * ng_cov * (1.0 / D)
        gate_pre = pre_ref[6 * DH :, at]
        gate = silu(gate_pre)
        normed = (h_ref[:, at].astype(F32) - mean) * inv
        mix_s[:, at] = (normed * gate).astype(BF)
        mg = mg_ref[:, at].astype(F32)
        g_s[6 * DH :, at] = (mg * normed * silu_grad(gate_pre)).astype(BF)
        hg = (inv * (mg * gate - ng_mean - normed * proj)).astype(BF)
        for hd in range(2):
            base = hd * 3 * DH
            q16 = (act[base + DH : base + 2 * DH] * 0.0625).astype(BF)
            k = act[base + 2 * DH : base + 3 * DH]
            q_s[hd, :, at] = q16
            kt_s[hd, :, at] = k
            k_s[hd, at, :] = k.T
            v_s[hd, at, :] = act[base : base + DH].T
            qn_s[hd, at, :] = q16.T
            o = hg[hd * DH : (hd + 1) * DH]
            ot_s[hd, :, at] = o
            o_s[hd, at, :] = o.T
            dv_s[hd, at, :] = jnp.zeros((chunk, DH), F32)
            dk_s[hd, at, :] = jnp.zeros((chunk, DH), F32)

    @pl.loop(0, pos // TQ)
    def _(i):
        at = pl.ds(pl.multiple_of(i * TQ, TQ), TQ)
        first = scalar_start(len_ref, i * TQ) // TK
        last = ((i + 1) * TQ - 1) // TK

        def step(j, accs):
            kat = pl.ds(pl.multiple_of(j * TK, TK), TK)
            allowed = tile_allowed(len_ref, j, i)
            outs = []
            for hd in range(2):
                t = mm(k_s[hd, kat, :], q_s[hd, :, at])
                dw = mm(v_s[hd, kat, :], ot_s[hd, :, at])
                a = 1.0 + jnp.tanh(t)
                w = t * a
                ds = jnp.where(allowed, dw * (a + w * (2.0 - a)), 0.0).astype(BF)
                w = jnp.where(allowed, w, 0.0).astype(BF)
                dv_s[hd, kat, :] += mm(w, o_s[hd, at, :])
                dk_s[hd, kat, :] += mm(ds, qn_s[hd, at, :])
                outs.append(accs[hd] + mm(kt_s[hd, :, kat], ds))
            return tuple(outs)

        zero = jnp.zeros((DH, TQ), F32)
        accs = lax.fori_loop(first, last + 1, step, (zero, zero))
        for hd in range(2):
            dq_s[hd, :, at] = accs[hd]

    fac = 0.0625 / maxlen

    @pl.loop(0, pos // chunk)
    def _(c):
        at = pl.ds(pl.multiple_of(c * chunk, chunk), chunk)
        sg = silu_grad(pre_ref[: 6 * DH, at])
        for hd in range(2):
            base = hd * 3 * DH
            dv = (dv_s[hd, at, :] * (1.0 / maxlen)).astype(BF).T
            dk = (dk_s[hd, at, :] * (16.0 * fac)).astype(BF).T
            dq = (dq_s[hd, :, at] * fac).astype(BF)
            for part, grad in enumerate((dv, dq, dk)):
                rows = slice(base + part * DH, base + (part + 1) * DH)
                g_s[rows, at] = (grad.astype(F32) * sg[rows]).astype(BF)
        gn_s[at, :] = g_s[:, at].T
        ig_ref[at, :] = mm(gn_s[at, :], wt_ref[...]).astype(BF)

    x_copy.wait()
    gw_ref[...] = mm(g_s[...], x_s[...]).astype(BF).T
    og_copy.wait()
    go_ref[...] = mm(mix_s[...], og_s[...]).astype(BF)


def vmem(count):
    return [pl.BlockSpec(memory_space=pltpu.VMEM)] * count


def forward(lens, pre, mg, pos, maxlen):
    return pl.pallas_call(
        functools.partial(fwd_kernel, pos, maxlen),
        out_shape=(
            jax.ShapeDtypeStruct((2 * DH, pos), BF),
            jax.ShapeDtypeStruct((8, pos // 2), F32),
        ),
        in_specs=[pl.BlockSpec(memory_space=pltpu.SMEM)] + vmem(2),
        out_specs=tuple(vmem(2)),
        scratch_shapes=[
            pltpu.VMEM((2, DH, pos), BF),
            pltpu.VMEM((2, DH, pos), BF),
            pltpu.VMEM((2, pos, DH), BF),
        ],
        compiler_params=pltpu.CompilerParams(vmem_limit_bytes=VMEM_BYTES),
        name="forward",
    )(lens, pre, mg)


def backward(lens, stats, pre, h, mg, wt, x_g, og_g, pos, maxlen, seq_count):
    heads_t = pltpu.VMEM((2, DH, pos), BF)
    heads_n = pltpu.VMEM((2, pos, DH), BF)
    sums_n = pltpu.VMEM((2, pos, DH), F32)
    return pl.pallas_call(
        functools.partial(bwd_kernel, pos, maxlen, seq_count),
        out_shape=(
            jax.ShapeDtypeStruct((pos, D), BF),
            jax.ShapeDtypeStruct((D, 8 * DH), BF),
            jax.ShapeDtypeStruct((2 * DH, D), BF),
        ),
        in_specs=[pl.BlockSpec(memory_space=pltpu.SMEM)] + vmem(5) + [pl.BlockSpec(memory_space=pl.ANY)] * 2,
        out_specs=tuple(vmem(3)),
        scratch_shapes=[
            pltpu.VMEM((pos, D), BF),
            pltpu.VMEM((pos, D), BF),
            pltpu.SemaphoreType.DMA((2,)),
            heads_t, heads_t, heads_n, heads_n, heads_n, heads_t, heads_n,
            pltpu.VMEM((2 * DH, pos), BF),
            pltpu.VMEM((8 * DH, pos), BF),
            pltpu.VMEM((pos, 8 * DH), BF),
            sums_n, sums_n,
            pltpu.VMEM((2, DH, pos), F32),
        ],
        compiler_params=pltpu.CompilerParams(vmem_limit_bytes=VMEM_BYTES),
        name="backward",
    )(lens, stats, pre, h, mg, wt, x_g, og_g)


def seq_peers():
    me = lax.axis_index("seq")
    z, c = me // 2, me % 2
    at = lambda step: lax.rem(z + step, 4) * 2
    return me, at(0) + 1 - c, at(1) + c, at(3) + c, at(2) + c, c


def gather_kernel(
    tokens,
    x_ref, og_ref, wa_hbm, wg_hbm, wo_ref,
    xg_ref, pre_ref, mg_ref, wt_ref,
    x_s, w_s, mine_s, load_sem, keep_sem, send_sem, recv_sem, mg_send, mg_recv,
):
    me, sib, right, left, far, c = seq_peers()
    half = tokens // 2
    loads = [
        pltpu.make_async_copy(wa_hbm.at[:, pl.ds(pl.multiple_of(me * 6 * DH, 128), 6 * DH)], w_s.at[:, : 6 * DH], load_sem.at[0]),
        pltpu.make_async_copy(wg_hbm.at[:, pl.ds(pl.multiple_of(me * 2 * DH, 128), 2 * DH)], w_s.at[:, 6 * DH :], load_sem.at[1]),
        pltpu.make_async_copy(x_ref, x_s.at[me], load_sem.at[2]),
    ]
    for load in loads:
        load.start()

    barrier = pltpu.get_barrier_semaphore()
    for step in range(1, 8):
        pl.semaphore_signal(barrier, inc=1, device_id={"seq": lax.rem(me + step, 8)}, device_id_type=MESH)
    pl.semaphore_wait(barrier, 7)

    def send(index, shard, part, to):
        if part is None:
            ref = x_s.at[shard]
        else:
            ref = x_s.at[shard, pl.ds(part * half, half)]
        copy = pltpu.make_async_remote_copy(
            src_ref=ref, dst_ref=ref, send_sem=send_sem.at[index], recv_sem=recv_sem.at[index],
            device_id={"seq": to}, device_id_type=MESH,
        )
        copy.start()
        return copy

    def project(shard):
        at = pl.ds(pl.multiple_of(shard * tokens, tokens), tokens)
        pre_ref[:, at] = mm(wt_ref[...], x_s[shard], NT)
        keep(shard)

    keeps = []

    def keep(shard):
        copy = pltpu.make_async_copy(x_s.at[shard], xg_ref.at[shard], keep_sem.at[len(keeps)])
        copy.start()
        keeps.append(copy)

    loads[2].wait()
    to_right = [send(0, me, 0, right), None]
    to_left = [None, send(1, me, 1, left)]
    to_right[1] = send(2, me, 1, right)
    to_left[0] = send(3, me, 0, left)
    to_sib = send(4, me, None, sib)

    mine_s[...] = mm(wo_ref[...], og_ref[...], NT).astype(BF)
    mine = pl.ds(pl.multiple_of(me * tokens, tokens), tokens)
    mg_copies = []
    for step in range(1, 8):
        to = lax.rem(me + step, 8)
        copy = pltpu.make_async_remote_copy(
            src_ref=mine_s.at[pl.ds(pl.multiple_of(to * 2 * DH, 2 * DH), 2 * DH)],
            dst_ref=mg_ref.at[:, mine],
            send_sem=mg_send.at[step], recv_sem=mg_recv.at[step],
            device_id={"seq": to}, device_id_type=MESH,
        )
        copy.start()
        mg_copies.append(copy)
    mg_ref[:, mine] = mine_s[pl.ds(pl.multiple_of(me * 2 * DH, 2 * DH), 2 * DH), :]
    loads[0].wait()
    loads[1].wait()
    wt_ref[...] = w_s[...].T
    project(me)

    z = me // 2
    s_left, s_right, s_far = left, right, far
    to_right[0].wait_recv()
    fwd_r = send(5, s_left, 0, right)
    to_left[1].wait_recv()
    fwd_l = send(6, s_right, 1, left)
    to_right[1].wait_recv()
    sib_left = send(7, s_left, None, sib)
    to_left[0].wait_recv()
    sib_right = send(8, s_right, None, sib)
    project(s_left)
    project(s_right)
    to_sib.wait_recv()
    project(sib)
    fwd_r.wait_recv()
    sib_far0 = send(9, s_far, 0, sib)
    fwd_l.wait_recv()
    sib_far1 = send(10, s_far, 1, sib)
    project(s_far)
    other = 1 - 2 * c
    sib_left.wait_recv()
    project(s_left + other)
    sib_right.wait_recv()
    project(s_right + other)
    sib_far0.wait_recv()
    sib_far1.wait_recv()
    project(s_far + other)
    for copy in mg_copies:
        copy.wait()
    for copy in to_right + to_left + [to_sib, fwd_r, fwd_l, sib_left, sib_right, sib_far0, sib_far1]:
        copy.wait_send()
    for copy in keeps:
        copy.wait()


def gather(x, og, w_attn, w_gate, w_out, tokens, seq_count):
    pos = tokens * seq_count
    hbm = pl.BlockSpec(memory_space=pl.ANY)
    x_g, pre, mg, wt = pl.pallas_call(
        functools.partial(gather_kernel, tokens),
        out_shape=(
            jax.ShapeDtypeStruct((seq_count, tokens, D), BF),
            jax.ShapeDtypeStruct((8 * DH, pos), F32),
            jax.ShapeDtypeStruct((2 * DH, pos), BF),
            jax.ShapeDtypeStruct((8 * DH, D), BF),
        ),
        in_specs=[hbm] + vmem(1) + [hbm, hbm] + vmem(1),
        out_specs=tuple([hbm] + vmem(3)),
        scratch_shapes=[
            pltpu.VMEM((seq_count, tokens, D), BF),
            pltpu.VMEM((D, 8 * DH), BF),
            pltpu.VMEM((D, tokens), BF),
            pltpu.SemaphoreType.DMA((3,)),
            pltpu.SemaphoreType.DMA((seq_count,)),
            pltpu.SemaphoreType.DMA((11,)),
            pltpu.SemaphoreType.DMA((11,)),
            pltpu.SemaphoreType.DMA((8,)),
            pltpu.SemaphoreType.DMA((8,)),
        ],
        compiler_params=pltpu.CompilerParams(
            vmem_limit_bytes=VMEM_BYTES, collective_id=0, has_side_effects=True
        ),
        name="gather",
    )(x, og, w_attn, w_gate, w_out)
    return x_g.reshape(pos, D), pre, mg, wt


def stats_kernel(st_ref, all_ref, buf_s, send_sem, recv_sem):
    me = lax.axis_index("seq")
    barrier = pltpu.get_barrier_semaphore()
    for step in range(1, 8):
        pl.semaphore_signal(barrier, inc=1, device_id={"seq": lax.rem(me + step, 8)}, device_id_type=MESH)
    pl.semaphore_wait(barrier, 7)
    copies = []
    for step in range(1, 8):
        copy = pltpu.make_async_remote_copy(
            src_ref=st_ref, dst_ref=buf_s.at[me], send_sem=send_sem.at[step], recv_sem=recv_sem.at[step],
            device_id={"seq": lax.rem(me + step, 8)}, device_id_type=MESH,
        )
        copy.start()
        copies.append(copy)
    buf_s[me] = st_ref[...]
    for copy in copies:
        copy.wait()
    all_ref[...] = buf_s[...]


def share_stats(stats, seq_count):
    shape = (seq_count,) + stats.shape
    return pl.pallas_call(
        stats_kernel,
        out_shape=jax.ShapeDtypeStruct(shape, F32),
        in_specs=vmem(1),
        out_specs=vmem(1)[0],
        scratch_shapes=[
            pltpu.VMEM(shape, F32),
            pltpu.SemaphoreType.DMA((8,)),
            pltpu.SemaphoreType.DMA((8,)),
        ],
        compiler_params=pltpu.CompilerParams(collective_id=1, has_side_effects=True),
        name="share_stats",
    )(stats)


def reduce_kernel(
    tokens, dp_count, capacity,
    ig_hbm, gw_hbm, go_hbm, og_ref, owner_col_ref, owner_row_ref, row_ref,
    gsum_ref, gosum_ref, send_ref,
    own_s, pair_s, sum_s, far_s, ring_s, gw_s, col_s, go_s,
    load_sem, pair_send, pair_recv, ring_send, ring_recv, gw_send, gw_recv, col_send, col_recv, go_send, go_recv,
):
    me, sib, right, left, far, c = seq_peers()
    z = me // 2
    dp = lax.axis_index("dp")
    half = tokens // 2
    block = D // dp_count

    loads = []
    for k in (2, 1, 3, 0):
        load = pltpu.make_async_copy(ig_hbm.at[lax.rem(z + k, 4) * 2 + c], own_s.at[k], load_sem.at[k])
        load.start()
        loads.append(load)
    own_col = pltpu.make_async_copy(go_hbm.at[:, pl.ds(pl.multiple_of(me * 2 * DH, 2 * DH), 2 * DH)], col_s.at[me], load_sem.at[4])
    own_col.start()
    own_gw = pltpu.make_async_copy(gw_hbm.at[pl.ds(pl.multiple_of(dp * block, block), block)], gw_s.at[dp], load_sem.at[5])
    own_gw.start()

    barrier = pltpu.get_barrier_semaphore()
    for step in range(1, 8):
        pl.semaphore_signal(barrier, inc=1, device_id={"seq": lax.rem(me + step, 8)}, device_id_type=MESH)
    for step in range(1, dp_count):
        pl.semaphore_signal(barrier, inc=1, device_id={"dp": lax.rem(dp + step, dp_count)}, device_id_type=MESH)
    pl.semaphore_wait(barrier, 7 + dp_count - 1)

    def remote(src, dst, send_sem, recv_sem, to):
        copy = pltpu.make_async_remote_copy(
            src_ref=src, dst_ref=dst, send_sem=send_sem, recv_sem=recv_sem, device_id=to, device_id_type=MESH
        )
        copy.start()
        return copy

    pairs = {}
    for k in (2, 1, 3, 0):
        pairs[k] = remote(
            ig_hbm.at[lax.rem(z + k, 4) * 2 + 1 - c], pair_s.at[k], pair_send.at[k], pair_recv.at[k], {"seq": sib}
        )
    cols = []
    for step in range(1, 8):
        to = lax.rem(me + step, 8)
        cols.append(remote(
            go_hbm.at[:, pl.ds(pl.multiple_of(to * 2 * DH, 2 * DH), 2 * DH)], col_s.at[me],
            col_send.at[step], col_recv.at[step], {"seq": to},
        ))
    blocks = []
    for step in range(1, dp_count):
        to = lax.rem(dp + step, dp_count)
        blocks.append(remote(
            gw_hbm.at[pl.ds(pl.multiple_of(to * block, block), block)], gw_s.at[dp],
            gw_send.at[step], gw_recv.at[step], {"dp": to},
        ))

    def pair_sum(k):
        loads[(2, 1, 3, 0).index(k)].wait()
        pairs[k].wait_recv()
        return own_s[k].astype(F32) + pair_s[k].astype(F32)

    low, high = pl.ds(0, half), pl.ds(half, half)
    sum_s[2] = pair_sum(2).astype(BF)
    far_r = remote(sum_s.at[2, low], far_s.at[0], ring_send.at[0], ring_recv.at[0], {"seq": right})
    far_l = remote(sum_s.at[2, high], far_s.at[1], ring_send.at[1], ring_recv.at[1], {"seq": left})
    sum_s[1] = pair_sum(1).astype(BF)
    near_r = remote(sum_s.at[1, high], ring_s.at[0, high], ring_send.at[2], ring_recv.at[2], {"seq": right})
    sum_s[3] = pair_sum(3).astype(BF)
    near_l = remote(sum_s.at[3, low], ring_s.at[1, low], ring_send.at[3], ring_recv.at[3], {"seq": left})

    own_col.wait()
    for copy in cols:
        copy.wait_recv()
    gos = []
    for step in range(1, dp_count):
        to = lax.rem(dp + step, dp_count)
        gos.append(remote(
            col_s.at[to // 2, pl.ds(pl.multiple_of(lax.rem(to, 2) * block, block), block)], go_s.at[dp],
            go_send.at[step], go_recv.at[step], {"dp": to},
        ))
    go_s[dp] = col_s[dp // 2, pl.ds(pl.multiple_of(lax.rem(dp, 2) * block, block), block), :]

    far_r.wait_recv()
    sum_s[0, low] = (sum_s[1, low].astype(F32) + far_s[0].astype(F32)).astype(BF)
    end_r = remote(sum_s.at[0, low], ring_s.at[0, low], ring_send.at[4], ring_recv.at[4], {"seq": right})
    far_l.wait_recv()
    sum_s[0, high] = (sum_s[3, high].astype(F32) + far_s[1].astype(F32)).astype(BF)
    end_l = remote(sum_s.at[0, high], ring_s.at[1, high], ring_send.at[5], ring_recv.at[5], {"seq": left})

    mine = pair_sum(0) + og_ref[...].astype(F32)
    earlier = (lax.broadcasted_iota(jnp.int32, (tokens, tokens), 0) < lax.broadcasted_iota(jnp.int32, (tokens, tokens), 1))
    same = owner_col_ref[...] == owner_row_ref[...]
    rank = jnp.sum(jnp.where(earlier & same, 1.0, 0.0), axis=0, keepdims=True).astype(jnp.int32)
    slot = owner_row_ref[...] * capacity + rank
    total = send_ref.shape[0]
    hit = lax.broadcasted_iota(jnp.int32, (total, tokens), 0) == slot
    ident = jnp.sum(jnp.where(hit, (row_ref[...] + 1).astype(F32), 0.0), axis=1, keepdims=True).astype(jnp.int32)
    lanes = lax.broadcasted_iota(jnp.int32, (total, 128), 1)
    code = jnp.where(lanes == 0, ident // 32, jnp.where(lanes == 1, ident % 32, 0))
    send_ref[:, D:] = code.astype(F32).astype(BF)
    place = jnp.where(hit, 1.0, 0.0).astype(BF)

    for copy in blocks:
        copy.wait_recv()
    own_gw.wait()
    acc = gw_s[0].astype(F32)
    for d in range(1, dp_count):
        acc = acc + gw_s[d].astype(F32)
    gsum_ref[...] = acc
    for copy in gos:
        copy.wait_recv()
    acc = go_s[0].astype(F32)
    for d in range(1, dp_count):
        acc = acc + go_s[d].astype(F32)
    gosum_ref[...] = acc

    near_r.wait_recv()
    near_l.wait_recv()
    end_r.wait_recv()
    end_l.wait_recv()
    total_grad = (mine + ring_s[0].astype(F32) + ring_s[1].astype(F32)).astype(BF)
    send_ref[:, :D] = mm(place, total_grad).astype(BF)

    for copy in list(pairs.values()) + cols + blocks + gos + [far_r, far_l, near_r, near_l, end_r, end_l]:
        copy.wait_send()


def reduce_all(ig, gw, go, og, item_owner, item_row, dp_count, capacity, devices):
    seq_count, tokens = ig.shape[0], ig.shape[1]
    hbm = pl.BlockSpec(memory_space=pl.ANY)
    block = D // dp_count
    shard = lambda n: pltpu.VMEM((n, tokens, D), BF)
    dma = lambda n: pltpu.SemaphoreType.DMA((n,))
    return pl.pallas_call(
        functools.partial(reduce_kernel, tokens, dp_count, capacity),
        out_shape=(
            jax.ShapeDtypeStruct((block, 8 * DH), F32),
            jax.ShapeDtypeStruct((block, 2 * DH), F32),
            jax.ShapeDtypeStruct((devices * capacity, D + 128), BF),
        ),
        in_specs=[hbm] * 3 + vmem(4),
        out_specs=tuple(vmem(3)),
        scratch_shapes=[
            shard(4), shard(4), shard(4),
            pltpu.VMEM((2, tokens // 2, D), BF),
            shard(2),
            pltpu.VMEM((dp_count, block, 8 * DH), BF),
            pltpu.VMEM((seq_count, 2 * DH, 2 * DH), BF),
            pltpu.VMEM((dp_count, block, 2 * DH), BF),
            dma(6), dma(4), dma(4), dma(6), dma(6), dma(dp_count), dma(dp_count),
            dma(seq_count), dma(seq_count), dma(dp_count), dma(dp_count),
        ],
        compiler_params=pltpu.CompilerParams(vmem_limit_bytes=VMEM_BYTES, collective_id=2, has_side_effects=True),
        name="reduce_all",
    )(ig, gw, go, og, item_owner, item_owner.reshape(1, tokens), item_row.reshape(1, tokens))


def body(
    layer_input,
    out_grad,
    lengths,
    item_owner,
    item_row,
    w_attn,
    w_gate,
    w_out,
    emb_table,
    row_accum,
):
    seq_count = lax.axis_size("seq")
    dp_count = lax.axis_size("dp")
    devices = seq_count * dp_count
    tokens_dev = layer_input.shape[0]
    pos = tokens_dev * seq_count
    maxlen = 2 * pos // 3
    capacity = max(2, 2 * tokens_dev // devices)
    lens = lengths[0]
    x_g, pre, mg, wt = gather(layer_input, out_grad, w_attn, w_gate, w_out, tokens_dev, seq_count)
    og_late, mg = lax.optimization_barrier((out_grad, mg))
    og_g = lax.all_gather(og_late, "seq", axis=0, tiled=True)
    h, stats = forward(lens, pre, mg, pos, maxlen)
    stats = share_stats(stats, seq_count)
    ig, gw, go = backward(lens, stats, pre, h, mg, wt, x_g, og_g, pos, maxlen, seq_count)
    gw, go, send_rows = reduce_all(
        ig.reshape(seq_count, tokens_dev, D), gw, go, out_grad, item_owner, item_row, dp_count, capacity, devices
    )
    got = lax.all_to_all(send_rows.reshape(devices, capacity, D + 128), ("seq", "dp"), 0, 0, tiled=True)
    total = devices * capacity
    got = got.reshape(total, D + 128)
    got_ids = (got[:, D].astype(F32) * 32.0 + got[:, D + 1].astype(F32)).astype(jnp.int32) - 1
    rows_own = emb_table.shape[0]
    pick = (jnp.arange(rows_own, dtype=jnp.int32)[:, None] == got_ids[None, :]).astype(BF)
    table_grad = mm(pick, got[:, :D])
    new_accum = row_accum + jnp.mean(table_grad * table_grad, axis=1)
    new_table = emb_table - LEARN_RATE * table_grad * lax.rsqrt(new_accum)[:, None]
    return (gw[:, : 6 * DH], gw[:, 6 * DH :], go, new_table, new_accum)


def solution(mesh):
    placed = (
        P(("dp", "seq"), None),
        P(("dp", "seq"), None),
        P("dp", None),
        P(("dp", "seq"), None),
        P(("dp", "seq")),
        P(),
        P(),
        P(),
        P(("seq", "dp"), None),
        P(("seq", "dp")),
    )
    return jax.shard_map(
        body,
        mesh=mesh,
        in_specs=placed,
        out_specs=(
            P("dp", "seq"),
            P("dp", "seq"),
            P("dp", "seq"),
            P(("seq", "dp"), None),
            P(("seq", "dp")),
        ),
        check_vma=False,
    )
```

```python
import functools

import jax
import jax.numpy as jnp
from jax import lax
from jax.experimental import pallas as pl
from jax.experimental.pallas import tpu as pltpu
from jax.sharding import PartitionSpec as P

D = 1024
H = 16
DH = 64
NORM_EPS = 1e-05
LEARN_RATE = 0.1
TQ = 512
TK = 512
VMEM_BYTES = 56 * 1024 * 1024

BF = jnp.bfloat16
F32 = jnp.float32
NN = (((1,), (0,)), ((), ()))
NT = (((1,), (1,)), ((), ()))
MESH = pl.DeviceIdType.MESH


def mm(a, b, dims=NN):
    return lax.dot_general(a, b, dims, preferred_element_type=F32)


def silu(z):
    t = 0.5 * z
    return t + t * jnp.tanh(t)


def silu_grad(z):
    t = 0.5 * z
    th = jnp.tanh(t)
    return 0.5 * ((1.0 + th) * (1.0 + t * (1.0 - th)))


def event_starts(len_ref, places):
    end0 = len_ref[0]
    end1 = end0 + len_ref[1]
    return jnp.where(places >= end1, end1, jnp.where(places >= end0, end0, 0))


def scalar_start(len_ref, place):
    end0 = len_ref[0]
    end1 = end0 + len_ref[1]
    return jnp.where(place >= end1, end1, jnp.where(place >= end0, end0, 0))


def tile_allowed(len_ref, j, i):
    keys = j * TK + lax.broadcasted_iota(jnp.int32, (TK, TQ), 0)
    places = i * TQ + lax.broadcasted_iota(jnp.int32, (1, TQ), 1)
    return (keys >= event_starts(len_ref, places)) & (keys <= places)


def stat_place(pos, chunk, c):
    first = c * chunk
    row = 4 * (first // (pos // 2))
    lane = first % (pos // 2)
    return row, slice(lane, lane + chunk)


def bwd_kernel(
    pos, maxlen, seq_count,
    len_ref, sta_ref, h_ref, gate_ref, gsg_ref, mg_ref, q_ref, kt_ref, k_ref, v_ref, sg_hbm,
    g_ref, mix_ref,
    sg_s, sem, ot_s, dv_s, dk_s,
):
    sg_copy = pltpu.make_async_copy(sg_hbm, sg_s, sem)
    sg_copy.start()
    chunk = 512
    for c in range(pos // chunk):
        at = slice(c * chunk, (c + 1) * chunk)
        row, lane = stat_place(pos, chunk, c)
        means = [sta_ref[d, row : row + 1, lane] for d in range(seq_count)]
        mean = functools.reduce(jnp.add, means) * (1.0 / seq_count)
        var = jnp.zeros_like(mean)
        ng_mean = jnp.zeros_like(mean)
        ng_cov = jnp.zeros_like(mean)
        for d in range(seq_count):
            off = means[d] - mean
            ng_sum = sta_ref[d, row + 2 : row + 3, lane]
            var = var + sta_ref[d, row + 1 : row + 2, lane] + (2 * DH) * off * off
            ng_mean = ng_mean + ng_sum
            ng_cov = ng_cov + sta_ref[d, row + 3 : row + 4, lane] + off * ng_sum
        inv = lax.rsqrt(var * (1.0 / D) + NORM_EPS)
        ng_mean = ng_mean * (1.0 / D)
        proj = inv * ng_cov * (1.0 / D)
        gate = gate_ref[:, at]
        normed = (h_ref[:, at].astype(F32) - mean) * inv
        mix_ref[:, at] = (normed * gate).astype(BF)
        mg = mg_ref[:, at].astype(F32)
        g_ref[6 * DH :, at] = (mg * normed * gsg_ref[:, at]).astype(BF)
        hg = (inv * (mg * gate - ng_mean - normed * proj)).astype(BF)
        for hd in range(2):
            ot_s[hd, :, at] = hg[hd * DH : (hd + 1) * DH]
    dv_s[...] = jnp.zeros_like(dv_s)
    dk_s[...] = jnp.zeros_like(dk_s)
    fac = 0.0625 / maxlen

    @pl.loop(0, pos // TQ)
    def _(i):
        at = pl.ds(pl.multiple_of(i * TQ, TQ), TQ)
        first = scalar_start(len_ref, i * TQ) // TK
        last = ((i + 1) * TQ - 1) // TK

        def step(j, accs):
            kat = pl.ds(pl.multiple_of(j * TK, TK), TK)
            allowed = tile_allowed(len_ref, j, i)
            outs = []
            for hd in range(2):
                t = mm(k_ref[hd, kat, :], q_ref[hd, :, at])
                dw = mm(v_ref[hd, kat, :], ot_s[hd, :, at])
                a = 1.0 + jnp.tanh(t)
                w = t * a
                ds = jnp.where(allowed, dw * (a + w * (2.0 - a)), 0.0).astype(BF)
                w = jnp.where(allowed, w, 0.0).astype(BF)
                dv_s[hd, :, kat] += mm(ot_s[hd, :, at], w, NT)
                dk_s[hd, :, kat] += mm(q_ref[hd, :, at], ds, NT)
                outs.append(accs[hd] + mm(kt_ref[hd, :, kat], ds))
            return tuple(outs)

        zero = jnp.zeros((DH, TQ), F32)
        accs = lax.fori_loop(first, last + 1, step, (zero, zero))
        for hd in range(2):
            base = hd * 3 * DH + DH
            g_ref[base : base + DH, at] = (accs[hd] * fac).astype(BF)

    sg_copy.wait()

    @pl.loop(0, pos // chunk)
    def _(c):
        at = pl.ds(pl.multiple_of(c * chunk, chunk), chunk)
        for hd in range(2):
            base = hd * 3 * DH
            dv = (dv_s[hd, :, at] * (1.0 / maxlen)).astype(BF)
            dk = (dk_s[hd, :, at] * (16.0 * fac)).astype(BF)
            dq = g_ref[base + DH : base + 2 * DH, at]
            for part, grad in enumerate((dv, dq, dk)):
                rows = slice(base + part * DH, base + (part + 1) * DH)
                g_ref[rows, at] = (grad.astype(F32) * sg_s[rows, at]).astype(BF)


def vmem(count):
    return [pl.BlockSpec(memory_space=pltpu.VMEM)] * count


def backward(lens, stats, h, acts, pos, maxlen, seq_count):
    heads = pltpu.VMEM((2, DH, pos), BF)
    sums = pltpu.VMEM((2, DH, pos), F32)
    return pl.pallas_call(
        functools.partial(bwd_kernel, pos, maxlen, seq_count),
        out_shape=(
            jax.ShapeDtypeStruct((8 * DH, pos), BF),
            jax.ShapeDtypeStruct((2 * DH, pos), BF),
        ),
        in_specs=[pl.BlockSpec(memory_space=pltpu.SMEM)] + vmem(9) + [pl.BlockSpec(memory_space=pl.ANY)],
        out_specs=tuple(vmem(2)),
        scratch_shapes=[
            pltpu.VMEM((6 * DH, pos), F32),
            pltpu.SemaphoreType.DMA,
            heads, sums, sums,
        ],
        compiler_params=pltpu.CompilerParams(vmem_limit_bytes=VMEM_BYTES),
        name="backward",
    )(
        lens, stats, h, acts["gate"], acts["gsg"], acts["mg"],
        acts["q"], acts["kt"], acts["k"], acts["v"], acts["sg"],
    )


def seq_peers():
    me = lax.axis_index("seq")
    z, c = me // 2, me % 2
    at = lambda step: lax.rem(z + step, 4) * 2
    return me, at(0) + 1 - c, at(1) + c, at(3) + c, at(2) + c, c


def block_step(m):
    return lax.rem(3 * m + 3 * (m // 2) + 2 * (m // 3), 4)


def gather_kernel(
    tokens, maxlen,
    len_ref, x_ref, og_ref, wa_hbm, wg_hbm, wo_hbm,
    xg_ref, w_out, q_out, kt_out, k_out, v_out, sg_out, gate_out, gsg_out, mg_ref, h_ref, sta_ref,
    w_s, q_s, kt_s, k_s, v_s, sg_s, gate_s, gsg_s,
    x_s, wt_s, wo_s, mine_s, vt_s, acc_s, st_s,
    load_sem, keep_sem, send_sem, recv_sem, mg_send, mg_recv, st_send, st_recv,
):
    me, sib, right, left, far, c = seq_peers()
    z = me // 2
    pos = 8 * tokens
    half = tokens // 2
    loads = [
        pltpu.make_async_copy(x_ref, x_s.at[me], load_sem.at[0]),
        pltpu.make_async_copy(wa_hbm.at[:, pl.ds(pl.multiple_of(me * 6 * DH, 128), 6 * DH)], w_s.at[:, : 6 * DH], load_sem.at[1]),
        pltpu.make_async_copy(wg_hbm.at[:, pl.ds(pl.multiple_of(me * 2 * DH, 128), 2 * DH)], w_s.at[:, 6 * DH :], load_sem.at[2]),
        pltpu.make_async_copy(wo_hbm, wo_s, load_sem.at[3]),
    ]
    for load in loads:
        load.start()

    barrier = pltpu.get_barrier_semaphore()
    for step in range(1, 8):
        pl.semaphore_signal(barrier, inc=1, device_id={"seq": lax.rem(me + step, 8)}, device_id_type=MESH)
    acc_s[...] = jnp.zeros_like(acc_s)
    loads[0].wait()
    pl.semaphore_wait(barrier, 7)

    def remote(src, dst, send_sem, recv_sem, to):
        copy = pltpu.make_async_remote_copy(
            src_ref=src, dst_ref=dst, send_sem=send_sem, recv_sem=recv_sem, device_id={"seq": to}, device_id_type=MESH
        )
        copy.start()
        return copy

    def send(index, shard, part, to):
        ref = x_s.at[shard] if part is None else x_s.at[shard, pl.ds(part * half, half)]
        return remote(ref, ref, send_sem.at[index], recv_sem.at[index], to)

    keeps = []

    def keep(src, dst):
        copy = pltpu.make_async_copy(src, dst, keep_sem.at[len(keeps)])
        copy.start()
        keeps.append(copy)

    def project(shard):
        at = pl.ds(pl.multiple_of(shard * tokens, tokens), tokens)
        keep(x_s.at[shard], xg_ref.at[shard])
        pre = mm(wt_s[...], x_s[shard], NT)
        attn = pre[: 6 * DH]
        act = silu(attn).astype(BF)
        sg_s[:, at] = silu_grad(attn)
        gate = pre[6 * DH :]
        gate_s[:, at] = silu(gate)
        gsg_s[:, at] = silu_grad(gate)
        act_n = silu(mm(x_s[shard], w_s[:, : 6 * DH]))
        for hd in range(2):
            base = hd * 3 * DH
            vt_s[hd, :, at] = act[base : base + DH]
            q_s[hd, :, at] = (act[base + DH : base + 2 * DH] * 0.0625).astype(BF)
            kt_s[hd, :, at] = act[base + 2 * DH : base + 3 * DH]
            v_s[hd, at, :] = act_n[:, base : base + DH].astype(BF)
            k_s[hd, at, :] = act_n[:, base + 2 * DH : base + 3 * DH].astype(BF)

    def attend(n):
        new = lax.rem(z + block_step(n), 4)

        def tile(m, carry):
            old = lax.rem(z + block_step(m), 4)
            later = (new - old + 4) // 4
            i = later * new + (1 - later) * old
            j = new + old - i
            at = pl.ds(pl.multiple_of(i * TQ, TQ), TQ)
            kat = pl.ds(pl.multiple_of(j * TK, TK), TK)
            allowed = tile_allowed(len_ref, j, i)
            for hd in range(2):
                t = mm(k_s[hd, kat, :], q_s[hd, :, at])
                w = jnp.where(allowed, t + t * jnp.tanh(t), 0.0).astype(BF)
                acc_s[hd, :, at] += mm(vt_s[hd, :, kat], w)
            return carry

        lax.fori_loop(0, n + 1, tile, 0)

    to_right = [send(0, me, 0, right), None]
    to_left = [None, send(1, me, 1, left)]
    to_right[1] = send(2, me, 1, right)
    to_left[0] = send(3, me, 0, left)
    to_sib = send(4, me, None, sib)

    loads[1].wait()
    loads[2].wait()
    wt_s[...] = w_s[...].T
    keep(w_s, w_out)
    project(me)
    loads[3].wait()
    mine_s[...] = mm(wo_s[...], og_ref[...], NT).astype(BF)
    mine = pl.ds(pl.multiple_of(me * tokens, tokens), tokens)
    mg_ref[:, mine] = mine_s[pl.ds(pl.multiple_of(me * 2 * DH, 2 * DH), 2 * DH), :]
    to_sib.wait_recv()
    project(sib)

    to_right[0].wait_recv()
    fwd_r = send(5, left, 0, right)
    to_left[1].wait_recv()
    fwd_l = send(6, right, 1, left)
    attend(0)
    to_right[1].wait_recv()
    sib_left = send(7, left, None, sib)
    to_left[0].wait_recv()
    sib_right = send(8, right, None, sib)
    mg_copies = []
    for step in range(1, 8):
        to = lax.rem(me + step, 8)
        mg_copies.append(remote(
            mine_s.at[pl.ds(pl.multiple_of(to * 2 * DH, 2 * DH), 2 * DH)], mg_ref.at[:, mine],
            mg_send.at[step], mg_recv.at[step], to,
        ))
    other = 1 - 2 * c
    project(left)
    sib_left.wait_recv()
    project(left + other)
    attend(1)
    project(right)
    sib_right.wait_recv()
    project(right + other)
    fwd_r.wait_recv()
    sib_far0 = send(9, far, 0, sib)
    fwd_l.wait_recv()
    sib_far1 = send(10, far, 1, sib)
    attend(2)
    project(far)
    sib_far0.wait_recv()
    sib_far1.wait_recv()
    project(far + other)
    for src, dst in (
        (q_s, q_out), (kt_s, kt_out), (k_s, k_out), (v_s, v_out), (sg_s, sg_out), (gate_s, gate_out), (gsg_s, gsg_out)
    ):
        keep(src, dst)
    attend(3)
    for copy in mg_copies:
        copy.wait_recv()

    chunk = 512
    for ch in range(pos // chunk):
        at = slice(ch * chunk, (ch + 1) * chunk)
        row, lane = stat_place(pos, chunk, ch)
        for hd in range(2):
            h_ref[hd * DH : (hd + 1) * DH, at] = (acc_s[hd, :, at] * (1.0 / maxlen)).astype(BF)
        h = h_ref[:, at].astype(F32)
        mean = jnp.sum(h, axis=0, keepdims=True) * (1.0 / (2 * DH))
        cen = h - mean
        ng = mg_ref[:, at].astype(F32) * gate_s[:, at]
        st_s[row : row + 1, lane] = mean
        st_s[row + 1 : row + 2, lane] = jnp.sum(cen * cen, axis=0, keepdims=True)
        st_s[row + 2 : row + 3, lane] = jnp.sum(ng, axis=0, keepdims=True)
        st_s[row + 3 : row + 4, lane] = jnp.sum(ng * cen, axis=0, keepdims=True)
    st_copies = []
    for step in range(1, 8):
        st_copies.append(remote(st_s, sta_ref.at[me], st_send.at[step], st_recv.at[step], lax.rem(me + step, 8)))
    sta_ref[me] = st_s[...]
    for copy in st_copies:
        copy.wait()

    for copy in mg_copies + to_right + to_left + [to_sib, fwd_r, fwd_l, sib_left, sib_right, sib_far0, sib_far1]:
        copy.wait_send()
    for copy in keeps:
        copy.wait()


def gather(lens, x, og, w_attn, w_gate, w_out, tokens, seq_count, maxlen):
    pos = tokens * seq_count
    hbm = pl.BlockSpec(memory_space=pl.ANY)
    kept = [
        ((D, 8 * DH), BF),
        ((2, DH, pos), BF),
        ((2, DH, pos), BF),
        ((2, pos, DH), BF),
        ((2, pos, DH), BF),
        ((6 * DH, pos), F32),
        ((2 * DH, pos), F32),
        ((2 * DH, pos), F32),
    ]
    names = ("x", "w", "q", "kt", "k", "v", "sg", "gate", "gsg", "mg", "h", "stats")
    dma = lambda n: pltpu.SemaphoreType.DMA((n,))
    outs = pl.pallas_call(
        functools.partial(gather_kernel, tokens, maxlen),
        out_shape=tuple(
            [jax.ShapeDtypeStruct((seq_count, tokens, D), BF)]
            + [jax.ShapeDtypeStruct(shape, dtype) for shape, dtype in kept]
            + [
                jax.ShapeDtypeStruct((2 * DH, pos), BF),
                jax.ShapeDtypeStruct((2 * DH, pos), BF),
                jax.ShapeDtypeStruct((seq_count, 8, pos // 2), F32),
            ]
        ),
        in_specs=[pl.BlockSpec(memory_space=pltpu.SMEM), hbm] + vmem(1) + [hbm] * 3,
        out_specs=tuple([hbm] * 9 + vmem(3)),
        scratch_shapes=[pltpu.VMEM(shape, dtype) for shape, dtype in kept]
        + [
            pltpu.VMEM((seq_count, tokens, D), BF),
            pltpu.VMEM((8 * DH, D), BF),
            pltpu.VMEM((D, D), BF),
            pltpu.VMEM((D, tokens), BF),
            pltpu.VMEM((2, DH, pos), BF),
            pltpu.VMEM((2, DH, pos), F32),
            pltpu.VMEM((8, pos // 2), F32),
            dma(4), dma(16), dma(11), dma(11), dma(8), dma(8), dma(8), dma(8),
        ],
        compiler_params=pltpu.CompilerParams(
            vmem_limit_bytes=VMEM_BYTES, collective_id=0, has_side_effects=True
        ),
        name="gather",
    )(lens, x, og, w_attn, w_gate, w_out)
    return dict(zip(names, outs))


def reduce_kernel(
    tokens, dp_count, capacity,
    g_ref, w_ref, mix_ref, x_hbm, og_hbm, og_ref, owner_col_ref, owner_row_ref, row_ref,
    gsum_ref, gosum_ref, send_ref,
    x_s, og_s, out_s, pair_s, sum_s, far_s, ring_s, gsrc_s, gw_s, gosrc_s, col_s, go_s,
    load_sem, pair_send, pair_recv, ring_send, ring_recv, gw_send, gw_recv, col_send, col_recv, go_send, go_recv,
):
    me, sib, right, left, far, c = seq_peers()
    z = me // 2
    dp = lax.axis_index("dp")
    half = D // 2
    block = D // dp_count

    x_load = pltpu.make_async_copy(x_hbm, x_s, load_sem.at[0])
    og_load = pltpu.make_async_copy(og_hbm, og_s, load_sem.at[1])
    og_load.start()
    x_load.start()

    barrier = pltpu.get_barrier_semaphore()
    for step in range(1, 8):
        pl.semaphore_signal(barrier, inc=1, device_id={"seq": lax.rem(me + step, 8)}, device_id_type=MESH)
    for step in range(1, dp_count):
        pl.semaphore_signal(barrier, inc=1, device_id={"dp": lax.rem(dp + step, dp_count)}, device_id_type=MESH)
    pl.semaphore_wait(barrier, 7 + dp_count - 1)

    def remote(src, dst, send_sem, recv_sem, to):
        copy = pltpu.make_async_remote_copy(
            src_ref=src, dst_ref=dst, send_sem=send_sem, recv_sem=recv_sem, device_id=to, device_id_type=MESH
        )
        copy.start()
        return copy

    def partial_grad(shard):
        return mm(w_ref[...], g_ref[:, pl.ds(pl.multiple_of(shard * tokens, tokens), tokens)])

    pairs = {}
    for k in (2, 1, 3, 0):
        out_s[k] = partial_grad(lax.rem(z + k, 4) * 2 + 1 - c).astype(BF)
        pairs[k] = remote(out_s.at[k], pair_s.at[k], pair_send.at[k], pair_recv.at[k], {"seq": sib})

    def pair_sum(k):
        own = partial_grad(lax.rem(z + k, 4) * 2 + c)
        pairs[k].wait_recv()
        return own + pair_s[k].astype(F32)

    low, high = pl.ds(0, half), pl.ds(half, half)
    sum_s[2] = pair_sum(2).astype(BF)
    far_r = remote(sum_s.at[2, low], far_s.at[0], ring_send.at[0], ring_recv.at[0], {"seq": right})
    far_l = remote(sum_s.at[2, high], far_s.at[1], ring_send.at[1], ring_recv.at[1], {"seq": left})
    sum_s[1] = pair_sum(1).astype(BF)
    near_r = remote(sum_s.at[1, high], ring_s.at[0, high], ring_send.at[2], ring_recv.at[2], {"seq": right})
    sum_s[3] = pair_sum(3).astype(BF)
    near_l = remote(sum_s.at[3, low], ring_s.at[1, low], ring_send.at[3], ring_recv.at[3], {"seq": left})

    og_load.wait()
    gosrc_s[...] = mm(mix_ref[...], og_s[...]).astype(BF)
    cols = []
    for step in range(1, 8):
        to = lax.rem(me + step, 8)
        cols.append(remote(
            gosrc_s.at[:, pl.ds(pl.multiple_of(to * 2 * DH, 2 * DH), 2 * DH)], col_s.at[me],
            col_send.at[step], col_recv.at[step], {"seq": to},
        ))
    col_s[me] = gosrc_s[:, pl.ds(pl.multiple_of(me * 2 * DH, 2 * DH), 2 * DH)]
    x_load.wait()
    gsrc_s[...] = mm(g_ref[...], x_s[...]).astype(BF).T
    blocks = []
    for step in range(1, dp_count):
        to = lax.rem(dp + step, dp_count)
        blocks.append(remote(
            gsrc_s.at[pl.ds(pl.multiple_of(to * block, block), block)], gw_s.at[dp],
            gw_send.at[step], gw_recv.at[step], {"dp": to},
        ))
    gw_s[dp] = gsrc_s[pl.ds(pl.multiple_of(dp * block, block), block), :]

    far_r.wait_recv()
    sum_s[0, low] = (sum_s[1, low].astype(F32) + far_s[0].astype(F32)).astype(BF)
    end_r = remote(sum_s.at[0, low], ring_s.at[0, low], ring_send.at[4], ring_recv.at[4], {"seq": right})
    far_l.wait_recv()
    sum_s[0, high] = (sum_s[3, high].astype(F32) + far_s[1].astype(F32)).astype(BF)
    end_l = remote(sum_s.at[0, high], ring_s.at[1, high], ring_send.at[5], ring_recv.at[5], {"seq": left})

    for copy in cols:
        copy.wait_recv()
    gos = []
    for step in range(1, dp_count):
        to = lax.rem(dp + step, dp_count)
        gos.append(remote(
            col_s.at[to // 2, pl.ds(pl.multiple_of(lax.rem(to, 2) * block, block), block)], go_s.at[dp],
            go_send.at[step], go_recv.at[step], {"dp": to},
        ))
    go_s[dp] = col_s[dp // 2, pl.ds(pl.multiple_of(lax.rem(dp, 2) * block, block), block), :]

    mine = pair_sum(0)
    earlier = (lax.broadcasted_iota(jnp.int32, (tokens, tokens), 0) < lax.broadcasted_iota(jnp.int32, (tokens, tokens), 1))
    same = owner_col_ref[...] == owner_row_ref[...]
    rank = jnp.sum(jnp.where(earlier & same, 1.0, 0.0), axis=0, keepdims=True).astype(jnp.int32)
    slot = owner_row_ref[...] * capacity + rank
    total = send_ref.shape[0]
    hit = lax.broadcasted_iota(jnp.int32, (total, tokens), 0) == slot
    ident = jnp.sum(jnp.where(hit, (row_ref[...] + 1).astype(F32), 0.0), axis=1, keepdims=True).astype(jnp.int32)
    lanes = lax.broadcasted_iota(jnp.int32, (total, 128), 1)
    code = jnp.where(lanes == 0, ident // 32, jnp.where(lanes == 1, ident % 32, 0))
    send_ref[:, D:] = code.astype(F32).astype(BF)
    place = jnp.where(hit, 1.0, 0.0).astype(BF)

    for copy in blocks:
        copy.wait_recv()
    acc = gw_s[0].astype(F32)
    for d in range(1, dp_count):
        acc = acc + gw_s[d].astype(F32)
    gsum_ref[...] = acc
    for copy in gos:
        copy.wait_recv()
    acc = go_s[0].astype(F32)
    for d in range(1, dp_count):
        acc = acc + go_s[d].astype(F32)
    gosum_ref[...] = acc

    near_r.wait_recv()
    near_l.wait_recv()
    end_r.wait_recv()
    end_l.wait_recv()
    total_grad = (mine + ring_s[0].astype(F32) + ring_s[1].astype(F32)).astype(BF)
    send_ref[:, :D] = (mm(place, total_grad, NT) + mm(place, og_ref[...])).astype(BF)

    for copy in list(pairs.values()) + cols + blocks + gos + [far_r, far_l, near_r, near_l, end_r, end_l]:
        copy.wait_send()


def reduce_all(
    g, w, mix, x_g, og_g, og, item_owner, item_row, seq_count, dp_count, capacity, devices
):
    tokens = og.shape[0]
    pos = tokens * seq_count
    hbm = pl.BlockSpec(memory_space=pl.ANY)
    block = D // dp_count
    shard = lambda n: pltpu.VMEM((n, D, tokens), BF)
    dma = lambda n: pltpu.SemaphoreType.DMA((n,))
    return pl.pallas_call(
        functools.partial(reduce_kernel, tokens, dp_count, capacity),
        out_shape=(
            jax.ShapeDtypeStruct((block, 8 * DH), F32),
            jax.ShapeDtypeStruct((block, 2 * DH), F32),
            jax.ShapeDtypeStruct((devices * capacity, D + 128), BF),
        ),
        in_specs=vmem(3) + [hbm] * 2 + vmem(4),
        out_specs=tuple(vmem(3)),
        scratch_shapes=[
            pltpu.VMEM((pos, D), BF),
            pltpu.VMEM((pos, D), BF),
            shard(4), shard(4), shard(4),
            pltpu.VMEM((2, D // 2, tokens), BF),
            shard(2),
            pltpu.VMEM((D, 8 * DH), BF),
            pltpu.VMEM((dp_count, block, 8 * DH), BF),
            pltpu.VMEM((2 * DH, D), BF),
            pltpu.VMEM((seq_count, 2 * DH, 2 * DH), BF),
            pltpu.VMEM((dp_count, block, 2 * DH), BF),
            dma(2), dma(4), dma(4), dma(6), dma(6), dma(dp_count), dma(dp_count),
            dma(seq_count), dma(seq_count), dma(dp_count), dma(dp_count),
        ],
        compiler_params=pltpu.CompilerParams(vmem_limit_bytes=VMEM_BYTES, collective_id=2, has_side_effects=True),
        name="reduce_all",
    )(g, w, mix, x_g, og_g, og, item_owner, item_owner.reshape(1, tokens), item_row.reshape(1, tokens))


def body(
    layer_input,
    out_grad,
    lengths,
    item_owner,
    item_row,
    w_attn,
    w_gate,
    w_out,
    emb_table,
    row_accum,
):
    seq_count = lax.axis_size("seq")
    dp_count = lax.axis_size("dp")
    devices = seq_count * dp_count
    tokens_dev = layer_input.shape[0]
    pos = tokens_dev * seq_count
    maxlen = 2 * pos // 3
    capacity = max(2, 2 * tokens_dev // devices)
    lens = lengths[0]
    acts = gather(lens, layer_input, out_grad, w_attn, w_gate, w_out, tokens_dev, seq_count, maxlen)
    og_late, acts["mg"] = lax.optimization_barrier((out_grad, acts["mg"]))
    og_g = lax.all_gather(og_late, "seq", axis=0, tiled=True)
    g, mix = backward(lens, acts["stats"], acts["h"], acts, pos, maxlen, seq_count)
    gw, go, send_rows = reduce_all(
        g, acts["w"], mix, acts["x"].reshape(pos, D), og_g, out_grad, item_owner, item_row,
        seq_count, dp_count, capacity, devices,
    )
    got = lax.all_to_all(send_rows.reshape(devices, capacity, D + 128), ("seq", "dp"), 0, 0, tiled=True)
    total = devices * capacity
    got = got.reshape(total, D + 128)
    got_ids = (got[:, D].astype(F32) * 32.0 + got[:, D + 1].astype(F32)).astype(jnp.int32) - 1
    rows_own = emb_table.shape[0]
    pick = (jnp.arange(rows_own, dtype=jnp.int32)[:, None] == got_ids[None, :]).astype(BF)
    table_grad = mm(pick, got[:, :D])
    new_accum = row_accum + jnp.mean(table_grad * table_grad, axis=1)
    new_table = emb_table - LEARN_RATE * table_grad * lax.rsqrt(new_accum)[:, None]
    return (gw[:, : 6 * DH], gw[:, 6 * DH :], go, new_table, new_accum)


def solution(mesh):
    placed = (
        P(("dp", "seq"), None),
        P(("dp", "seq"), None),
        P("dp", None),
        P(("dp", "seq"), None),
        P(("dp", "seq")),
        P(),
        P(),
        P(),
        P(("seq", "dp"), None),
        P(("seq", "dp")),
    )
    return jax.shard_map(
        body,
        mesh=mesh,
        in_specs=placed,
        out_specs=(
            P("dp", "seq"),
            P("dp", "seq"),
            P("dp", "seq"),
            P(("seq", "dp"), None),
            P(("seq", "dp")),
        ),
        check_vma=False,
    )
```

```python
import functools

import jax
import jax.numpy as jnp
from jax import lax
from jax.experimental import pallas as pl
from jax.experimental.pallas import tpu as pltpu
from jax.sharding import PartitionSpec as P

D = 1024
H = 16
DH = 64
NORM_EPS = 1e-05
LEARN_RATE = 0.1
TQ = 512
TK = 512
VMEM_BYTES = 56 * 1024 * 1024

BF = jnp.bfloat16
F32 = jnp.float32
NN = (((1,), (0,)), ((), ()))
NT = (((1,), (1,)), ((), ()))
MESH = pl.DeviceIdType.MESH


def mm(a, b, dims=NN):
    return lax.dot_general(a, b, dims, preferred_element_type=F32)


def silu(z):
    t = 0.5 * z
    return t + t * jnp.tanh(t)


def silu_grad(z):
    t = 0.5 * z
    th = jnp.tanh(t)
    return 0.5 * ((1.0 + th) * (1.0 + t * (1.0 - th)))


def event_starts(len_ref, places):
    end0 = len_ref[0]
    end1 = end0 + len_ref[1]
    return jnp.where(places >= end1, end1, jnp.where(places >= end0, end0, 0))


def scalar_start(len_ref, place):
    end0 = len_ref[0]
    end1 = end0 + len_ref[1]
    return jnp.where(place >= end1, end1, jnp.where(place >= end0, end0, 0))


def tile_allowed(len_ref, j, i):
    keys = j * TK + lax.broadcasted_iota(jnp.int32, (TK, TQ), 0)
    places = i * TQ + lax.broadcasted_iota(jnp.int32, (1, TQ), 1)
    return (keys >= event_starts(len_ref, places)) & (keys <= places)


def stat_place(pos, chunk, c):
    first = c * chunk
    row = 4 * (first // (pos // 2))
    lane = first % (pos // 2)
    return row, slice(lane, lane + chunk)


def vmem(count):
    return [pl.BlockSpec(memory_space=pltpu.VMEM)] * count


def seq_peers():
    me = lax.axis_index("seq")
    z, c = me // 2, me % 2
    at = lambda step: lax.rem(z + step, 4) * 2
    return me, at(0) + 1 - c, at(1) + c, at(3) + c, at(2) + c, c


def block_step(m):
    return lax.rem(3 * m + 3 * (m // 2) + 2 * (m // 3), 4)


def gather_kernel(
    tokens, maxlen,
    len_ref, x_ref, og_ref, wa_hbm, wg_hbm, wo_hbm,
    xg_ref, w_out, q_out, kt_out, k_out, v_out, sg_out, gate_out, gsg_out, mg_ref, h_ref, sta_ref,
    w_s, q_s, kt_s, k_s, v_s, sg_s, gate_s, gsg_s,
    x_s, wt_s, wo_s, mine_s, vt_s, acc_s, st_s,
    load_sem, keep_sem, send_sem, recv_sem, mg_send, mg_recv, st_send, st_recv,
):
    me, sib, right, left, far, c = seq_peers()
    z = me // 2
    pos = 8 * tokens
    half = tokens // 2
    loads = [
        pltpu.make_async_copy(x_ref, x_s.at[me], load_sem.at[0]),
        pltpu.make_async_copy(wa_hbm.at[:, pl.ds(pl.multiple_of(me * 6 * DH, 128), 6 * DH)], w_s.at[:, : 6 * DH], load_sem.at[1]),
        pltpu.make_async_copy(wg_hbm.at[:, pl.ds(pl.multiple_of(me * 2 * DH, 128), 2 * DH)], w_s.at[:, 6 * DH :], load_sem.at[2]),
        pltpu.make_async_copy(wo_hbm, wo_s, load_sem.at[3]),
    ]
    for load in loads:
        load.start()

    barrier = pltpu.get_barrier_semaphore()
    for step in range(1, 8):
        pl.semaphore_signal(barrier, inc=1, device_id={"seq": lax.rem(me + step, 8)}, device_id_type=MESH)
    acc_s[...] = jnp.zeros_like(acc_s)
    loads[0].wait()
    pl.semaphore_wait(barrier, 7)

    def remote(src, dst, send_sem, recv_sem, to):
        copy = pltpu.make_async_remote_copy(
            src_ref=src, dst_ref=dst, send_sem=send_sem, recv_sem=recv_sem, device_id={"seq": to}, device_id_type=MESH
        )
        copy.start()
        return copy

    def send(index, shard, part, to):
        ref = x_s.at[shard] if part is None else x_s.at[shard, pl.ds(part * half, half)]
        return remote(ref, ref, send_sem.at[index], recv_sem.at[index], to)

    keeps = []

    def keep(src, dst):
        copy = pltpu.make_async_copy(src, dst, keep_sem.at[len(keeps)])
        copy.start()
        keeps.append(copy)

    def project(shard):
        at = pl.ds(pl.multiple_of(shard * tokens, tokens), tokens)
        keep(x_s.at[shard], xg_ref.at[shard])
        pre = mm(wt_s[...], x_s[shard], NT)
        attn = pre[: 6 * DH]
        act = silu(attn).astype(BF)
        sg_s[:, at] = silu_grad(attn)
        gate = pre[6 * DH :]
        gate_s[:, at] = silu(gate)
        gsg_s[:, at] = silu_grad(gate)
        act_n = silu(mm(x_s[shard], w_s[:, : 6 * DH]))
        for hd in range(2):
            base = hd * 3 * DH
            vt_s[hd, :, at] = act[base : base + DH]
            q_s[hd, :, at] = (act[base + DH : base + 2 * DH] * 0.0625).astype(BF)
            kt_s[hd, :, at] = act[base + 2 * DH : base + 3 * DH]
            v_s[hd, at, :] = act_n[:, base : base + DH].astype(BF)
            k_s[hd, at, :] = act_n[:, base + 2 * DH : base + 3 * DH].astype(BF)

    def attend(n):
        new = lax.rem(z + block_step(n), 4)

        def tile(m, carry):
            old = lax.rem(z + block_step(m), 4)
            later = (new - old + 4) // 4
            i = later * new + (1 - later) * old
            j = new + old - i
            at = pl.ds(pl.multiple_of(i * TQ, TQ), TQ)
            kat = pl.ds(pl.multiple_of(j * TK, TK), TK)
            allowed = tile_allowed(len_ref, j, i)
            for hd in range(2):
                t = mm(k_s[hd, kat, :], q_s[hd, :, at])
                w = jnp.where(allowed, t + t * jnp.tanh(t), 0.0).astype(BF)
                acc_s[hd, :, at] += mm(vt_s[hd, :, kat], w)
            return carry

        lax.fori_loop(0, n + 1, tile, 0)

    to_right = [send(0, me, 0, right), None]
    to_left = [None, send(1, me, 1, left)]
    to_right[1] = send(2, me, 1, right)
    to_left[0] = send(3, me, 0, left)
    to_sib = send(4, me, None, sib)

    loads[1].wait()
    loads[2].wait()
    wt_s[...] = w_s[...].T
    keep(w_s, w_out)
    project(me)
    loads[3].wait()
    mine_s[...] = mm(wo_s[...], og_ref[...], NT).astype(BF)
    mine = pl.ds(pl.multiple_of(me * tokens, tokens), tokens)
    mg_ref[:, mine] = mine_s[pl.ds(pl.multiple_of(me * 2 * DH, 2 * DH), 2 * DH), :]
    to_sib.wait_recv()
    project(sib)

    to_right[0].wait_recv()
    fwd_r = send(5, left, 0, right)
    to_left[1].wait_recv()
    fwd_l = send(6, right, 1, left)
    attend(0)
    to_right[1].wait_recv()
    sib_left = send(7, left, None, sib)
    to_left[0].wait_recv()
    sib_right = send(8, right, None, sib)
    other = 1 - 2 * c
    project(left)
    sib_left.wait_recv()
    project(left + other)
    attend(1)
    project(right)
    sib_right.wait_recv()
    project(right + other)
    fwd_r.wait_recv()
    sib_far0 = send(9, far, 0, sib)
    fwd_l.wait_recv()
    sib_far1 = send(10, far, 1, sib)
    mg_copies = []
    for step in range(1, 8):
        to = lax.rem(me + step, 8)
        mg_copies.append(remote(
            mine_s.at[pl.ds(pl.multiple_of(to * 2 * DH, 2 * DH), 2 * DH)], mg_ref.at[:, mine],
            mg_send.at[step], mg_recv.at[step], to,
        ))
    attend(2)
    project(far)
    sib_far0.wait_recv()
    sib_far1.wait_recv()
    project(far + other)
    for src, dst in (
        (q_s, q_out), (kt_s, kt_out), (k_s, k_out), (v_s, v_out), (sg_s, sg_out), (gate_s, gate_out), (gsg_s, gsg_out)
    ):
        keep(src, dst)
    attend(3)
    for copy in mg_copies:
        copy.wait_recv()

    chunk = 512
    for ch in range(pos // chunk):
        at = slice(ch * chunk, (ch + 1) * chunk)
        row, lane = stat_place(pos, chunk, ch)
        for hd in range(2):
            h_ref[hd * DH : (hd + 1) * DH, at] = (acc_s[hd, :, at] * (1.0 / maxlen)).astype(BF)
        h = h_ref[:, at].astype(F32)
        mean = jnp.sum(h, axis=0, keepdims=True) * (1.0 / (2 * DH))
        cen = h - mean
        ng = mg_ref[:, at].astype(F32) * gate_s[:, at]
        st_s[row : row + 1, lane] = mean
        st_s[row + 1 : row + 2, lane] = jnp.sum(cen * cen, axis=0, keepdims=True)
        st_s[row + 2 : row + 3, lane] = jnp.sum(ng, axis=0, keepdims=True)
        st_s[row + 3 : row + 4, lane] = jnp.sum(ng * cen, axis=0, keepdims=True)
    st_copies = []
    for step in range(1, 8):
        st_copies.append(remote(st_s, sta_ref.at[me], st_send.at[step], st_recv.at[step], lax.rem(me + step, 8)))
    sta_ref[me] = st_s[...]
    for copy in st_copies:
        copy.wait()

    for copy in mg_copies + to_right + to_left + [to_sib, fwd_r, fwd_l, sib_left, sib_right, sib_far0, sib_far1]:
        copy.wait_send()
    for copy in keeps:
        copy.wait()


def gather(lens, x, og, w_attn, w_gate, w_out, tokens, seq_count, maxlen):
    pos = tokens * seq_count
    hbm = pl.BlockSpec(memory_space=pl.ANY)
    kept = [
        ((D, 8 * DH), BF),
        ((2, DH, pos), BF),
        ((2, DH, pos), BF),
        ((2, pos, DH), BF),
        ((2, pos, DH), BF),
        ((6 * DH, pos), F32),
        ((2 * DH, pos), F32),
        ((2 * DH, pos), F32),
    ]
    names = ("x", "w", "q", "kt", "k", "v", "sg", "gate", "gsg", "mg", "h", "stats")
    dma = lambda n: pltpu.SemaphoreType.DMA((n,))
    outs = pl.pallas_call(
        functools.partial(gather_kernel, tokens, maxlen),
        out_shape=tuple(
            [jax.ShapeDtypeStruct((seq_count, tokens, D), BF)]
            + [jax.ShapeDtypeStruct(shape, dtype) for shape, dtype in kept]
            + [
                jax.ShapeDtypeStruct((2 * DH, pos), BF),
                jax.ShapeDtypeStruct((2 * DH, pos), BF),
                jax.ShapeDtypeStruct((seq_count, 8, pos // 2), F32),
            ]
        ),
        in_specs=[pl.BlockSpec(memory_space=pltpu.SMEM), hbm] + vmem(1) + [hbm] * 3,
        out_specs=tuple([hbm] * 9 + vmem(3)),
        scratch_shapes=[pltpu.VMEM(shape, dtype) for shape, dtype in kept]
        + [
            pltpu.VMEM((seq_count, tokens, D), BF),
            pltpu.VMEM((8 * DH, D), BF),
            pltpu.VMEM((D, D), BF),
            pltpu.VMEM((D, tokens), BF),
            pltpu.VMEM((2, DH, pos), BF),
            pltpu.VMEM((2, DH, pos), F32),
            pltpu.VMEM((8, pos // 2), F32),
            dma(4), dma(16), dma(11), dma(11), dma(8), dma(8), dma(8), dma(8),
        ],
        compiler_params=pltpu.CompilerParams(
            vmem_limit_bytes=VMEM_BYTES, collective_id=0, has_side_effects=True
        ),
        name="gather",
    )(lens, x, og, w_attn, w_gate, w_out)
    return dict(zip(names, outs))


def grads_kernel(
    tokens, maxlen, dp_count, capacity,
    len_ref, sta_ref, h_ref, gate_ref, gsg_ref, mg_ref, q_ref, kt_ref, k_ref, v_ref, w_ref, sg_hbm, x_hbm,
    og_ref, owner_col_ref, owner_row_ref, row_ref,
    gsum_ref, gosum_ref, send_ref,
    sg_s, x_s, mix_s, ot_s, dv_s, dk_s, dq_s, g_s, gacc_s,
    out_s, pair_s, sum_s, far_s, ring_s,
    mixr_s, gop_s, gopair_s, gosum_s, gor_s, goout_s, gocol_s, gsrc_s, gw_s,
    load_sem, mix_send, mix_recv, pair_send, pair_recv, ring_send, ring_recv,
    gp_send, gp_recv, go_send, go_recv, gc_send, gc_recv, gw_send, gw_recv,
):
    me, sib, right, left, _, c = seq_peers()
    z = me // 2
    dp = lax.axis_index("dp")
    seq_count = 8
    pos = seq_count * tokens
    span = 2 * tokens
    half = D // 2
    block = D // dp_count
    hb = block // 2

    sg_load = pltpu.make_async_copy(sg_hbm, sg_s, load_sem.at[0])
    x_load = pltpu.make_async_copy(x_hbm, x_s, load_sem.at[1])
    sg_load.start()
    x_load.start()
    barrier = pltpu.get_barrier_semaphore()
    for step in range(1, seq_count):
        pl.semaphore_signal(barrier, inc=1, device_id={"seq": lax.rem(me + step, seq_count)}, device_id_type=MESH)
    for step in range(1, dp_count):
        pl.semaphore_signal(barrier, inc=1, device_id={"dp": lax.rem(dp + step, dp_count)}, device_id_type=MESH)

    def describe(src, dst, send_sem, recv_sem, to):
        return pltpu.make_async_remote_copy(
            src_ref=src, dst_ref=dst, send_sem=send_sem, recv_sem=recv_sem, device_id=to, device_id_type=MESH
        )

    def remote(*args):
        copy = describe(*args)
        copy.start()
        return copy

    for ch in range(pos // span):
        at = slice(ch * span, (ch + 1) * span)
        row, lane = stat_place(pos, span, ch)
        means = [sta_ref[d, row : row + 1, lane] for d in range(seq_count)]
        mean = functools.reduce(jnp.add, means) * (1.0 / seq_count)
        var = jnp.zeros_like(mean)
        ng_mean = jnp.zeros_like(mean)
        ng_cov = jnp.zeros_like(mean)
        for d in range(seq_count):
            off = means[d] - mean
            ng_sum = sta_ref[d, row + 2 : row + 3, lane]
            var = var + sta_ref[d, row + 1 : row + 2, lane] + (2 * DH) * off * off
            ng_mean = ng_mean + ng_sum
            ng_cov = ng_cov + sta_ref[d, row + 3 : row + 4, lane] + off * ng_sum
        inv = lax.rsqrt(var * (1.0 / D) + NORM_EPS)
        ng_mean = ng_mean * (1.0 / D)
        proj = inv * ng_cov * (1.0 / D)
        gate = gate_ref[:, at]
        normed = (h_ref[:, at].astype(F32) - mean) * inv
        mix_s[:, at] = (normed * gate).astype(BF)
        mg = mg_ref[:, at].astype(F32)
        g_s[6 * DH :, at] = (mg * normed * gsg_ref[:, at]).astype(BF)
        hg = (inv * (mg * gate - ng_mean - normed * proj)).astype(BF)
        for hd in range(2):
            ot_s[hd, :, at] = hg[hd * DH : (hd + 1) * DH]
    dv_s[...] = jnp.zeros_like(dv_s)
    dk_s[...] = jnp.zeros_like(dk_s)
    dq_s[...] = jnp.zeros_like(dq_s)
    fac = 0.0625 / maxlen

    pl.semaphore_wait(barrier, seq_count - 1 + dp_count - 1)
    feats = pl.ds(pl.multiple_of(me * 2 * DH, 2 * DH), 2 * DH)
    mixes = []
    for step in range(1, seq_count):
        to = lax.rem(me + step, seq_count)
        mixes.append(remote(
            mix_s.at[:, pl.ds(pl.multiple_of(to * tokens, tokens), tokens)], mixr_s.at[feats],
            mix_send.at[step], mix_recv.at[step], {"seq": to},
        ))
    mixr_s[feats, :] = mix_s[:, pl.ds(pl.multiple_of(me * tokens, tokens), tokens)]

    def chip_block(k):
        return lax.rem(z + k, 4)

    def lanes_of(b):
        return pl.ds(pl.multiple_of(b * span, span), span)

    def attend(n):
        new = chip_block(block_step(3 - n))

        def tile(m, carry):
            old = chip_block(block_step(3 - m))
            later = (new - old + 4) // 4
            i = later * new + (1 - later) * old
            j = new + old - i
            at, kat = lanes_of(i), lanes_of(j)
            allowed = tile_allowed(len_ref, j, i)
            for hd in range(2):
                t = mm(k_ref[hd, kat, :], q_ref[hd, :, at])
                dw = mm(v_ref[hd, kat, :], ot_s[hd, :, at])
                a = 1.0 + jnp.tanh(t)
                w = t * a
                ds = jnp.where(allowed, dw * (a + w * (2.0 - a)), 0.0).astype(BF)
                w = jnp.where(allowed, w, 0.0).astype(BF)
                dv_s[hd, :, kat] += mm(ot_s[hd, :, at], w, NT)
                dk_s[hd, :, kat] += mm(q_ref[hd, :, at], ds, NT)
                dq_s[hd, :, at] += mm(kt_ref[hd, :, kat], ds)
            return carry

        lax.fori_loop(n, 4, tile, 0)
        at = lanes_of(new)
        for hd in range(2):
            base = hd * 3 * DH
            dv = (dv_s[hd, :, at] * (1.0 / maxlen)).astype(BF)
            dk = (dk_s[hd, :, at] * (16.0 * fac)).astype(BF)
            dq = (dq_s[hd, :, at] * fac).astype(BF)
            for part, grad in enumerate((dv, dq, dk)):
                rows = slice(base + part * DH, base + (part + 1) * DH)
                g_s[rows, at] = (grad.astype(F32) * sg_s[rows, at]).astype(BF)

    def partial_grad(k, core):
        first = chip_block(k) * span + core * tokens
        return mm(w_ref[...], g_s[:, pl.ds(pl.multiple_of(first, tokens), tokens)])

    pairs = {}

    def share(k):
        out_s[k] = partial_grad(k, 1 - c).astype(BF)
        pairs[k] = remote(out_s.at[k], pair_s.at[k], pair_send.at[k], pair_recv.at[k], {"seq": sib})
        at = lanes_of(chip_block(k))
        part = mm(g_s[:, at], x_s[at, :])
        gacc_s[...] = part if k == 2 else gacc_s[...] + part

    low, high = pl.ds(0, half), pl.ds(half, half)
    hops = [
        describe(sum_s.at[2, low], far_s.at[0], ring_send.at[0], ring_recv.at[0], {"seq": right}),
        describe(sum_s.at[2, high], far_s.at[1], ring_send.at[1], ring_recv.at[1], {"seq": left}),
        describe(sum_s.at[1, high], ring_s.at[0, high], ring_send.at[2], ring_recv.at[2], {"seq": right}),
        describe(sum_s.at[3, low], ring_s.at[1, low], ring_send.at[3], ring_recv.at[3], {"seq": left}),
        describe(sum_s.at[1, low], ring_s.at[0, low], ring_send.at[4], ring_recv.at[4], {"seq": right}),
        describe(sum_s.at[3, high], ring_s.at[1, high], ring_send.at[5], ring_recv.at[5], {"seq": left}),
    ]

    def settle(k):
        own = partial_grad(k, c)
        pairs[k].wait_recv()
        sum_s[k] = (own + pair_s[k].astype(F32)).astype(BF)

    sg_load.wait()
    attend(0)
    x_load.wait()
    share(2)
    settle(2)
    hops[0].start()
    hops[1].start()

    for copy in mixes:
        copy.wait_recv()
    gop_s[...] = mm(mixr_s[...], og_ref[...]).astype(BF).reshape(dp_count, block, D)
    mine = pl.ds(pl.multiple_of(c * hb, hb), hb)
    theirs = pl.ds(pl.multiple_of((1 - c) * hb, hb), hb)
    go_pair = remote(gop_s.at[:, theirs], gopair_s, gp_send.at[0], gp_recv.at[0], {"seq": sib})

    attend(1)
    share(1)
    settle(1)
    hops[2].start()
    go_pair.wait_recv()
    gosum_s[...] = (gop_s[:, mine, :].astype(F32) + gopair_s[...].astype(F32)).astype(BF)
    gos = []
    for step in range(1, dp_count):
        to = lax.rem(dp + step, dp_count)
        gos.append(remote(gosum_s.at[to], gor_s.at[dp], go_send.at[step], go_recv.at[step], {"dp": to}))
    gor_s[dp] = gosum_s[dp]
    hops[0].wait_recv()
    sum_s[1, low] = (sum_s[1, low].astype(F32) + far_s[0].astype(F32)).astype(BF)
    hops[4].start()

    attend(2)
    share(3)
    settle(3)
    hops[3].start()
    hops[1].wait_recv()
    sum_s[3, high] = (sum_s[3, high].astype(F32) + far_s[1].astype(F32)).astype(BF)
    hops[5].start()

    attend(3)
    share(0)
    gsrc_s[...] = gacc_s[...].astype(BF).T
    blocks = []
    for step in range(1, dp_count):
        to = lax.rem(dp + step, dp_count)
        blocks.append(remote(
            gsrc_s.at[pl.ds(pl.multiple_of(to * block, block), block)], gw_s.at[dp],
            gw_send.at[step], gw_recv.at[step], {"dp": to},
        ))
    gw_s[dp] = gsrc_s[pl.ds(pl.multiple_of(dp * block, block), block), :]
    settle(0)

    earlier = (lax.broadcasted_iota(jnp.int32, (tokens, tokens), 0) < lax.broadcasted_iota(jnp.int32, (tokens, tokens), 1))
    same = owner_col_ref[...] == owner_row_ref[...]
    rank = jnp.sum(jnp.where(earlier & same, 1.0, 0.0), axis=0, keepdims=True).astype(jnp.int32)
    slot = owner_row_ref[...] * capacity + rank
    total = send_ref.shape[0]
    hit = lax.broadcasted_iota(jnp.int32, (total, tokens), 0) == slot
    ident = jnp.sum(jnp.where(hit, (row_ref[...] + 1).astype(F32), 0.0), axis=1, keepdims=True).astype(jnp.int32)
    lanes = lax.broadcasted_iota(jnp.int32, (total, 128), 1)
    code = jnp.where(lanes == 0, ident // 32, jnp.where(lanes == 1, ident % 32, 0))
    send_ref[:, D:] = code.astype(F32).astype(BF)
    place = jnp.where(hit, 1.0, 0.0).astype(BF)

    for copy in gos:
        copy.wait_recv()
    acc = gor_s[0].astype(F32)
    for d in range(1, dp_count):
        acc = acc + gor_s[d].astype(F32)
    goout_s[...] = acc.astype(BF)
    cols = []
    for step in range(1, seq_count):
        to = lax.rem(me + step, seq_count)
        cols.append(remote(
            goout_s.at[:, pl.ds(pl.multiple_of(to * 2 * DH, 2 * DH), 2 * DH)], gocol_s.at[me],
            gc_send.at[step], gc_recv.at[step], {"seq": to},
        ))
    gocol_s[me] = goout_s[:, pl.ds(pl.multiple_of(me * 2 * DH, 2 * DH), 2 * DH)]

    for hop in hops[2:]:
        hop.wait_recv()
    total_grad = (sum_s[0].astype(F32) + ring_s[0].astype(F32) + ring_s[1].astype(F32)).astype(BF)
    send_ref[:, :D] = (mm(place, total_grad, NT) + mm(place, og_ref[...])).astype(BF)

    for copy in cols:
        copy.wait_recv()
    for core in range(2):
        acc = gocol_s[core].astype(F32)
        for chip in range(1, 4):
            acc = acc + gocol_s[2 * chip + core].astype(F32)
        gosum_ref[core * hb : (core + 1) * hb, :] = acc
    for copy in blocks:
        copy.wait_recv()
    acc = gw_s[0].astype(F32)
    for d in range(1, dp_count):
        acc = acc + gw_s[d].astype(F32)
    gsum_ref[...] = acc

    for copy in mixes + list(pairs.values()) + hops + [go_pair] + gos + cols + blocks:
        copy.wait_send()


def grads(lens, acts, og, item_owner, item_row, seq_count, dp_count, capacity, devices, maxlen):
    tokens = og.shape[0]
    pos = tokens * seq_count
    hbm = pl.BlockSpec(memory_space=pl.ANY)
    block = D // dp_count
    bf = lambda *shape: pltpu.VMEM(shape, BF)
    f32 = lambda *shape: pltpu.VMEM(shape, F32)
    dma = lambda n: pltpu.SemaphoreType.DMA((n,))
    return pl.pallas_call(
        functools.partial(grads_kernel, tokens, maxlen, dp_count, capacity),
        out_shape=(
            jax.ShapeDtypeStruct((block, 8 * DH), F32),
            jax.ShapeDtypeStruct((block, 2 * DH), F32),
            jax.ShapeDtypeStruct((devices * capacity, D + 128), BF),
        ),
        in_specs=[pl.BlockSpec(memory_space=pltpu.SMEM)] + vmem(10) + [hbm] * 2 + vmem(4),
        out_specs=tuple(vmem(3)),
        scratch_shapes=[
            f32(6 * DH, pos), bf(pos, D), bf(2 * DH, pos), bf(2, DH, pos),
            f32(2, DH, pos), f32(2, DH, pos), f32(2, DH, pos), bf(8 * DH, pos), f32(8 * DH, D),
            bf(4, D, tokens), bf(4, D, tokens), bf(4, D, tokens), bf(2, D // 2, tokens), bf(2, D, tokens),
            bf(D, tokens), bf(dp_count, block, D), bf(dp_count, block // 2, D), bf(dp_count, block // 2, D),
            bf(dp_count, block // 2, D), bf(block // 2, D), bf(seq_count, block // 2, 2 * DH),
            bf(D, 8 * DH), bf(dp_count, block, 8 * DH),
            dma(2), dma(seq_count), dma(seq_count), dma(4), dma(4), dma(6), dma(6),
            dma(1), dma(1), dma(dp_count), dma(dp_count), dma(seq_count), dma(seq_count), dma(dp_count), dma(dp_count),
        ],
        compiler_params=pltpu.CompilerParams(vmem_limit_bytes=VMEM_BYTES, collective_id=2, has_side_effects=True),
        name="grads",
    )(
        lens, acts["stats"], acts["h"], acts["gate"], acts["gsg"], acts["mg"], acts["q"], acts["kt"], acts["k"],
        acts["v"], acts["w"], acts["sg"], acts["x"].reshape(pos, D),
        og, item_owner, item_owner.reshape(1, tokens), item_row.reshape(1, tokens),
    )


def body(
    layer_input,
    out_grad,
    lengths,
    item_owner,
    item_row,
    w_attn,
    w_gate,
    w_out,
    emb_table,
    row_accum,
):
    seq_count = lax.axis_size("seq")
    dp_count = lax.axis_size("dp")
    devices = seq_count * dp_count
    tokens_dev = layer_input.shape[0]
    pos = tokens_dev * seq_count
    maxlen = 2 * pos // 3
    capacity = max(2, 2 * tokens_dev // devices)
    lens = lengths[0]
    acts = gather(lens, layer_input, out_grad, w_attn, w_gate, w_out, tokens_dev, seq_count, maxlen)
    gw, go, send_rows = grads(
        lens, acts, out_grad, item_owner, item_row, seq_count, dp_count, capacity, devices, maxlen
    )
    got = lax.all_to_all(send_rows.reshape(devices, capacity, D + 128), ("seq", "dp"), 0, 0, tiled=True)
    total = devices * capacity
    got = got.reshape(total, D + 128)
    got_ids = (got[:, D].astype(F32) * 32.0 + got[:, D + 1].astype(F32)).astype(jnp.int32) - 1
    rows_own = emb_table.shape[0]
    pick = (jnp.arange(rows_own, dtype=jnp.int32)[:, None] == got_ids[None, :]).astype(BF)
    table_grad = mm(pick, got[:, :D])
    new_accum = row_accum + jnp.mean(table_grad * table_grad, axis=1)
    new_table = emb_table - LEARN_RATE * table_grad * lax.rsqrt(new_accum)[:, None]
    return (gw[:, : 6 * DH], gw[:, 6 * DH :], go, new_table, new_accum)


def solution(mesh):
    placed = (
        P(("dp", "seq"), None),
        P(("dp", "seq"), None),
        P("dp", None),
        P(("dp", "seq"), None),
        P(("dp", "seq")),
        P(),
        P(),
        P(),
        P(("seq", "dp"), None),
        P(("seq", "dp")),
    )
    return jax.shard_map(
        body,
        mesh=mesh,
        in_specs=placed,
        out_specs=(
            P("dp", "seq"),
            P("dp", "seq"),
            P("dp", "seq"),
            P(("seq", "dp"), None),
            P(("seq", "dp")),
        ),
        check_vma=False,
    )
```

```python
import functools

import jax
import jax.numpy as jnp
from jax import lax
from jax.experimental import pallas as pl
from jax.experimental.pallas import tpu as pltpu
from jax.sharding import PartitionSpec as P

D = 1024
H = 16
DH = 64
NORM_EPS = 1e-05
LEARN_RATE = 0.1
TQ = 512
TK = 512
VMEM_BYTES = 56 * 1024 * 1024

BF = jnp.bfloat16
F32 = jnp.float32
NN = (((1,), (0,)), ((), ()))
NT = (((1,), (1,)), ((), ()))
MESH = pl.DeviceIdType.MESH


def mm(a, b, dims=NN):
    return lax.dot_general(a, b, dims, preferred_element_type=F32)


def silu(z):
    t = 0.5 * z
    return t + t * jnp.tanh(t)


def silu_grad(z):
    t = 0.5 * z
    th = jnp.tanh(t)
    return 0.5 * ((1.0 + th) * (1.0 + t * (1.0 - th)))


def event_starts(len_ref, places):
    end0 = len_ref[0]
    end1 = end0 + len_ref[1]
    return jnp.where(places >= end1, end1, jnp.where(places >= end0, end0, 0))


def scalar_start(len_ref, place):
    end0 = len_ref[0]
    end1 = end0 + len_ref[1]
    return jnp.where(place >= end1, end1, jnp.where(place >= end0, end0, 0))


def tile_allowed(len_ref, j, i):
    keys = j * TK + lax.broadcasted_iota(jnp.int32, (TK, TQ), 0)
    places = i * TQ + lax.broadcasted_iota(jnp.int32, (1, TQ), 1)
    return (keys >= event_starts(len_ref, places)) & (keys <= places)


def stat_place(pos, chunk, c):
    first = c * chunk
    row = 4 * (first // (pos // 2))
    lane = first % (pos // 2)
    return row, slice(lane, lane + chunk)


def vmem(count):
    return [pl.BlockSpec(memory_space=pltpu.VMEM)] * count


def seq_peers():
    me = lax.axis_index("seq")
    z, c = me // 2, me % 2
    at = lambda step: lax.rem(z + step, 4) * 2
    return me, at(0) + 1 - c, at(1) + c, at(3) + c, at(2) + c, c


def block_step(m):
    return lax.rem(3 * m + 3 * (m // 2) + 2 * (m // 3), 4)


def gather_kernel(
    tokens, maxlen,
    len_ref, id_ref, x_ref, og_ref, wa_hbm, wg_hbm, wo_hbm,
    xg_ref, w_out, q_out, kt_out, k_out, v_out, sg_out, gate_out, gsg_out, mg_ref, h_ref, sta_ref, idg_ref,
    w_s, q_s, kt_s, k_s, v_s, sg_s, gate_s, gsg_s,
    x_s, wt_s, wo_s, mine_s, vt_s, acc_s, st_s,
    load_sem, keep_sem, send_sem, recv_sem, mg_send, mg_recv, st_send, st_recv, id_send, id_recv,
):
    me, sib, right, left, far, c = seq_peers()
    z = me // 2
    pos = 8 * tokens
    half = tokens // 2
    loads = [
        pltpu.make_async_copy(x_ref, x_s.at[me], load_sem.at[0]),
        pltpu.make_async_copy(wa_hbm.at[:, pl.ds(pl.multiple_of(me * 6 * DH, 128), 6 * DH)], w_s.at[:, : 6 * DH], load_sem.at[1]),
        pltpu.make_async_copy(wg_hbm.at[:, pl.ds(pl.multiple_of(me * 2 * DH, 128), 2 * DH)], w_s.at[:, 6 * DH :], load_sem.at[2]),
        pltpu.make_async_copy(wo_hbm, wo_s, load_sem.at[3]),
    ]
    for load in loads:
        load.start()

    barrier = pltpu.get_barrier_semaphore()
    for step in range(1, 8):
        pl.semaphore_signal(barrier, inc=1, device_id={"seq": lax.rem(me + step, 8)}, device_id_type=MESH)
    acc_s[...] = jnp.zeros_like(acc_s)
    loads[0].wait()
    pl.semaphore_wait(barrier, 7)

    def remote(src, dst, send_sem, recv_sem, to):
        copy = pltpu.make_async_remote_copy(
            src_ref=src, dst_ref=dst, send_sem=send_sem, recv_sem=recv_sem, device_id={"seq": to}, device_id_type=MESH
        )
        copy.start()
        return copy

    def send(index, shard, part, to):
        ref = x_s.at[shard] if part is None else x_s.at[shard, pl.ds(part * half, half)]
        return remote(ref, ref, send_sem.at[index], recv_sem.at[index], to)

    keeps = []

    def keep(src, dst):
        copy = pltpu.make_async_copy(src, dst, keep_sem.at[len(keeps)])
        copy.start()
        keeps.append(copy)

    def project(shard):
        at = pl.ds(pl.multiple_of(shard * tokens, tokens), tokens)
        keep(x_s.at[shard], xg_ref.at[shard])
        pre = mm(wt_s[...], x_s[shard], NT)
        attn = pre[: 6 * DH]
        act = silu(attn).astype(BF)
        sg_s[:, at] = silu_grad(attn)
        gate = pre[6 * DH :]
        gate_s[:, at] = silu(gate)
        gsg_s[:, at] = silu_grad(gate)
        act_n = silu(mm(x_s[shard], w_s[:, : 6 * DH]))
        for hd in range(2):
            base = hd * 3 * DH
            vt_s[hd, :, at] = act[base : base + DH]
            q_s[hd, :, at] = (act[base + DH : base + 2 * DH] * 0.0625).astype(BF)
            kt_s[hd, :, at] = act[base + 2 * DH : base + 3 * DH]
            v_s[hd, at, :] = act_n[:, base : base + DH].astype(BF)
            k_s[hd, at, :] = act_n[:, base + 2 * DH : base + 3 * DH].astype(BF)

    def attend(n):
        new = lax.rem(z + block_step(n), 4)

        def tile(m, carry):
            old = lax.rem(z + block_step(m), 4)
            later = (new - old + 4) // 4
            i = later * new + (1 - later) * old
            j = new + old - i
            at = pl.ds(pl.multiple_of(i * TQ, TQ), TQ)
            kat = pl.ds(pl.multiple_of(j * TK, TK), TK)
            allowed = tile_allowed(len_ref, j, i)
            for hd in range(2):
                t = mm(k_s[hd, kat, :], q_s[hd, :, at])
                w = jnp.where(allowed, t + t * jnp.tanh(t), 0.0).astype(BF)
                acc_s[hd, :, at] += mm(vt_s[hd, :, kat], w)
            return carry

        lax.fori_loop(0, n + 1, tile, 0)

    to_right = [send(0, me, 0, right), None]
    to_left = [None, send(1, me, 1, left)]
    to_right[1] = send(2, me, 1, right)
    to_left[0] = send(3, me, 0, left)
    to_sib = send(4, me, None, sib)
    id_copies = []
    for step in range(1, 8):
        id_copies.append(remote(id_ref, idg_ref.at[me], id_send.at[step], id_recv.at[step], lax.rem(me + step, 8)))
    idg_ref[me] = id_ref[...]

    loads[1].wait()
    loads[2].wait()
    wt_s[...] = w_s[...].T
    keep(w_s, w_out)
    project(me)
    loads[3].wait()
    mine_s[...] = mm(wo_s[...], og_ref[...], NT).astype(BF)
    mine = pl.ds(pl.multiple_of(me * tokens, tokens), tokens)
    mg_ref[:, mine] = mine_s[pl.ds(pl.multiple_of(me * 2 * DH, 2 * DH), 2 * DH), :]
    to_sib.wait_recv()
    project(sib)

    to_right[0].wait_recv()
    fwd_r = send(5, left, 0, right)
    to_left[1].wait_recv()
    fwd_l = send(6, right, 1, left)
    attend(0)
    to_right[1].wait_recv()
    sib_left = send(7, left, None, sib)
    to_left[0].wait_recv()
    sib_right = send(8, right, None, sib)
    other = 1 - 2 * c
    project(left)
    sib_left.wait_recv()
    project(left + other)
    attend(1)
    project(right)
    sib_right.wait_recv()
    project(right + other)
    fwd_r.wait_recv()
    sib_far0 = send(9, far, 0, sib)
    fwd_l.wait_recv()
    sib_far1 = send(10, far, 1, sib)
    mg_copies = []
    for step in range(1, 8):
        to = lax.rem(me + step, 8)
        mg_copies.append(remote(
            mine_s.at[pl.ds(pl.multiple_of(to * 2 * DH, 2 * DH), 2 * DH)], mg_ref.at[:, mine],
            mg_send.at[step], mg_recv.at[step], to,
        ))
    attend(2)
    project(far)
    sib_far0.wait_recv()
    sib_far1.wait_recv()
    project(far + other)
    for src, dst in (
        (q_s, q_out), (kt_s, kt_out), (k_s, k_out), (v_s, v_out), (sg_s, sg_out), (gate_s, gate_out), (gsg_s, gsg_out)
    ):
        keep(src, dst)
    attend(3)
    for copy in mg_copies:
        copy.wait_recv()

    chunk = 512
    for ch in range(pos // chunk):
        at = slice(ch * chunk, (ch + 1) * chunk)
        row, lane = stat_place(pos, chunk, ch)
        for hd in range(2):
            h_ref[hd * DH : (hd + 1) * DH, at] = (acc_s[hd, :, at] * (1.0 / maxlen)).astype(BF)
        h = h_ref[:, at].astype(F32)
        mean = jnp.sum(h, axis=0, keepdims=True) * (1.0 / (2 * DH))
        cen = h - mean
        ng = mg_ref[:, at].astype(F32) * gate_s[:, at]
        st_s[row : row + 1, lane] = mean
        st_s[row + 1 : row + 2, lane] = jnp.sum(cen * cen, axis=0, keepdims=True)
        st_s[row + 2 : row + 3, lane] = jnp.sum(ng, axis=0, keepdims=True)
        st_s[row + 3 : row + 4, lane] = jnp.sum(ng * cen, axis=0, keepdims=True)
    st_copies = []
    for step in range(1, 8):
        st_copies.append(remote(st_s, sta_ref.at[me], st_send.at[step], st_recv.at[step], lax.rem(me + step, 8)))
    sta_ref[me] = st_s[...]
    for copy in st_copies + id_copies:
        copy.wait()

    for copy in mg_copies + to_right + to_left + [to_sib, fwd_r, fwd_l, sib_left, sib_right, sib_far0, sib_far1]:
        copy.wait_send()
    for copy in keeps:
        copy.wait()


def gather(lens, ids, x, og, w_attn, w_gate, w_out, tokens, seq_count, maxlen):
    pos = tokens * seq_count
    hbm = pl.BlockSpec(memory_space=pl.ANY)
    kept = [
        ((D, 8 * DH), BF),
        ((2, DH, pos), BF),
        ((2, DH, pos), BF),
        ((2, pos, DH), BF),
        ((2, pos, DH), BF),
        ((6 * DH, pos), F32),
        ((2 * DH, pos), F32),
        ((2 * DH, pos), F32),
    ]
    names = ("x", "w", "q", "kt", "k", "v", "sg", "gate", "gsg", "mg", "h", "stats", "ids")
    dma = lambda n: pltpu.SemaphoreType.DMA((n,))
    outs = pl.pallas_call(
        functools.partial(gather_kernel, tokens, maxlen),
        out_shape=tuple(
            [jax.ShapeDtypeStruct((seq_count, tokens, D), BF)]
            + [jax.ShapeDtypeStruct(shape, dtype) for shape, dtype in kept]
            + [
                jax.ShapeDtypeStruct((2 * DH, pos), BF),
                jax.ShapeDtypeStruct((2 * DH, pos), BF),
                jax.ShapeDtypeStruct((seq_count, 8, pos // 2), F32),
                jax.ShapeDtypeStruct((seq_count,) + ids.shape, jnp.int32),
            ]
        ),
        in_specs=[pl.BlockSpec(memory_space=pltpu.SMEM)] + vmem(1) + [hbm] + vmem(1) + [hbm] * 3,
        out_specs=tuple([hbm] * 9 + vmem(4)),
        scratch_shapes=[pltpu.VMEM(shape, dtype) for shape, dtype in kept]
        + [
            pltpu.VMEM((seq_count, tokens, D), BF),
            pltpu.VMEM((8 * DH, D), BF),
            pltpu.VMEM((D, D), BF),
            pltpu.VMEM((D, tokens), BF),
            pltpu.VMEM((2, DH, pos), BF),
            pltpu.VMEM((2, DH, pos), F32),
            pltpu.VMEM((8, pos // 2), F32),
            dma(4), dma(16), dma(11), dma(11), dma(8), dma(8), dma(8), dma(8), dma(8), dma(8),
        ],
        compiler_params=pltpu.CompilerParams(
            vmem_limit_bytes=VMEM_BYTES, collective_id=0, has_side_effects=True
        ),
        name="gather",
    )(lens, ids, x, og, w_attn, w_gate, w_out)
    return dict(zip(names, outs))


def grads_kernel(
    tokens, maxlen, dp_count,
    len_ref, sta_ref, h_ref, gate_ref, gsg_ref, mg_ref, q_ref, kt_ref, k_ref, v_ref, w_ref, sg_hbm, x_hbm,
    og_ref, id_ref,
    gattn_ref, ggate_ref, gosum_ref, tot_ref, idall_ref,
    sg_s, x_s, mix_s, ot_s, dv_s, dk_s, dq_s, g_s, gacc_s,
    out_s, pair_s, sum_s, far_s, ring_s,
    mixr_s, gop_s, gopair_s, gosum_s, gor_s, goout_s, gocol_s, gsrc_s, gw_s, gtsrc_s, gt_s,
    load_sem, mix_send, mix_recv, pair_send, pair_recv, ring_send, ring_recv,
    gp_send, gp_recv, go_send, go_recv, gc_send, gc_recv, gw_send, gw_recv, id_send, id_recv, gt_send, gt_recv,
):
    me, sib, right, left, _, c = seq_peers()
    z = me // 2
    dp = lax.axis_index("dp")
    seq_count = 8
    pos = seq_count * tokens
    span = 2 * tokens
    half = D // 2
    block = D // dp_count
    hb = block // 2

    sg_load = pltpu.make_async_copy(sg_hbm, sg_s, load_sem.at[0])
    x_load = pltpu.make_async_copy(x_hbm, x_s, load_sem.at[1])
    sg_load.start()
    x_load.start()
    barrier = pltpu.get_barrier_semaphore()
    for step in range(1, seq_count):
        pl.semaphore_signal(barrier, inc=1, device_id={"seq": lax.rem(me + step, seq_count)}, device_id_type=MESH)
    for step in range(1, dp_count):
        pl.semaphore_signal(barrier, inc=1, device_id={"dp": lax.rem(dp + step, dp_count)}, device_id_type=MESH)

    def describe(src, dst, send_sem, recv_sem, to):
        return pltpu.make_async_remote_copy(
            src_ref=src, dst_ref=dst, send_sem=send_sem, recv_sem=recv_sem, device_id=to, device_id_type=MESH
        )

    def remote(*args):
        copy = describe(*args)
        copy.start()
        return copy

    for ch in range(pos // span):
        at = slice(ch * span, (ch + 1) * span)
        row, lane = stat_place(pos, span, ch)
        means = [sta_ref[d, row : row + 1, lane] for d in range(seq_count)]
        mean = functools.reduce(jnp.add, means) * (1.0 / seq_count)
        var = jnp.zeros_like(mean)
        ng_mean = jnp.zeros_like(mean)
        ng_cov = jnp.zeros_like(mean)
        for d in range(seq_count):
            off = means[d] - mean
            ng_sum = sta_ref[d, row + 2 : row + 3, lane]
            var = var + sta_ref[d, row + 1 : row + 2, lane] + (2 * DH) * off * off
            ng_mean = ng_mean + ng_sum
            ng_cov = ng_cov + sta_ref[d, row + 3 : row + 4, lane] + off * ng_sum
        inv = lax.rsqrt(var * (1.0 / D) + NORM_EPS)
        ng_mean = ng_mean * (1.0 / D)
        proj = inv * ng_cov * (1.0 / D)
        gate = gate_ref[:, at]
        normed = (h_ref[:, at].astype(F32) - mean) * inv
        mix_s[:, at] = (normed * gate).astype(BF)
        mg = mg_ref[:, at].astype(F32)
        g_s[6 * DH :, at] = (mg * normed * gsg_ref[:, at]).astype(BF)
        hg = (inv * (mg * gate - ng_mean - normed * proj)).astype(BF)
        for hd in range(2):
            ot_s[hd, :, at] = hg[hd * DH : (hd + 1) * DH]
    dv_s[...] = jnp.zeros_like(dv_s)
    dk_s[...] = jnp.zeros_like(dk_s)
    dq_s[...] = jnp.zeros_like(dq_s)
    fac = 0.0625 / maxlen

    pl.semaphore_wait(barrier, seq_count - 1 + dp_count - 1)
    feats = pl.ds(pl.multiple_of(me * 2 * DH, 2 * DH), 2 * DH)
    mixes = []
    for step in range(1, seq_count):
        to = lax.rem(me + step, seq_count)
        mixes.append(remote(
            mix_s.at[:, pl.ds(pl.multiple_of(to * tokens, tokens), tokens)], mixr_s.at[feats],
            mix_send.at[step], mix_recv.at[step], {"seq": to},
        ))
    id_copies = []
    for step in range(1, dp_count):
        to = lax.rem(dp + step, dp_count)
        id_copies.append(remote(id_ref, idall_ref.at[dp], id_send.at[step], id_recv.at[step], {"dp": to}))
    idall_ref[dp] = id_ref[...]
    mixr_s[feats, :] = mix_s[:, pl.ds(pl.multiple_of(me * tokens, tokens), tokens)]
    x_load.wait()
    gtsrc_s[...] = mm(g_s[6 * DH :, :], x_s[...]).astype(BF).T
    gates = []
    for step in range(1, dp_count):
        to = lax.rem(dp + step, dp_count)
        gates.append(remote(
            gtsrc_s.at[pl.ds(pl.multiple_of(to * block, block), block)], gt_s.at[dp],
            gt_send.at[step], gt_recv.at[step], {"dp": to},
        ))
    gt_s[dp] = gtsrc_s[pl.ds(pl.multiple_of(dp * block, block), block), :]

    def chip_block(k):
        return lax.rem(z + k, 4)

    def lanes_of(b):
        return pl.ds(pl.multiple_of(b * span, span), span)

    def attend(n):
        new = chip_block(block_step(3 - n))

        def tile(m, carry):
            old = chip_block(block_step(3 - m))
            later = (new - old + 4) // 4
            i = later * new + (1 - later) * old
            j = new + old - i
            at, kat = lanes_of(i), lanes_of(j)
            allowed = tile_allowed(len_ref, j, i)
            for hd in range(2):
                t = mm(k_ref[hd, kat, :], q_ref[hd, :, at])
                dw = mm(v_ref[hd, kat, :], ot_s[hd, :, at])
                a = 1.0 + jnp.tanh(t)
                w = t * a
                ds = jnp.where(allowed, dw * (a + w * (2.0 - a)), 0.0).astype(BF)
                w = jnp.where(allowed, w, 0.0).astype(BF)
                dv_s[hd, :, kat] += mm(ot_s[hd, :, at], w, NT)
                dk_s[hd, :, kat] += mm(q_ref[hd, :, at], ds, NT)
                dq_s[hd, :, at] += mm(kt_ref[hd, :, kat], ds)
            return carry

        lax.fori_loop(n, 4, tile, 0)
        at = lanes_of(new)
        for hd in range(2):
            base = hd * 3 * DH
            dv = (dv_s[hd, :, at] * (1.0 / maxlen)).astype(BF)
            dk = (dk_s[hd, :, at] * (16.0 * fac)).astype(BF)
            dq = (dq_s[hd, :, at] * fac).astype(BF)
            for part, grad in enumerate((dv, dq, dk)):
                rows = slice(base + part * DH, base + (part + 1) * DH)
                g_s[rows, at] = (grad.astype(F32) * sg_s[rows, at]).astype(BF)

    def partial_grad(k, core):
        first = chip_block(k) * span + core * tokens
        return mm(w_ref[...], g_s[:, pl.ds(pl.multiple_of(first, tokens), tokens)])

    pairs = {}

    def share(k):
        out_s[k] = partial_grad(k, 1 - c).astype(BF)
        pairs[k] = remote(out_s.at[k], pair_s.at[k], pair_send.at[k], pair_recv.at[k], {"seq": sib})
        at = lanes_of(chip_block(k))
        part = mm(g_s[: 6 * DH, at], x_s[at, :])
        gacc_s[...] = part if k == 2 else gacc_s[...] + part

    low, high = pl.ds(0, half), pl.ds(half, half)
    hops = [
        describe(sum_s.at[2, low], far_s.at[0], ring_send.at[0], ring_recv.at[0], {"seq": right}),
        describe(sum_s.at[2, high], far_s.at[1], ring_send.at[1], ring_recv.at[1], {"seq": left}),
        describe(sum_s.at[1, high], ring_s.at[0, high], ring_send.at[2], ring_recv.at[2], {"seq": right}),
        describe(sum_s.at[3, low], ring_s.at[1, low], ring_send.at[3], ring_recv.at[3], {"seq": left}),
        describe(sum_s.at[1, low], ring_s.at[0, low], ring_send.at[4], ring_recv.at[4], {"seq": right}),
        describe(sum_s.at[3, high], ring_s.at[1, high], ring_send.at[5], ring_recv.at[5], {"seq": left}),
    ]

    def settle(k):
        own = partial_grad(k, c)
        pairs[k].wait_recv()
        sum_s[k] = (own + pair_s[k].astype(F32)).astype(BF)

    sg_load.wait()
    attend(0)
    for copy in mixes:
        copy.wait_recv()
    gop_s[...] = mm(mixr_s[...], og_ref[...]).astype(BF).reshape(dp_count, block, D)
    mine = pl.ds(pl.multiple_of(c * hb, hb), hb)
    theirs = pl.ds(pl.multiple_of((1 - c) * hb, hb), hb)
    go_pair = remote(gop_s.at[:, theirs], gopair_s, gp_send.at[0], gp_recv.at[0], {"seq": sib})
    share(2)
    settle(2)
    hops[0].start()
    hops[1].start()
    go_pair.wait_recv()
    gosum_s[...] = (gop_s[:, mine, :].astype(F32) + gopair_s[...].astype(F32)).astype(BF)
    gos = []
    for step in range(1, dp_count):
        to = lax.rem(dp + step, dp_count)
        gos.append(remote(gosum_s.at[to], gor_s.at[dp], go_send.at[step], go_recv.at[step], {"dp": to}))
    gor_s[dp] = gosum_s[dp]

    attend(1)
    share(1)
    settle(1)
    hops[2].start()
    hops[0].wait_recv()
    sum_s[1, low] = (sum_s[1, low].astype(F32) + far_s[0].astype(F32)).astype(BF)
    hops[4].start()

    attend(2)
    share(3)
    settle(3)
    hops[3].start()
    hops[1].wait_recv()
    sum_s[3, high] = (sum_s[3, high].astype(F32) + far_s[1].astype(F32)).astype(BF)
    hops[5].start()

    attend(3)
    share(0)
    gsrc_s[...] = gacc_s[...].astype(BF).T
    blocks = []
    for step in range(1, dp_count):
        to = lax.rem(dp + step, dp_count)
        blocks.append(remote(
            gsrc_s.at[pl.ds(pl.multiple_of(to * block, block), block)], gw_s.at[dp],
            gw_send.at[step], gw_recv.at[step], {"dp": to},
        ))
    gw_s[dp] = gsrc_s[pl.ds(pl.multiple_of(dp * block, block), block), :]
    settle(0)

    for copy in gos:
        copy.wait_recv()
    acc = gor_s[0].astype(F32)
    for d in range(1, dp_count):
        acc = acc + gor_s[d].astype(F32)
    goout_s[...] = acc.astype(BF)
    cols = []
    for step in range(1, seq_count):
        to = lax.rem(me + step, seq_count)
        cols.append(remote(
            goout_s.at[:, pl.ds(pl.multiple_of(to * 2 * DH, 2 * DH), 2 * DH)], gocol_s.at[me],
            gc_send.at[step], gc_recv.at[step], {"seq": to},
        ))
    gocol_s[me] = goout_s[:, pl.ds(pl.multiple_of(me * 2 * DH, 2 * DH), 2 * DH)]

    for hop in hops[2:]:
        hop.wait_recv()
    tot_ref[...] = (sum_s[0].astype(F32) + ring_s[0].astype(F32) + ring_s[1].astype(F32)).astype(BF)

    for copy in cols:
        copy.wait_recv()
    for core in range(2):
        acc = gocol_s[core].astype(F32)
        for chip in range(1, 4):
            acc = acc + gocol_s[2 * chip + core].astype(F32)
        gosum_ref[core * hb : (core + 1) * hb, :] = acc
    for copy in blocks:
        copy.wait_recv()
    acc = gw_s[0].astype(F32)
    for d in range(1, dp_count):
        acc = acc + gw_s[d].astype(F32)
    gattn_ref[...] = acc
    for copy in gates:
        copy.wait_recv()
    acc = gt_s[0].astype(F32)
    for d in range(1, dp_count):
        acc = acc + gt_s[d].astype(F32)
    ggate_ref[...] = acc

    for copy in id_copies:
        copy.wait_recv()
    for copy in id_copies + gates + mixes + list(pairs.values()) + hops + [go_pair] + gos + cols + blocks:
        copy.wait_send()


def grads(lens, acts, og, seq_count, dp_count, maxlen):
    tokens = og.shape[0]
    pos = tokens * seq_count
    hbm = pl.BlockSpec(memory_space=pl.ANY)
    block = D // dp_count
    bf = lambda *shape: pltpu.VMEM(shape, BF)
    f32 = lambda *shape: pltpu.VMEM(shape, F32)
    dma = lambda n: pltpu.SemaphoreType.DMA((n,))
    return pl.pallas_call(
        functools.partial(grads_kernel, tokens, maxlen, dp_count),
        out_shape=(
            jax.ShapeDtypeStruct((block, 6 * DH), F32),
            jax.ShapeDtypeStruct((block, 2 * DH), F32),
            jax.ShapeDtypeStruct((block, 2 * DH), F32),
            jax.ShapeDtypeStruct((D, tokens), BF),
            jax.ShapeDtypeStruct((dp_count,) + acts["ids"].shape, jnp.int32),
        ),
        in_specs=[pl.BlockSpec(memory_space=pltpu.SMEM)] + vmem(10) + [hbm] * 2 + vmem(2),
        out_specs=tuple(vmem(5)),
        scratch_shapes=[
            f32(6 * DH, pos), bf(pos, D), bf(2 * DH, pos), bf(2, DH, pos),
            f32(2, DH, pos), f32(2, DH, pos), f32(2, DH, pos), bf(8 * DH, pos), f32(6 * DH, D),
            bf(4, D, tokens), bf(4, D, tokens), bf(4, D, tokens), bf(2, D // 2, tokens), bf(2, D, tokens),
            bf(D, tokens), bf(dp_count, block, D), bf(dp_count, block // 2, D), bf(dp_count, block // 2, D),
            bf(dp_count, block // 2, D), bf(block // 2, D), bf(seq_count, block // 2, 2 * DH),
            bf(D, 6 * DH), bf(dp_count, block, 6 * DH), bf(D, 2 * DH), bf(dp_count, block, 2 * DH),
            dma(2), dma(seq_count), dma(seq_count), dma(4), dma(4), dma(6), dma(6),
            dma(1), dma(1), dma(dp_count), dma(dp_count), dma(seq_count), dma(seq_count), dma(dp_count), dma(dp_count), dma(dp_count), dma(dp_count), dma(dp_count), dma(dp_count),
        ],
        compiler_params=pltpu.CompilerParams(vmem_limit_bytes=VMEM_BYTES, collective_id=2, has_side_effects=True),
        name="grads",
    )(
        lens, acts["stats"], acts["h"], acts["gate"], acts["gsg"], acts["mg"], acts["q"], acts["kt"], acts["k"],
        acts["v"], acts["w"], acts["sg"], acts["x"].reshape(pos, D),
        og, acts["ids"],
    )


def route_kernel(
    dp_count, devices, capacity,
    tot_ref, og_ref, owner_col_ref, owner_row_ref,
    got_ref,
    wide_s, msg_s, send_sem, recv_sem,
):
    tokens = og_ref.shape[0]
    me = lax.axis_index("seq") * dp_count + lax.axis_index("dp")
    lines = D // 128
    barrier = pltpu.get_barrier_semaphore()

    def place_of(step):
        to = lax.rem(me + step, devices)
        return to, {"seq": to // dp_count, "dp": lax.rem(to, dp_count)}

    def greet(step, carry):
        pl.semaphore_signal(barrier, inc=1, device_id=place_of(step)[1], device_id_type=MESH)
        return carry

    lax.fori_loop(1, devices, greet, 0)
    earlier = (lax.broadcasted_iota(jnp.int32, (tokens, tokens), 0) < lax.broadcasted_iota(jnp.int32, (tokens, tokens), 1))
    same = owner_col_ref[...] == owner_row_ref[...]
    rank = jnp.sum(jnp.where(earlier & same, 1.0, 0.0), axis=0, keepdims=True).astype(jnp.int32)
    named = lax.broadcasted_iota(jnp.int32, (devices, tokens), 0) == owner_row_ref[...]
    for slot in range(capacity):
        place = jnp.where(named & (rank == slot), 1.0, 0.0).astype(BF)
        rows = mm(place, tot_ref[...], NT) + mm(place, og_ref[...])
        for line in range(lines):
            wide_s[pl.ds(slot * lines + line, devices, stride=capacity * lines), :] = rows[:, line * 128 : (line + 1) * 128]
    msg_s[...] = wide_s[...].astype(BF).reshape(msg_s.shape)
    mine = lax.axis_index("dp") * (devices // dp_count) + lax.axis_index("seq")
    got_ref[mine] = msg_s[me]
    pl.semaphore_wait(barrier, devices - 1)

    def push(step, carry):
        to, where = place_of(step)
        pltpu.make_async_remote_copy(
            src_ref=msg_s.at[to], dst_ref=got_ref.at[mine], send_sem=send_sem, recv_sem=recv_sem,
            device_id=where, device_id_type=MESH,
        ).start()
        return carry

    lax.fori_loop(1, devices, push, 0)
    others = pl.ds(0, devices - 1)
    pltpu.make_async_copy(msg_s.at[others], got_ref.at[others], recv_sem).wait()
    pltpu.make_async_copy(msg_s.at[others], got_ref.at[others], send_sem).wait()


def route(tot, og, item_owner, dp_count, devices, capacity):
    tokens = og.shape[0]
    lines = capacity * D // 128
    return pl.pallas_call(
        functools.partial(route_kernel, dp_count, devices, capacity),
        out_shape=jax.ShapeDtypeStruct((devices, lines, 128), BF),
        in_specs=vmem(4),
        out_specs=vmem(1)[0],
        scratch_shapes=[
            pltpu.VMEM((devices * lines, 128), F32),
            pltpu.VMEM((devices, lines, 128), BF),
            pltpu.SemaphoreType.DMA,
            pltpu.SemaphoreType.DMA,
        ],
        compiler_params=pltpu.CompilerParams(
            vmem_limit_bytes=VMEM_BYTES, collective_id=3, has_side_effects=True
        ),
        name="route",
    )(tot, og, item_owner, item_owner.reshape(1, tokens))


def update_kernel(
    capacity, devices,
    got_ref, ids_ref, me_ref, accum_ref, gattn_ref, ggate_ref, go_ref, tab_hbm,
    gattn_out, ggate_out, go_out, tab_out, accum_out,
    wide_s, rows_s, tab_ref, load_sem, keep_sem,
):
    lines = D // 128
    load = pltpu.make_async_copy(tab_hbm, tab_ref, load_sem)
    load.start()
    gattn_out[...] = gattn_ref[...]
    ggate_out[...] = ggate_ref[...]
    go_out[...] = go_ref[...]
    tokens = ids_ref.shape[1] // 2
    rows_own = tab_ref.shape[0]
    wide_s[...] = got_ref[...].astype(F32).reshape(wide_s.shape)
    hit = ids_ref[:, :tokens] == me_ref[0]
    hit_f = jnp.where(hit, 1.0, 0.0)
    before = lax.broadcasted_iota(jnp.int32, (tokens, tokens), 0) < lax.broadcasted_iota(jnp.int32, (tokens, tokens), 1)
    rank = mm(hit_f.astype(BF), jnp.where(before, 1.0, 0.0).astype(BF))
    row = (ids_ref[:, tokens:] + 1).astype(F32)
    eye = lax.broadcasted_iota(jnp.int32, (128, 128), 0) == lax.broadcasted_iota(jnp.int32, (128, 128), 1)
    grad = jnp.zeros((rows_own, D), F32)
    for slot in range(capacity):
        name = jnp.sum(jnp.where(hit & (rank == float(slot)), row, 0.0), axis=1, keepdims=True)
        name = jnp.sum(jnp.where(eye, name, 0.0), axis=0, keepdims=True) - 1.0
        pick = jnp.where(lax.broadcasted_iota(jnp.int32, (rows_own, devices), 0).astype(F32) == name, 1.0, 0.0).astype(BF)
        for line in range(lines):
            rows_s[:, line * 128 : (line + 1) * 128] = wide_s[
                pl.ds(slot * lines + line, devices, stride=capacity * lines), :
            ].astype(BF)
        grad = grad + mm(pick, rows_s[...])
    load.wait()
    keeps = []
    square = jnp.sum(grad * grad, axis=1, keepdims=True) * (1.0 / D)
    for part in range(rows_own // 128):
        at = slice(part * 128, (part + 1) * 128)
        old = jnp.sum(jnp.where(eye, accum_ref[part : part + 1, :], 0.0), axis=1, keepdims=True)
        new = old + square[at]
        tab_ref[at, :] = tab_ref[at, :] - LEARN_RATE * grad[at] * lax.rsqrt(new)
        keep = pltpu.make_async_copy(tab_ref.at[at], tab_out.at[at], keep_sem.at[part])
        keep.start()
        keeps.append(keep)
        accum_out[part : part + 1, :] = jnp.sum(jnp.where(eye, new, 0.0), axis=0, keepdims=True)
    for keep in keeps:
        keep.wait()


def update(got, ids, me, table, accum, gattn, ggate, go, capacity, devices):
    rows_own = table.shape[0]
    lines = capacity * D // 128
    like = lambda a: jax.ShapeDtypeStruct(a.shape, a.dtype)
    hbm = pl.BlockSpec(memory_space=pl.ANY)
    accum = accum.reshape(rows_own // 128, 128)
    gattn, ggate, go, table, accum = pl.pallas_call(
        functools.partial(update_kernel, capacity, devices),
        out_shape=(like(gattn), like(ggate), like(go), like(table), like(accum)),
        in_specs=vmem(2) + [pl.BlockSpec(memory_space=pltpu.SMEM)] + vmem(4) + [hbm],
        out_specs=tuple(vmem(3) + [hbm] + vmem(1)),
        scratch_shapes=[
            pltpu.VMEM((devices * lines, 128), F32),
            pltpu.VMEM((devices, D), BF),
            pltpu.VMEM((rows_own, D), F32),
            pltpu.SemaphoreType.DMA,
            pltpu.SemaphoreType.DMA((rows_own // 128,)),
        ],
        compiler_params=pltpu.CompilerParams(vmem_limit_bytes=VMEM_BYTES),
        name="update",
    )(got, ids, me.reshape(1), accum, gattn, ggate, go, table)
    return gattn, ggate, go, table, accum.reshape(rows_own)


def body(
    layer_input,
    out_grad,
    lengths,
    item_owner,
    item_row,
    w_attn,
    w_gate,
    w_out,
    emb_table,
    row_accum,
):
    seq_count = lax.axis_size("seq")
    dp_count = lax.axis_size("dp")
    devices = seq_count * dp_count
    tokens_dev = layer_input.shape[0]
    pos = tokens_dev * seq_count
    maxlen = 2 * pos // 3
    capacity = max(2, 2 * tokens_dev // devices)
    lens = lengths[0]
    ids = jnp.concatenate([item_owner.reshape(1, tokens_dev), item_row.reshape(1, tokens_dev)], axis=1)
    acts = gather(lens, ids, layer_input, out_grad, w_attn, w_gate, w_out, tokens_dev, seq_count, maxlen)
    gattn, ggate, go, tot, ids = grads(lens, acts, out_grad, seq_count, dp_count, maxlen)
    got = route(tot, out_grad, item_owner, dp_count, devices, capacity)
    me = lax.axis_index("seq") * dp_count + lax.axis_index("dp")
    ids = ids.reshape(devices, 2 * tokens_dev)
    return update(got, ids, me, emb_table, row_accum, gattn, ggate, go, capacity, devices)


def solution(mesh):
    placed = (
        P(("dp", "seq"), None),
        P(("dp", "seq"), None),
        P("dp", None),
        P(("dp", "seq"), None),
        P(("dp", "seq")),
        P(),
        P(),
        P(),
        P(("seq", "dp"), None),
        P(("seq", "dp")),
    )
    return jax.shard_map(
        body,
        mesh=mesh,
        in_specs=placed,
        out_specs=(
            P("dp", "seq"),
            P("dp", "seq"),
            P("dp", "seq"),
            P(("seq", "dp"), None),
            P(("seq", "dp")),
        ),
        check_vma=False,
    )
```

```python
import functools

import jax
import jax.numpy as jnp
from jax import lax
from jax.experimental import pallas as pl
from jax.experimental.pallas import tpu as pltpu
from jax.sharding import PartitionSpec as P

D = 1024
H = 16
DH = 64
NORM_EPS = 1e-05
LEARN_RATE = 0.1
TQ = 512
TK = 512
VMEM_BYTES = 56 * 1024 * 1024

BF = jnp.bfloat16
F32 = jnp.float32
NN = (((1,), (0,)), ((), ()))
NT = (((1,), (1,)), ((), ()))
MESH = pl.DeviceIdType.MESH


def mm(a, b, dims=NN):
    return lax.dot_general(a, b, dims, preferred_element_type=F32)


def silu(z):
    t = 0.5 * z
    return t + t * jnp.tanh(t)


def silu_grad(z):
    t = 0.5 * z
    th = jnp.tanh(t)
    return 0.5 * ((1.0 + th) * (1.0 + t * (1.0 - th)))


def event_starts(len_ref, places):
    end0 = len_ref[0]
    end1 = end0 + len_ref[1]
    return jnp.where(places >= end1, end1, jnp.where(places >= end0, end0, 0))


def scalar_start(len_ref, place):
    end0 = len_ref[0]
    end1 = end0 + len_ref[1]
    return jnp.where(place >= end1, end1, jnp.where(place >= end0, end0, 0))


def tile_allowed(len_ref, j, i):
    keys = j * TK + lax.broadcasted_iota(jnp.int32, (TK, TQ), 0)
    places = i * TQ + lax.broadcasted_iota(jnp.int32, (1, TQ), 1)
    return (keys >= event_starts(len_ref, places)) & (keys <= places)


def stat_place(pos, chunk, c):
    first = c * chunk
    row = 4 * (first // (pos // 2))
    lane = first % (pos // 2)
    return row, slice(lane, lane + chunk)


def vmem(count):
    return [pl.BlockSpec(memory_space=pltpu.VMEM)] * count


def seq_peers():
    me = lax.axis_index("seq")
    z, c = me // 2, me % 2
    at = lambda step: lax.rem(z + step, 4) * 2
    return me, at(0) + 1 - c, at(1) + c, at(3) + c, at(2) + c, c


def block_step(m):
    return lax.rem(3 * m + 3 * (m // 2) + 2 * (m // 3), 4)


def gather_kernel(
    tokens, maxlen,
    len_ref, id_ref, x_ref, og_ref, wa_hbm, wg_hbm, wo_hbm,
    xg_ref, w_out, q_out, kt_out, k_out, v_out, sg_out, gate_out, gsg_out, mg_ref, h_ref, sta_ref, idg_ref,
    w_s, q_s, kt_s, k_s, v_s, sg_s, gate_s, gsg_s,
    x_s, wt_s, wo_s, mine_s, vt_s, acc_s, st_s,
    load_sem, keep_sem, send_sem, recv_sem, mg_send, mg_recv, st_send, st_recv, id_send, id_recv,
):
    me, sib, right, left, far, c = seq_peers()
    z = me // 2
    pos = 8 * tokens
    half = tokens // 2
    loads = [
        pltpu.make_async_copy(x_ref, x_s.at[me], load_sem.at[0]),
        pltpu.make_async_copy(wa_hbm.at[:, pl.ds(pl.multiple_of(me * 6 * DH, 128), 6 * DH)], w_s.at[:, : 6 * DH], load_sem.at[1]),
        pltpu.make_async_copy(wg_hbm.at[:, pl.ds(pl.multiple_of(me * 2 * DH, 128), 2 * DH)], w_s.at[:, 6 * DH :], load_sem.at[2]),
        pltpu.make_async_copy(wo_hbm, wo_s, load_sem.at[3]),
    ]
    for load in loads:
        load.start()

    barrier = pltpu.get_barrier_semaphore()
    for step in range(1, 8):
        pl.semaphore_signal(barrier, inc=1, device_id={"seq": lax.rem(me + step, 8)}, device_id_type=MESH)
    acc_s[...] = jnp.zeros_like(acc_s)
    loads[0].wait()
    pl.semaphore_wait(barrier, 7)

    def remote(src, dst, send_sem, recv_sem, to):
        copy = pltpu.make_async_remote_copy(
            src_ref=src, dst_ref=dst, send_sem=send_sem, recv_sem=recv_sem, device_id={"seq": to}, device_id_type=MESH
        )
        copy.start()
        return copy

    def send(index, shard, part, to):
        ref = x_s.at[shard] if part is None else x_s.at[shard, pl.ds(part * half, half)]
        return remote(ref, ref, send_sem.at[index], recv_sem.at[index], to)

    keeps = []

    def keep(src, dst):
        copy = pltpu.make_async_copy(src, dst, keep_sem.at[len(keeps)])
        copy.start()
        keeps.append(copy)

    def project(shard):
        at = pl.ds(pl.multiple_of(shard * tokens, tokens), tokens)
        keep(x_s.at[shard], xg_ref.at[shard])
        pre = mm(wt_s[...], x_s[shard], NT)
        attn = pre[: 6 * DH]
        act = silu(attn).astype(BF)
        sg_s[:, at] = silu_grad(attn)
        gate = pre[6 * DH :]
        gate_s[:, at] = silu(gate)
        gsg_s[:, at] = silu_grad(gate)
        act_n = silu(mm(x_s[shard], w_s[:, : 6 * DH]))
        for hd in range(2):
            base = hd * 3 * DH
            vt_s[hd, :, at] = act[base : base + DH]
            q_s[hd, :, at] = (act[base + DH : base + 2 * DH] * 0.0625).astype(BF)
            kt_s[hd, :, at] = act[base + 2 * DH : base + 3 * DH]
            v_s[hd, at, :] = act_n[:, base : base + DH].astype(BF)
            k_s[hd, at, :] = act_n[:, base + 2 * DH : base + 3 * DH].astype(BF)

    def attend(n):
        new = lax.rem(z + block_step(n), 4)

        def tile(m, carry):
            old = lax.rem(z + block_step(m), 4)
            later = (new - old + 4) // 4
            i = later * new + (1 - later) * old
            j = new + old - i
            at = pl.ds(pl.multiple_of(i * TQ, TQ), TQ)
            kat = pl.ds(pl.multiple_of(j * TK, TK), TK)
            allowed = tile_allowed(len_ref, j, i)
            for hd in range(2):
                t = mm(k_s[hd, kat, :], q_s[hd, :, at])
                w = jnp.where(allowed, t + t * jnp.tanh(t), 0.0).astype(BF)
                acc_s[hd, :, at] += mm(vt_s[hd, :, kat], w)
            return carry

        lax.fori_loop(0, n + 1, tile, 0)

    to_right = [send(0, me, 0, right), None]
    to_left = [None, send(1, me, 1, left)]
    to_right[1] = send(2, me, 1, right)
    to_left[0] = send(3, me, 0, left)
    to_sib = send(4, me, None, sib)
    id_copies = []
    for step in range(1, 8):
        id_copies.append(remote(id_ref, idg_ref.at[me], id_send.at[step], id_recv.at[step], lax.rem(me + step, 8)))
    idg_ref[me] = id_ref[...]

    loads[1].wait()
    loads[2].wait()
    wt_s[...] = w_s[...].T
    keep(w_s, w_out)
    project(me)
    loads[3].wait()
    mine_s[...] = mm(wo_s[...], og_ref[...], NT).astype(BF)
    mine = pl.ds(pl.multiple_of(me * tokens, tokens), tokens)
    mg_ref[:, mine] = mine_s[pl.ds(pl.multiple_of(me * 2 * DH, 2 * DH), 2 * DH), :]
    to_sib.wait_recv()
    project(sib)

    to_right[0].wait_recv()
    fwd_r = send(5, left, 0, right)
    to_left[1].wait_recv()
    fwd_l = send(6, right, 1, left)
    attend(0)
    to_right[1].wait_recv()
    sib_left = send(7, left, None, sib)
    to_left[0].wait_recv()
    sib_right = send(8, right, None, sib)
    other = 1 - 2 * c
    project(left)
    sib_left.wait_recv()
    project(left + other)
    attend(1)
    project(right)
    sib_right.wait_recv()
    project(right + other)
    fwd_r.wait_recv()
    sib_far0 = send(9, far, 0, sib)
    fwd_l.wait_recv()
    sib_far1 = send(10, far, 1, sib)
    mg_copies = []
    for step in range(1, 8):
        to = lax.rem(me + step, 8)
        mg_copies.append(remote(
            mine_s.at[pl.ds(pl.multiple_of(to * 2 * DH, 2 * DH), 2 * DH)], mg_ref.at[:, mine],
            mg_send.at[step], mg_recv.at[step], to,
        ))
    attend(2)
    project(far)
    sib_far0.wait_recv()
    sib_far1.wait_recv()
    project(far + other)
    for src, dst in (
        (q_s, q_out), (kt_s, kt_out), (k_s, k_out), (v_s, v_out), (sg_s, sg_out), (gate_s, gate_out), (gsg_s, gsg_out)
    ):
        keep(src, dst)
    attend(3)
    for copy in mg_copies:
        copy.wait_recv()

    chunk = 512
    for ch in range(pos // chunk):
        at = slice(ch * chunk, (ch + 1) * chunk)
        row, lane = stat_place(pos, chunk, ch)
        for hd in range(2):
            h_ref[hd * DH : (hd + 1) * DH, at] = (acc_s[hd, :, at] * (1.0 / maxlen)).astype(BF)
        h = h_ref[:, at].astype(F32)
        mean = jnp.sum(h, axis=0, keepdims=True) * (1.0 / (2 * DH))
        cen = h - mean
        ng = mg_ref[:, at].astype(F32) * gate_s[:, at]
        st_s[row : row + 1, lane] = mean
        st_s[row + 1 : row + 2, lane] = jnp.sum(cen * cen, axis=0, keepdims=True)
        st_s[row + 2 : row + 3, lane] = jnp.sum(ng, axis=0, keepdims=True)
        st_s[row + 3 : row + 4, lane] = jnp.sum(ng * cen, axis=0, keepdims=True)
    st_copies = []
    for step in range(1, 8):
        st_copies.append(remote(st_s, sta_ref.at[me], st_send.at[step], st_recv.at[step], lax.rem(me + step, 8)))
    sta_ref[me] = st_s[...]
    for copy in st_copies + id_copies:
        copy.wait()

    for copy in mg_copies + to_right + to_left + [to_sib, fwd_r, fwd_l, sib_left, sib_right, sib_far0, sib_far1]:
        copy.wait_send()
    for copy in keeps:
        copy.wait()


def gather(lens, ids, x, og, w_attn, w_gate, w_out, tokens, seq_count, maxlen):
    pos = tokens * seq_count
    hbm = pl.BlockSpec(memory_space=pl.ANY)
    kept = [
        ((D, 8 * DH), BF),
        ((2, DH, pos), BF),
        ((2, DH, pos), BF),
        ((2, pos, DH), BF),
        ((2, pos, DH), BF),
        ((6 * DH, pos), F32),
        ((2 * DH, pos), F32),
        ((2 * DH, pos), F32),
    ]
    names = ("x", "w", "q", "kt", "k", "v", "sg", "gate", "gsg", "mg", "h", "stats", "ids")
    dma = lambda n: pltpu.SemaphoreType.DMA((n,))
    outs = pl.pallas_call(
        functools.partial(gather_kernel, tokens, maxlen),
        out_shape=tuple(
            [jax.ShapeDtypeStruct((seq_count, tokens, D), BF)]
            + [jax.ShapeDtypeStruct(shape, dtype) for shape, dtype in kept]
            + [
                jax.ShapeDtypeStruct((2 * DH, pos), BF),
                jax.ShapeDtypeStruct((2 * DH, pos), BF),
                jax.ShapeDtypeStruct((seq_count, 8, pos // 2), F32),
                jax.ShapeDtypeStruct((seq_count,) + ids.shape, jnp.int32),
            ]
        ),
        in_specs=[pl.BlockSpec(memory_space=pltpu.SMEM)] + vmem(1) + [hbm] + vmem(1) + [hbm] * 3,
        out_specs=tuple([hbm] * 9 + vmem(4)),
        scratch_shapes=[pltpu.VMEM(shape, dtype) for shape, dtype in kept]
        + [
            pltpu.VMEM((seq_count, tokens, D), BF),
            pltpu.VMEM((8 * DH, D), BF),
            pltpu.VMEM((D, D), BF),
            pltpu.VMEM((D, tokens), BF),
            pltpu.VMEM((2, DH, pos), BF),
            pltpu.VMEM((2, DH, pos), F32),
            pltpu.VMEM((8, pos // 2), F32),
            dma(4), dma(16), dma(11), dma(11), dma(8), dma(8), dma(8), dma(8), dma(8), dma(8),
        ],
        compiler_params=pltpu.CompilerParams(
            vmem_limit_bytes=VMEM_BYTES, collective_id=0, has_side_effects=True
        ),
        name="gather",
    )(lens, ids, x, og, w_attn, w_gate, w_out)
    return dict(zip(names, outs))


def grads_kernel(
    tokens, maxlen, dp_count, capacity,
    len_ref, sta_ref, h_ref, gate_ref, gsg_ref, mg_ref, q_ref, kt_ref, k_ref, v_ref, w_ref, sg_hbm, x_hbm,
    og_ref, id_ref, owner_col_ref, owner_row_ref,
    gattn_ref, ggate_ref, gosum_ref, got_ref, idall_ref,
    sg_s, x_s, mix_s, ot_s, dv_s, dk_s, dq_s, g_s, gacc_s,
    out_s, pair_s, sum_s, far_s, ring_s,
    mixr_s, gop_s, gopair_s, gosum_s, gor_s, goout_s, gocol_s, gsrc_s, gw_s, gtsrc_s, gt_s, place_s, wide_s, msg_s,
    load_sem, mix_send, mix_recv, pair_send, pair_recv, ring_send, ring_recv,
    gp_send, gp_recv, go_send, go_recv, gc_send, gc_recv, gw_send, gw_recv, id_send, id_recv, gt_send, gt_recv, row_send, row_recv,
):
    me, sib, right, left, _, c = seq_peers()
    z = me // 2
    dp = lax.axis_index("dp")
    seq_count = 8
    pos = seq_count * tokens
    span = 2 * tokens
    half = D // 2
    block = D // dp_count
    hb = block // 2

    sg_load = pltpu.make_async_copy(sg_hbm, sg_s, load_sem.at[0])
    x_load = pltpu.make_async_copy(x_hbm, x_s, load_sem.at[1])
    sg_load.start()
    x_load.start()
    barrier = pltpu.get_barrier_semaphore()
    devices = seq_count * dp_count
    here = me * dp_count + dp

    def place_of(step):
        to = lax.rem(here + step, devices)
        return to, {"seq": to // dp_count, "dp": lax.rem(to, dp_count)}

    def greet(step, carry):
        pl.semaphore_signal(barrier, inc=1, device_id=place_of(step)[1], device_id_type=MESH)
        return carry

    lax.fori_loop(1, devices, greet, 0)

    def describe(src, dst, send_sem, recv_sem, to):
        return pltpu.make_async_remote_copy(
            src_ref=src, dst_ref=dst, send_sem=send_sem, recv_sem=recv_sem, device_id=to, device_id_type=MESH
        )

    def remote(*args):
        copy = describe(*args)
        copy.start()
        return copy

    for ch in range(pos // span):
        at = slice(ch * span, (ch + 1) * span)
        row, lane = stat_place(pos, span, ch)
        means = [sta_ref[d, row : row + 1, lane] for d in range(seq_count)]
        mean = functools.reduce(jnp.add, means) * (1.0 / seq_count)
        var = jnp.zeros_like(mean)
        ng_mean = jnp.zeros_like(mean)
        ng_cov = jnp.zeros_like(mean)
        for d in range(seq_count):
            off = means[d] - mean
            ng_sum = sta_ref[d, row + 2 : row + 3, lane]
            var = var + sta_ref[d, row + 1 : row + 2, lane] + (2 * DH) * off * off
            ng_mean = ng_mean + ng_sum
            ng_cov = ng_cov + sta_ref[d, row + 3 : row + 4, lane] + off * ng_sum
        inv = lax.rsqrt(var * (1.0 / D) + NORM_EPS)
        ng_mean = ng_mean * (1.0 / D)
        proj = inv * ng_cov * (1.0 / D)
        gate = gate_ref[:, at]
        normed = (h_ref[:, at].astype(F32) - mean) * inv
        mix_s[:, at] = (normed * gate).astype(BF)
        mg = mg_ref[:, at].astype(F32)
        g_s[6 * DH :, at] = (mg * normed * gsg_ref[:, at]).astype(BF)
        hg = (inv * (mg * gate - ng_mean - normed * proj)).astype(BF)
        for hd in range(2):
            ot_s[hd, :, at] = hg[hd * DH : (hd + 1) * DH]
    dv_s[...] = jnp.zeros_like(dv_s)
    dk_s[...] = jnp.zeros_like(dk_s)
    dq_s[...] = jnp.zeros_like(dq_s)
    fac = 0.0625 / maxlen

    pl.semaphore_wait(barrier, devices - 1)
    feats = pl.ds(pl.multiple_of(me * 2 * DH, 2 * DH), 2 * DH)
    mixes = []
    for step in range(1, seq_count):
        to = lax.rem(me + step, seq_count)
        mixes.append(remote(
            mix_s.at[:, pl.ds(pl.multiple_of(to * tokens, tokens), tokens)], mixr_s.at[feats],
            mix_send.at[step], mix_recv.at[step], {"seq": to},
        ))
    id_copies = []
    for step in range(1, dp_count):
        to = lax.rem(dp + step, dp_count)
        id_copies.append(remote(id_ref, idall_ref.at[dp], id_send.at[step], id_recv.at[step], {"dp": to}))
    idall_ref[dp] = id_ref[...]
    mixr_s[feats, :] = mix_s[:, pl.ds(pl.multiple_of(me * tokens, tokens), tokens)]
    x_load.wait()
    gtsrc_s[...] = mm(g_s[6 * DH :, :], x_s[...]).astype(BF).T
    gates = []
    for step in range(1, dp_count):
        to = lax.rem(dp + step, dp_count)
        gates.append(remote(
            gtsrc_s.at[pl.ds(pl.multiple_of(to * block, block), block)], gt_s.at[dp],
            gt_send.at[step], gt_recv.at[step], {"dp": to},
        ))
    gt_s[dp] = gtsrc_s[pl.ds(pl.multiple_of(dp * block, block), block), :]

    def chip_block(k):
        return lax.rem(z + k, 4)

    def lanes_of(b):
        return pl.ds(pl.multiple_of(b * span, span), span)

    def attend(n):
        new = chip_block(block_step(3 - n))

        def tile(m, carry):
            old = chip_block(block_step(3 - m))
            later = (new - old + 4) // 4
            i = later * new + (1 - later) * old
            j = new + old - i
            at, kat = lanes_of(i), lanes_of(j)
            allowed = tile_allowed(len_ref, j, i)
            for hd in range(2):
                t = mm(k_ref[hd, kat, :], q_ref[hd, :, at])
                dw = mm(v_ref[hd, kat, :], ot_s[hd, :, at])
                a = 1.0 + jnp.tanh(t)
                w = t * a
                ds = jnp.where(allowed, dw * (a + w * (2.0 - a)), 0.0).astype(BF)
                w = jnp.where(allowed, w, 0.0).astype(BF)
                dv_s[hd, :, kat] += mm(ot_s[hd, :, at], w, NT)
                dk_s[hd, :, kat] += mm(q_ref[hd, :, at], ds, NT)
                dq_s[hd, :, at] += mm(kt_ref[hd, :, kat], ds)
            return carry

        lax.fori_loop(n, 4, tile, 0)
        at = lanes_of(new)
        for hd in range(2):
            base = hd * 3 * DH
            dv = (dv_s[hd, :, at] * (1.0 / maxlen)).astype(BF)
            dk = (dk_s[hd, :, at] * (16.0 * fac)).astype(BF)
            dq = (dq_s[hd, :, at] * fac).astype(BF)
            for part, grad in enumerate((dv, dq, dk)):
                rows = slice(base + part * DH, base + (part + 1) * DH)
                g_s[rows, at] = (grad.astype(F32) * sg_s[rows, at]).astype(BF)

    def partial_grad(k, core):
        first = chip_block(k) * span + core * tokens
        return mm(w_ref[...], g_s[:, pl.ds(pl.multiple_of(first, tokens), tokens)])

    pairs = {}

    def share(k):
        out_s[k] = partial_grad(k, 1 - c).astype(BF)
        pairs[k] = remote(out_s.at[k], pair_s.at[k], pair_send.at[k], pair_recv.at[k], {"seq": sib})
        at = lanes_of(chip_block(k))
        part = mm(g_s[: 6 * DH, at], x_s[at, :])
        gacc_s[...] = part if k == 2 else gacc_s[...] + part

    low, high = pl.ds(0, half), pl.ds(half, half)
    hops = [
        describe(sum_s.at[2, low], far_s.at[0], ring_send.at[0], ring_recv.at[0], {"seq": right}),
        describe(sum_s.at[2, high], far_s.at[1], ring_send.at[1], ring_recv.at[1], {"seq": left}),
        describe(sum_s.at[1, high], ring_s.at[0, high], ring_send.at[2], ring_recv.at[2], {"seq": right}),
        describe(sum_s.at[3, low], ring_s.at[1, low], ring_send.at[3], ring_recv.at[3], {"seq": left}),
        describe(sum_s.at[1, low], ring_s.at[0, low], ring_send.at[4], ring_recv.at[4], {"seq": right}),
        describe(sum_s.at[3, high], ring_s.at[1, high], ring_send.at[5], ring_recv.at[5], {"seq": left}),
    ]

    def settle(k):
        own = partial_grad(k, c)
        pairs[k].wait_recv()
        sum_s[k] = (own + pair_s[k].astype(F32)).astype(BF)

    sg_load.wait()
    attend(0)
    for copy in mixes:
        copy.wait_recv()
    gop_s[...] = mm(mixr_s[...], og_ref[...]).astype(BF).reshape(dp_count, block, D)
    mine = pl.ds(pl.multiple_of(c * hb, hb), hb)
    theirs = pl.ds(pl.multiple_of((1 - c) * hb, hb), hb)
    go_pair = remote(gop_s.at[:, theirs], gopair_s, gp_send.at[0], gp_recv.at[0], {"seq": sib})
    share(2)
    settle(2)
    hops[0].start()
    hops[1].start()
    go_pair.wait_recv()
    gosum_s[...] = (gop_s[:, mine, :].astype(F32) + gopair_s[...].astype(F32)).astype(BF)
    gos = []
    for step in range(1, dp_count):
        to = lax.rem(dp + step, dp_count)
        gos.append(remote(gosum_s.at[to], gor_s.at[dp], go_send.at[step], go_recv.at[step], {"dp": to}))
    gor_s[dp] = gosum_s[dp]

    attend(1)
    share(1)
    settle(1)
    hops[2].start()
    hops[0].wait_recv()
    sum_s[1, low] = (sum_s[1, low].astype(F32) + far_s[0].astype(F32)).astype(BF)
    hops[4].start()

    attend(2)
    share(3)
    settle(3)
    hops[3].start()
    hops[1].wait_recv()
    sum_s[3, high] = (sum_s[3, high].astype(F32) + far_s[1].astype(F32)).astype(BF)
    hops[5].start()

    attend(3)
    share(0)
    gsrc_s[...] = gacc_s[...].astype(BF).T
    blocks = []
    for step in range(1, dp_count):
        to = lax.rem(dp + step, dp_count)
        blocks.append(remote(
            gsrc_s.at[pl.ds(pl.multiple_of(to * block, block), block)], gw_s.at[dp],
            gw_send.at[step], gw_recv.at[step], {"dp": to},
        ))
    gw_s[dp] = gsrc_s[pl.ds(pl.multiple_of(dp * block, block), block), :]
    settle(0)

    earlier = (lax.broadcasted_iota(jnp.int32, (tokens, tokens), 0) < lax.broadcasted_iota(jnp.int32, (tokens, tokens), 1))
    same = owner_col_ref[...] == owner_row_ref[...]
    rank = jnp.sum(jnp.where(earlier & same, 1.0, 0.0), axis=0, keepdims=True).astype(jnp.int32)
    named = lax.broadcasted_iota(jnp.int32, (devices, tokens), 0) == owner_row_ref[...]
    for slot in range(capacity):
        place_s[slot] = jnp.where(named & (rank == slot), 1.0, 0.0).astype(BF)

    for copy in gos:
        copy.wait_recv()
    acc = gor_s[0].astype(F32)
    for d in range(1, dp_count):
        acc = acc + gor_s[d].astype(F32)
    goout_s[...] = acc.astype(BF)
    cols = []
    for step in range(1, seq_count):
        to = lax.rem(me + step, seq_count)
        cols.append(remote(
            goout_s.at[:, pl.ds(pl.multiple_of(to * 2 * DH, 2 * DH), 2 * DH)], gocol_s.at[me],
            gc_send.at[step], gc_recv.at[step], {"seq": to},
        ))
    gocol_s[me] = goout_s[:, pl.ds(pl.multiple_of(me * 2 * DH, 2 * DH), 2 * DH)]

    for hop in hops[2:]:
        hop.wait_recv()
    total = (sum_s[0].astype(F32) + ring_s[0].astype(F32) + ring_s[1].astype(F32)).astype(BF)
    lines = D // 128
    for slot in range(capacity):
        rows = mm(place_s[slot], total, NT) + mm(place_s[slot], og_ref[...])
        for line in range(lines):
            wide_s[pl.ds(slot * lines + line, devices, stride=capacity * lines), :] = rows[:, line * 128 : (line + 1) * 128]
    msg_s[...] = wide_s[...].astype(BF).reshape(msg_s.shape)
    source = dp * seq_count + me

    def push(step, carry):
        to, where = place_of(step)
        pltpu.make_async_remote_copy(
            src_ref=msg_s.at[to], dst_ref=got_ref.at[source], send_sem=row_send, recv_sem=row_recv,
            device_id=where, device_id_type=MESH,
        ).start()
        return carry

    lax.fori_loop(1, devices, push, 0)
    got_ref[source] = msg_s[here]

    for copy in cols:
        copy.wait_recv()
    for core in range(2):
        acc = gocol_s[core].astype(F32)
        for chip in range(1, 4):
            acc = acc + gocol_s[2 * chip + core].astype(F32)
        gosum_ref[core * hb : (core + 1) * hb, :] = acc
    for copy in blocks:
        copy.wait_recv()
    acc = gw_s[0].astype(F32)
    for d in range(1, dp_count):
        acc = acc + gw_s[d].astype(F32)
    gattn_ref[...] = acc
    for copy in gates:
        copy.wait_recv()
    acc = gt_s[0].astype(F32)
    for d in range(1, dp_count):
        acc = acc + gt_s[d].astype(F32)
    ggate_ref[...] = acc

    for copy in id_copies:
        copy.wait_recv()
    others = pl.ds(0, devices - 1)
    pltpu.make_async_copy(msg_s.at[others], got_ref.at[others], row_recv).wait()
    pltpu.make_async_copy(msg_s.at[others], got_ref.at[others], row_send).wait()
    for copy in id_copies + gates + mixes + list(pairs.values()) + hops + [go_pair] + gos + cols + blocks:
        copy.wait_send()


def grads(lens, acts, og, item_owner, seq_count, dp_count, capacity, maxlen):
    tokens = og.shape[0]
    devices = seq_count * dp_count
    lines = capacity * D // 128
    pos = tokens * seq_count
    hbm = pl.BlockSpec(memory_space=pl.ANY)
    block = D // dp_count
    bf = lambda *shape: pltpu.VMEM(shape, BF)
    f32 = lambda *shape: pltpu.VMEM(shape, F32)
    dma = lambda n: pltpu.SemaphoreType.DMA((n,))
    return pl.pallas_call(
        functools.partial(grads_kernel, tokens, maxlen, dp_count, capacity),
        out_shape=(
            jax.ShapeDtypeStruct((block, 6 * DH), F32),
            jax.ShapeDtypeStruct((block, 2 * DH), F32),
            jax.ShapeDtypeStruct((block, 2 * DH), F32),
            jax.ShapeDtypeStruct((devices, lines, 128), BF),
            jax.ShapeDtypeStruct((dp_count,) + acts["ids"].shape, jnp.int32),
        ),
        in_specs=[pl.BlockSpec(memory_space=pltpu.SMEM)] + vmem(10) + [hbm] * 2 + vmem(4),
        out_specs=tuple(vmem(5)),
        scratch_shapes=[
            f32(6 * DH, pos), bf(pos, D), bf(2 * DH, pos), bf(2, DH, pos),
            f32(2, DH, pos), f32(2, DH, pos), f32(2, DH, pos), bf(8 * DH, pos), f32(6 * DH, D),
            bf(4, D, tokens), bf(4, D, tokens), bf(4, D, tokens), bf(2, D // 2, tokens), bf(2, D, tokens),
            bf(D, tokens), bf(dp_count, block, D), bf(dp_count, block // 2, D), bf(dp_count, block // 2, D),
            bf(dp_count, block // 2, D), bf(block // 2, D), bf(seq_count, block // 2, 2 * DH),
            bf(D, 6 * DH), bf(dp_count, block, 6 * DH), bf(D, 2 * DH), bf(dp_count, block, 2 * DH),
            bf(capacity, devices, tokens), f32(devices * lines, 128), bf(devices, lines, 128),
            dma(2), dma(seq_count), dma(seq_count), dma(4), dma(4), dma(6), dma(6),
            dma(1), dma(1), dma(dp_count), dma(dp_count), dma(seq_count), dma(seq_count), dma(dp_count), dma(dp_count), dma(dp_count), dma(dp_count), dma(dp_count), dma(dp_count),
            pltpu.SemaphoreType.DMA, pltpu.SemaphoreType.DMA,
        ],
        compiler_params=pltpu.CompilerParams(vmem_limit_bytes=VMEM_BYTES, collective_id=2, has_side_effects=True),
        name="grads",
    )(
        lens, acts["stats"], acts["h"], acts["gate"], acts["gsg"], acts["mg"], acts["q"], acts["kt"], acts["k"],
        acts["v"], acts["w"], acts["sg"], acts["x"].reshape(pos, D),
        og, acts["ids"], item_owner, item_owner.reshape(1, tokens),
    )


def update_kernel(
    capacity, devices,
    got_ref, ids_ref, me_ref, accum_ref, gattn_ref, ggate_ref, go_ref, tab_hbm,
    gattn_out, ggate_out, go_out, tab_out, accum_out,
    wide_s, rows_s, tab_ref, load_sem, keep_sem,
):
    lines = D // 128
    load = pltpu.make_async_copy(tab_hbm, tab_ref, load_sem)
    load.start()
    gattn_out[...] = gattn_ref[...]
    ggate_out[...] = ggate_ref[...]
    go_out[...] = go_ref[...]
    tokens = ids_ref.shape[1] // 2
    rows_own = tab_ref.shape[0]
    wide_s[...] = got_ref[...].astype(F32).reshape(wide_s.shape)
    hit = ids_ref[:, :tokens] == me_ref[0]
    hit_f = jnp.where(hit, 1.0, 0.0)
    before = lax.broadcasted_iota(jnp.int32, (tokens, tokens), 0) < lax.broadcasted_iota(jnp.int32, (tokens, tokens), 1)
    rank = mm(hit_f.astype(BF), jnp.where(before, 1.0, 0.0).astype(BF))
    row = (ids_ref[:, tokens:] + 1).astype(F32)
    eye = lax.broadcasted_iota(jnp.int32, (128, 128), 0) == lax.broadcasted_iota(jnp.int32, (128, 128), 1)
    grad = jnp.zeros((rows_own, D), F32)
    for slot in range(capacity):
        name = jnp.sum(jnp.where(hit & (rank == float(slot)), row, 0.0), axis=1, keepdims=True)
        name = jnp.sum(jnp.where(eye, name, 0.0), axis=0, keepdims=True) - 1.0
        pick = jnp.where(lax.broadcasted_iota(jnp.int32, (rows_own, devices), 0).astype(F32) == name, 1.0, 0.0).astype(BF)
        for line in range(lines):
            rows_s[:, line * 128 : (line + 1) * 128] = wide_s[
                pl.ds(slot * lines + line, devices, stride=capacity * lines), :
            ].astype(BF)
        grad = grad + mm(pick, rows_s[...])
    load.wait()
    keeps = []
    square = jnp.sum(grad * grad, axis=1, keepdims=True) * (1.0 / D)
    for part in range(rows_own // 128):
        at = slice(part * 128, (part + 1) * 128)
        old = jnp.sum(jnp.where(eye, accum_ref[part : part + 1, :], 0.0), axis=1, keepdims=True)
        new = old + square[at]
        tab_ref[at, :] = tab_ref[at, :] - LEARN_RATE * grad[at] * lax.rsqrt(new)
        keep = pltpu.make_async_copy(tab_ref.at[at], tab_out.at[at], keep_sem.at[part])
        keep.start()
        keeps.append(keep)
        accum_out[part : part + 1, :] = jnp.sum(jnp.where(eye, new, 0.0), axis=0, keepdims=True)
    for keep in keeps:
        keep.wait()


def update(got, ids, me, table, accum, gattn, ggate, go, capacity, devices):
    rows_own = table.shape[0]
    lines = capacity * D // 128
    like = lambda a: jax.ShapeDtypeStruct(a.shape, a.dtype)
    hbm = pl.BlockSpec(memory_space=pl.ANY)
    accum = accum.reshape(rows_own // 128, 128)
    gattn, ggate, go, table, accum = pl.pallas_call(
        functools.partial(update_kernel, capacity, devices),
        out_shape=(like(gattn), like(ggate), like(go), like(table), like(accum)),
        in_specs=vmem(2) + [pl.BlockSpec(memory_space=pltpu.SMEM)] + vmem(4) + [hbm],
        out_specs=tuple(vmem(3) + [hbm] + vmem(1)),
        scratch_shapes=[
            pltpu.VMEM((devices * lines, 128), F32),
            pltpu.VMEM((devices, D), BF),
            pltpu.VMEM((rows_own, D), F32),
            pltpu.SemaphoreType.DMA,
            pltpu.SemaphoreType.DMA((rows_own // 128,)),
        ],
        compiler_params=pltpu.CompilerParams(vmem_limit_bytes=VMEM_BYTES),
        name="update",
    )(got, ids, me.reshape(1), accum, gattn, ggate, go, table)
    return gattn, ggate, go, table, accum.reshape(rows_own)


def body(
    layer_input,
    out_grad,
    lengths,
    item_owner,
    item_row,
    w_attn,
    w_gate,
    w_out,
    emb_table,
    row_accum,
):
    seq_count = lax.axis_size("seq")
    dp_count = lax.axis_size("dp")
    devices = seq_count * dp_count
    tokens_dev = layer_input.shape[0]
    pos = tokens_dev * seq_count
    maxlen = 2 * pos // 3
    capacity = max(2, 2 * tokens_dev // devices)
    lens = lengths[0]
    ids = jnp.concatenate([item_owner.reshape(1, tokens_dev), item_row.reshape(1, tokens_dev)], axis=1)
    acts = gather(lens, ids, layer_input, out_grad, w_attn, w_gate, w_out, tokens_dev, seq_count, maxlen)
    gattn, ggate, go, got, ids = grads(lens, acts, out_grad, item_owner, seq_count, dp_count, capacity, maxlen)
    me = lax.axis_index("seq") * dp_count + lax.axis_index("dp")
    ids = ids.reshape(devices, 2 * tokens_dev)
    return update(got, ids, me, emb_table, row_accum, gattn, ggate, go, capacity, devices)


def solution(mesh):
    placed = (
        P(("dp", "seq"), None),
        P(("dp", "seq"), None),
        P("dp", None),
        P(("dp", "seq"), None),
        P(("dp", "seq")),
        P(),
        P(),
        P(),
        P(("seq", "dp"), None),
        P(("seq", "dp")),
    )
    return jax.shard_map(
        body,
        mesh=mesh,
        in_specs=placed,
        out_specs=(
            P("dp", "seq"),
            P("dp", "seq"),
            P("dp", "seq"),
            P(("seq", "dp"), None),
            P(("seq", "dp")),
        ),
        check_vma=False,
    )
```

```python
import functools

import jax
import jax.numpy as jnp
from jax import lax
from jax.experimental import pallas as pl
from jax.experimental.pallas import tpu as pltpu
from jax.sharding import PartitionSpec as P

D = 1024
H = 16
DH = 64
NORM_EPS = 1e-05
LEARN_RATE = 0.1
TQ = 512
TK = 512
VMEM_BYTES = 56 * 1024 * 1024

BF = jnp.bfloat16
F32 = jnp.float32
NN = (((1,), (0,)), ((), ()))
NT = (((1,), (1,)), ((), ()))
MESH = pl.DeviceIdType.MESH


def mm(a, b, dims=NN):
    return lax.dot_general(a, b, dims, preferred_element_type=F32)


def silu(z):
    t = 0.5 * z
    return t + t * jnp.tanh(t)


def silu_grad(z):
    t = 0.5 * z
    th = jnp.tanh(t)
    return 0.5 * ((1.0 + th) * (1.0 + t * (1.0 - th)))


def event_starts(len_ref, places):
    end0 = len_ref[0]
    end1 = end0 + len_ref[1]
    return jnp.where(places >= end1, end1, jnp.where(places >= end0, end0, 0))


def scalar_start(len_ref, place):
    end0 = len_ref[0]
    end1 = end0 + len_ref[1]
    return jnp.where(place >= end1, end1, jnp.where(place >= end0, end0, 0))


def tile_allowed(len_ref, j, i):
    keys = j * TK + lax.broadcasted_iota(jnp.int32, (TK, TQ), 0)
    places = i * TQ + lax.broadcasted_iota(jnp.int32, (1, TQ), 1)
    return (keys >= event_starts(len_ref, places)) & (keys <= places)


def stat_place(pos, chunk, c):
    first = c * chunk
    row = 4 * (first // (pos // 2))
    lane = first % (pos // 2)
    return row, slice(lane, lane + chunk)


def vmem(count):
    return [pl.BlockSpec(memory_space=pltpu.VMEM)] * count


def seq_peers():
    me = lax.axis_index("seq")
    z, c = me // 2, me % 2
    at = lambda step: lax.rem(z + step, 4) * 2
    return me, at(0) + 1 - c, at(1) + c, at(3) + c, at(2) + c, c


def block_step(m):
    return lax.rem(3 * m + 3 * (m // 2) + 2 * (m // 3), 4)


def gather_kernel(
    tokens, maxlen,
    len_ref, owner_ref, item_ref, x_ref, og_ref, wa_hbm, wg_hbm, wo_hbm,
    xg_ref, w_out, q_out, kt_out, k_out, v_out, sg_out, gate_out, gsg_out, mg_ref, h_ref, sta_ref, idg_ref,
    w_s, q_s, kt_s, k_s, v_s, sg_s, gate_s, gsg_s,
    x_s, wt_s, wo_s, mine_s, vt_s, acc_s, st_s, id_s,
    load_sem, keep_sem, send_sem, recv_sem, mg_send, mg_recv, st_send, st_recv, id_send, id_recv,
):
    me, sib, right, left, far, c = seq_peers()
    z = me // 2
    pos = 8 * tokens
    half = tokens // 2
    loads = [
        pltpu.make_async_copy(x_ref, x_s.at[me], load_sem.at[0]),
        pltpu.make_async_copy(wa_hbm.at[:, pl.ds(pl.multiple_of(me * 6 * DH, 128), 6 * DH)], w_s.at[:, : 6 * DH], load_sem.at[1]),
        pltpu.make_async_copy(wg_hbm.at[:, pl.ds(pl.multiple_of(me * 2 * DH, 128), 2 * DH)], w_s.at[:, 6 * DH :], load_sem.at[2]),
        pltpu.make_async_copy(wo_hbm, wo_s, load_sem.at[3]),
    ]
    for load in loads:
        load.start()

    barrier = pltpu.get_barrier_semaphore()
    for step in range(1, 8):
        pl.semaphore_signal(barrier, inc=1, device_id={"seq": lax.rem(me + step, 8)}, device_id_type=MESH)
    acc_s[...] = jnp.zeros_like(acc_s)
    loads[0].wait()
    pl.semaphore_wait(barrier, 7)

    def remote(src, dst, send_sem, recv_sem, to):
        copy = pltpu.make_async_remote_copy(
            src_ref=src, dst_ref=dst, send_sem=send_sem, recv_sem=recv_sem, device_id={"seq": to}, device_id_type=MESH
        )
        copy.start()
        return copy

    def send(index, shard, part, to):
        ref = x_s.at[shard] if part is None else x_s.at[shard, pl.ds(part * half, half)]
        return remote(ref, ref, send_sem.at[index], recv_sem.at[index], to)

    keeps = []

    def keep(src, dst):
        copy = pltpu.make_async_copy(src, dst, keep_sem.at[len(keeps)])
        copy.start()
        keeps.append(copy)

    def project(shard):
        at = pl.ds(pl.multiple_of(shard * tokens, tokens), tokens)
        keep(x_s.at[shard], xg_ref.at[shard])
        pre = mm(wt_s[...], x_s[shard], NT)
        attn = pre[: 6 * DH]
        act = silu(attn).astype(BF)
        sg_s[:, at] = silu_grad(attn)
        gate = pre[6 * DH :]
        gate_s[:, at] = silu(gate)
        gsg_s[:, at] = silu_grad(gate)
        act_n = silu(mm(x_s[shard], w_s[:, : 6 * DH]))
        for hd in range(2):
            base = hd * 3 * DH
            vt_s[hd, :, at] = act[base : base + DH]
            q_s[hd, :, at] = (act[base + DH : base + 2 * DH] * 0.0625).astype(BF)
            kt_s[hd, :, at] = act[base + 2 * DH : base + 3 * DH]
            v_s[hd, at, :] = act_n[:, base : base + DH].astype(BF)
            k_s[hd, at, :] = act_n[:, base + 2 * DH : base + 3 * DH].astype(BF)

    def attend(n):
        new = lax.rem(z + block_step(n), 4)

        def tile(m, carry):
            old = lax.rem(z + block_step(m), 4)
            later = (new - old + 4) // 4
            i = later * new + (1 - later) * old
            j = new + old - i
            at = pl.ds(pl.multiple_of(i * TQ, TQ), TQ)
            kat = pl.ds(pl.multiple_of(j * TK, TK), TK)
            allowed = tile_allowed(len_ref, j, i)
            for hd in range(2):
                t = mm(k_s[hd, kat, :], q_s[hd, :, at])
                w = jnp.where(allowed, t + t * jnp.tanh(t), 0.0).astype(BF)
                acc_s[hd, :, at] += mm(vt_s[hd, :, kat], w)
            return carry

        lax.fori_loop(0, n + 1, tile, 0)

    to_right = [send(0, me, 0, right), None]
    to_left = [None, send(1, me, 1, left)]
    to_right[1] = send(2, me, 1, right)
    to_left[0] = send(3, me, 0, left)
    to_sib = send(4, me, None, sib)
    eye = lax.broadcasted_iota(jnp.int32, (tokens, tokens), 0) == lax.broadcasted_iota(jnp.int32, (tokens, tokens), 1)
    owners = jnp.sum(jnp.where(eye, owner_ref[...].astype(F32), 0.0), axis=0, keepdims=True)
    id_s[:, :tokens] = owners.astype(jnp.int32)
    id_s[:, tokens:] = item_ref[...]
    id_copies = []
    for step in range(1, 8):
        id_copies.append(remote(id_s, idg_ref.at[me], id_send.at[step], id_recv.at[step], lax.rem(me + step, 8)))
    idg_ref[me] = id_s[...]

    loads[1].wait()
    loads[2].wait()
    wt_s[...] = w_s[...].T
    keep(w_s, w_out)
    project(me)
    loads[3].wait()
    mine_s[...] = mm(wo_s[...], og_ref[...], NT).astype(BF)
    mine = pl.ds(pl.multiple_of(me * tokens, tokens), tokens)
    mg_ref[:, mine] = mine_s[pl.ds(pl.multiple_of(me * 2 * DH, 2 * DH), 2 * DH), :]
    to_sib.wait_recv()
    project(sib)

    to_right[0].wait_recv()
    fwd_r = send(5, left, 0, right)
    to_left[1].wait_recv()
    fwd_l = send(6, right, 1, left)
    attend(0)
    to_right[1].wait_recv()
    sib_left = send(7, left, None, sib)
    to_left[0].wait_recv()
    sib_right = send(8, right, None, sib)
    other = 1 - 2 * c
    project(left)
    sib_left.wait_recv()
    project(left + other)
    attend(1)
    project(right)
    sib_right.wait_recv()
    project(right + other)
    fwd_r.wait_recv()
    sib_far0 = send(9, far, 0, sib)
    fwd_l.wait_recv()
    sib_far1 = send(10, far, 1, sib)
    mg_copies = []
    for step in range(1, 8):
        to = lax.rem(me + step, 8)
        mg_copies.append(remote(
            mine_s.at[pl.ds(pl.multiple_of(to * 2 * DH, 2 * DH), 2 * DH)], mg_ref.at[:, mine],
            mg_send.at[step], mg_recv.at[step], to,
        ))
    attend(2)
    project(far)
    sib_far0.wait_recv()
    sib_far1.wait_recv()
    project(far + other)
    for src, dst in (
        (q_s, q_out), (kt_s, kt_out), (k_s, k_out), (v_s, v_out), (sg_s, sg_out), (gate_s, gate_out), (gsg_s, gsg_out)
    ):
        keep(src, dst)
    attend(3)
    for copy in mg_copies:
        copy.wait_recv()

    chunk = 512
    for ch in range(pos // chunk):
        at = slice(ch * chunk, (ch + 1) * chunk)
        row, lane = stat_place(pos, chunk, ch)
        for hd in range(2):
            h_ref[hd * DH : (hd + 1) * DH, at] = (acc_s[hd, :, at] * (1.0 / maxlen)).astype(BF)
        h = h_ref[:, at].astype(F32)
        mean = jnp.sum(h, axis=0, keepdims=True) * (1.0 / (2 * DH))
        cen = h - mean
        ng = mg_ref[:, at].astype(F32) * gate_s[:, at]
        st_s[row : row + 1, lane] = mean
        st_s[row + 1 : row + 2, lane] = jnp.sum(cen * cen, axis=0, keepdims=True)
        st_s[row + 2 : row + 3, lane] = jnp.sum(ng, axis=0, keepdims=True)
        st_s[row + 3 : row + 4, lane] = jnp.sum(ng * cen, axis=0, keepdims=True)
    st_copies = []
    for step in range(1, 8):
        st_copies.append(remote(st_s, sta_ref.at[me], st_send.at[step], st_recv.at[step], lax.rem(me + step, 8)))
    sta_ref[me] = st_s[...]
    for copy in st_copies + id_copies:
        copy.wait()

    for copy in mg_copies + to_right + to_left + [to_sib, fwd_r, fwd_l, sib_left, sib_right, sib_far0, sib_far1]:
        copy.wait_send()
    for copy in keeps:
        copy.wait()


def gather(lens, item_owner, item_row, x, og, w_attn, w_gate, w_out, tokens, seq_count, maxlen):
    pos = tokens * seq_count
    hbm = pl.BlockSpec(memory_space=pl.ANY)
    kept = [
        ((D, 8 * DH), BF),
        ((2, DH, pos), BF),
        ((2, DH, pos), BF),
        ((2, pos, DH), BF),
        ((2, pos, DH), BF),
        ((6 * DH, pos), F32),
        ((2 * DH, pos), F32),
        ((2 * DH, pos), F32),
    ]
    names = ("x", "w", "q", "kt", "k", "v", "sg", "gate", "gsg", "mg", "h", "stats", "ids")
    dma = lambda n: pltpu.SemaphoreType.DMA((n,))
    outs = pl.pallas_call(
        functools.partial(gather_kernel, tokens, maxlen),
        out_shape=tuple(
            [jax.ShapeDtypeStruct((seq_count, tokens, D), BF)]
            + [jax.ShapeDtypeStruct(shape, dtype) for shape, dtype in kept]
            + [
                jax.ShapeDtypeStruct((2 * DH, pos), BF),
                jax.ShapeDtypeStruct((2 * DH, pos), BF),
                jax.ShapeDtypeStruct((seq_count, 8, pos // 2), F32),
                jax.ShapeDtypeStruct((seq_count, 1, 2 * tokens), jnp.int32),
            ]
        ),
        in_specs=[pl.BlockSpec(memory_space=pltpu.SMEM)] + vmem(2) + [hbm] + vmem(1) + [hbm] * 3,
        out_specs=tuple([hbm] * 9 + vmem(4)),
        scratch_shapes=[pltpu.VMEM(shape, dtype) for shape, dtype in kept]
        + [
            pltpu.VMEM((seq_count, tokens, D), BF),
            pltpu.VMEM((8 * DH, D), BF),
            pltpu.VMEM((D, D), BF),
            pltpu.VMEM((D, tokens), BF),
            pltpu.VMEM((2, DH, pos), BF),
            pltpu.VMEM((2, DH, pos), F32),
            pltpu.VMEM((8, pos // 2), F32),
            pltpu.VMEM((1, 2 * tokens), jnp.int32),
            dma(4), dma(16), dma(11), dma(11), dma(8), dma(8), dma(8), dma(8), dma(8), dma(8),
        ],
        compiler_params=pltpu.CompilerParams(
            vmem_limit_bytes=VMEM_BYTES, collective_id=0, has_side_effects=True
        ),
        name="gather",
    )(lens, item_owner, item_row.reshape(1, tokens), x, og, w_attn, w_gate, w_out)
    return dict(zip(names, outs))


def grads_kernel(
    tokens, maxlen, dp_count, capacity,
    len_ref, sta_ref, h_ref, gate_ref, gsg_ref, mg_ref, q_ref, kt_ref, k_ref, v_ref, w_ref, sg_hbm, x_hbm,
    og_ref, id_ref, owner_col_ref, owner_row_ref,
    gattn_ref, ggate_ref, gosum_ref, got_ref, idall_ref,
    sg_s, x_s, mix_s, ot_s, dv_s, dk_s, dq_s, g_s, gacc_s,
    out_s, pair_s, sum_s, far_s, ring_s,
    mixr_s, gop_s, gopair_s, gosum_s, gor_s, goout_s, gocol_s, gsrc_s, gw_s, gtsrc_s, gt_s, place_s, wide_s, msg_s, ids_s,
    load_sem, mix_send, mix_recv, pair_send, pair_recv, ring_send, ring_recv,
    gp_send, gp_recv, go_send, go_recv, gc_send, gc_recv, gw_send, gw_recv, id_send, id_recv, gt_send, gt_recv, row_send, row_recv,
):
    me, sib, right, left, _, c = seq_peers()
    z = me // 2
    dp = lax.axis_index("dp")
    seq_count = 8
    pos = seq_count * tokens
    span = 2 * tokens
    half = D // 2
    block = D // dp_count
    hb = block // 2

    sg_load = pltpu.make_async_copy(sg_hbm, sg_s, load_sem.at[0])
    x_load = pltpu.make_async_copy(x_hbm, x_s, load_sem.at[1])
    sg_load.start()
    x_load.start()
    barrier = pltpu.get_barrier_semaphore()
    devices = seq_count * dp_count
    here = me * dp_count + dp

    def place_of(step):
        to = lax.rem(here + step, devices)
        return to, {"seq": to // dp_count, "dp": lax.rem(to, dp_count)}

    def greet(step, carry):
        pl.semaphore_signal(barrier, inc=1, device_id=place_of(step)[1], device_id_type=MESH)
        return carry

    lax.fori_loop(1, devices, greet, 0)

    def describe(src, dst, send_sem, recv_sem, to):
        return pltpu.make_async_remote_copy(
            src_ref=src, dst_ref=dst, send_sem=send_sem, recv_sem=recv_sem, device_id=to, device_id_type=MESH
        )

    def remote(*args):
        copy = describe(*args)
        copy.start()
        return copy

    for ch in range(pos // span):
        at = slice(ch * span, (ch + 1) * span)
        row, lane = stat_place(pos, span, ch)
        means = [sta_ref[d, row : row + 1, lane] for d in range(seq_count)]
        mean = functools.reduce(jnp.add, means) * (1.0 / seq_count)
        var = jnp.zeros_like(mean)
        ng_mean = jnp.zeros_like(mean)
        ng_cov = jnp.zeros_like(mean)
        for d in range(seq_count):
            off = means[d] - mean
            ng_sum = sta_ref[d, row + 2 : row + 3, lane]
            var = var + sta_ref[d, row + 1 : row + 2, lane] + (2 * DH) * off * off
            ng_mean = ng_mean + ng_sum
            ng_cov = ng_cov + sta_ref[d, row + 3 : row + 4, lane] + off * ng_sum
        inv = lax.rsqrt(var * (1.0 / D) + NORM_EPS)
        ng_mean = ng_mean * (1.0 / D)
        proj = inv * ng_cov * (1.0 / D)
        gate = gate_ref[:, at]
        normed = (h_ref[:, at].astype(F32) - mean) * inv
        mix_s[:, at] = (normed * gate).astype(BF)
        mg = mg_ref[:, at].astype(F32)
        g_s[6 * DH :, at] = (mg * normed * gsg_ref[:, at]).astype(BF)
        hg = (inv * (mg * gate - ng_mean - normed * proj)).astype(BF)
        for hd in range(2):
            ot_s[hd, :, at] = hg[hd * DH : (hd + 1) * DH]
    for d in range(seq_count):
        ids_s[d : d + 1, :] = id_ref[d]
    dv_s[...] = jnp.zeros_like(dv_s)
    dk_s[...] = jnp.zeros_like(dk_s)
    dq_s[...] = jnp.zeros_like(dq_s)
    fac = 0.0625 / maxlen

    pl.semaphore_wait(barrier, devices - 1)
    feats = pl.ds(pl.multiple_of(me * 2 * DH, 2 * DH), 2 * DH)
    mixes = []
    for step in range(1, seq_count):
        to = lax.rem(me + step, seq_count)
        mixes.append(remote(
            mix_s.at[:, pl.ds(pl.multiple_of(to * tokens, tokens), tokens)], mixr_s.at[feats],
            mix_send.at[step], mix_recv.at[step], {"seq": to},
        ))
    id_copies = []
    for step in range(1, dp_count):
        to = lax.rem(dp + step, dp_count)
        id_copies.append(remote(ids_s, idall_ref.at[dp], id_send.at[step], id_recv.at[step], {"dp": to}))
    idall_ref[dp] = ids_s[...]
    mixr_s[feats, :] = mix_s[:, pl.ds(pl.multiple_of(me * tokens, tokens), tokens)]
    x_load.wait()
    gtsrc_s[...] = mm(g_s[6 * DH :, :], x_s[...]).astype(BF).T
    gates = []
    for step in range(1, dp_count):
        to = lax.rem(dp + step, dp_count)
        gates.append(remote(
            gtsrc_s.at[pl.ds(pl.multiple_of(to * block, block), block)], gt_s.at[dp],
            gt_send.at[step], gt_recv.at[step], {"dp": to},
        ))
    gt_s[dp] = gtsrc_s[pl.ds(pl.multiple_of(dp * block, block), block), :]

    def chip_block(k):
        return lax.rem(z + k, 4)

    def lanes_of(b):
        return pl.ds(pl.multiple_of(b * span, span), span)

    def attend(n):
        new = chip_block(block_step(3 - n))

        def tile(m, carry):
            old = chip_block(block_step(3 - m))
            later = (new - old + 4) // 4
            i = later * new + (1 - later) * old
            j = new + old - i
            at, kat = lanes_of(i), lanes_of(j)
            allowed = tile_allowed(len_ref, j, i)
            for hd in range(2):
                t = mm(k_ref[hd, kat, :], q_ref[hd, :, at])
                dw = mm(v_ref[hd, kat, :], ot_s[hd, :, at])
                a = 1.0 + jnp.tanh(t)
                w = t * a
                ds = jnp.where(allowed, dw * (a + w * (2.0 - a)), 0.0).astype(BF)
                w = jnp.where(allowed, w, 0.0).astype(BF)
                dv_s[hd, :, kat] += mm(ot_s[hd, :, at], w, NT)
                dk_s[hd, :, kat] += mm(q_ref[hd, :, at], ds, NT)
                dq_s[hd, :, at] += mm(kt_ref[hd, :, kat], ds)
            return carry

        lax.fori_loop(n, 4, tile, 0)
        at = lanes_of(new)
        for hd in range(2):
            base = hd * 3 * DH
            dv = (dv_s[hd, :, at] * (1.0 / maxlen)).astype(BF)
            dk = (dk_s[hd, :, at] * (16.0 * fac)).astype(BF)
            dq = (dq_s[hd, :, at] * fac).astype(BF)
            for part, grad in enumerate((dv, dq, dk)):
                rows = slice(base + part * DH, base + (part + 1) * DH)
                g_s[rows, at] = (grad.astype(F32) * sg_s[rows, at]).astype(BF)

    def partial_grad(k, core):
        first = chip_block(k) * span + core * tokens
        return mm(w_ref[...], g_s[:, pl.ds(pl.multiple_of(first, tokens), tokens)])

    pairs = {}

    def share(k):
        out_s[k] = partial_grad(k, 1 - c).astype(BF)
        pairs[k] = remote(out_s.at[k], pair_s.at[k], pair_send.at[k], pair_recv.at[k], {"seq": sib})
        at = lanes_of(chip_block(k))
        part = mm(g_s[: 6 * DH, at], x_s[at, :])
        gacc_s[...] = part if k == 2 else gacc_s[...] + part

    low, high = pl.ds(0, half), pl.ds(half, half)
    hops = [
        describe(sum_s.at[2, low], far_s.at[0], ring_send.at[0], ring_recv.at[0], {"seq": right}),
        describe(sum_s.at[2, high], far_s.at[1], ring_send.at[1], ring_recv.at[1], {"seq": left}),
        describe(sum_s.at[1, high], ring_s.at[0, high], ring_send.at[2], ring_recv.at[2], {"seq": right}),
        describe(sum_s.at[3, low], ring_s.at[1, low], ring_send.at[3], ring_recv.at[3], {"seq": left}),
        describe(sum_s.at[1, low], ring_s.at[0, low], ring_send.at[4], ring_recv.at[4], {"seq": right}),
        describe(sum_s.at[3, high], ring_s.at[1, high], ring_send.at[5], ring_recv.at[5], {"seq": left}),
    ]

    def settle(k):
        own = partial_grad(k, c)
        pairs[k].wait_recv()
        sum_s[k] = (own + pair_s[k].astype(F32)).astype(BF)

    sg_load.wait()
    attend(0)
    for copy in mixes:
        copy.wait_recv()
    gop_s[...] = mm(mixr_s[...], og_ref[...]).astype(BF).reshape(dp_count, block, D)
    mine = pl.ds(pl.multiple_of(c * hb, hb), hb)
    theirs = pl.ds(pl.multiple_of((1 - c) * hb, hb), hb)
    go_pair = remote(gop_s.at[:, theirs], gopair_s, gp_send.at[0], gp_recv.at[0], {"seq": sib})
    share(2)
    settle(2)
    hops[0].start()
    hops[1].start()
    go_pair.wait_recv()
    gosum_s[...] = (gop_s[:, mine, :].astype(F32) + gopair_s[...].astype(F32)).astype(BF)
    gos = []
    for step in range(1, dp_count):
        to = lax.rem(dp + step, dp_count)
        gos.append(remote(gosum_s.at[to], gor_s.at[dp], go_send.at[step], go_recv.at[step], {"dp": to}))
    gor_s[dp] = gosum_s[dp]

    attend(1)
    share(1)
    settle(1)
    hops[2].start()
    hops[0].wait_recv()
    sum_s[1, low] = (sum_s[1, low].astype(F32) + far_s[0].astype(F32)).astype(BF)
    hops[4].start()

    attend(2)
    share(3)
    settle(3)
    hops[3].start()
    hops[1].wait_recv()
    sum_s[3, high] = (sum_s[3, high].astype(F32) + far_s[1].astype(F32)).astype(BF)
    hops[5].start()

    attend(3)
    share(0)
    gsrc_s[...] = gacc_s[...].astype(BF).T
    blocks = []
    for step in range(1, dp_count):
        to = lax.rem(dp + step, dp_count)
        blocks.append(remote(
            gsrc_s.at[pl.ds(pl.multiple_of(to * block, block), block)], gw_s.at[dp],
            gw_send.at[step], gw_recv.at[step], {"dp": to},
        ))
    gw_s[dp] = gsrc_s[pl.ds(pl.multiple_of(dp * block, block), block), :]
    settle(0)

    earlier = (lax.broadcasted_iota(jnp.int32, (tokens, tokens), 0) < lax.broadcasted_iota(jnp.int32, (tokens, tokens), 1))
    same = owner_col_ref[...] == owner_row_ref[...]
    rank = jnp.sum(jnp.where(earlier & same, 1.0, 0.0), axis=0, keepdims=True).astype(jnp.int32)
    named = lax.broadcasted_iota(jnp.int32, (devices, tokens), 0) == owner_row_ref[...]
    for slot in range(capacity):
        place_s[slot] = jnp.where(named & (rank == slot), 1.0, 0.0).astype(BF)

    for copy in gos:
        copy.wait_recv()
    acc = gor_s[0].astype(F32)
    for d in range(1, dp_count):
        acc = acc + gor_s[d].astype(F32)
    goout_s[...] = acc.astype(BF)
    cols = []
    for step in range(1, seq_count):
        to = lax.rem(me + step, seq_count)
        cols.append(remote(
            goout_s.at[:, pl.ds(pl.multiple_of(to * 2 * DH, 2 * DH), 2 * DH)], gocol_s.at[me],
            gc_send.at[step], gc_recv.at[step], {"seq": to},
        ))
    gocol_s[me] = goout_s[:, pl.ds(pl.multiple_of(me * 2 * DH, 2 * DH), 2 * DH)]

    for hop in hops[2:]:
        hop.wait_recv()
    total = (sum_s[0].astype(F32) + ring_s[0].astype(F32) + ring_s[1].astype(F32)).astype(BF)
    lines = D // 128
    for slot in range(capacity):
        rows = mm(place_s[slot], total, NT) + mm(place_s[slot], og_ref[...])
        for line in range(lines):
            wide_s[pl.ds(slot * lines + line, devices, stride=capacity * lines), :] = rows[:, line * 128 : (line + 1) * 128]
    msg_s[...] = wide_s[...].astype(BF).reshape(msg_s.shape)
    source = dp * seq_count + me

    def push(step, carry):
        to, where = place_of(step)
        pltpu.make_async_remote_copy(
            src_ref=msg_s.at[to], dst_ref=got_ref.at[source], send_sem=row_send, recv_sem=row_recv,
            device_id=where, device_id_type=MESH,
        ).start()
        return carry

    lax.fori_loop(1, devices, push, 0)
    got_ref[source] = msg_s[here]

    for copy in cols:
        copy.wait_recv()
    for core in range(2):
        acc = gocol_s[core].astype(F32)
        for chip in range(1, 4):
            acc = acc + gocol_s[2 * chip + core].astype(F32)
        gosum_ref[core * hb : (core + 1) * hb, :] = acc
    for copy in blocks:
        copy.wait_recv()
    acc = gw_s[0].astype(F32)
    for d in range(1, dp_count):
        acc = acc + gw_s[d].astype(F32)
    gattn_ref[...] = acc
    for copy in gates:
        copy.wait_recv()
    acc = gt_s[0].astype(F32)
    for d in range(1, dp_count):
        acc = acc + gt_s[d].astype(F32)
    ggate_ref[...] = acc

    for copy in id_copies:
        copy.wait_recv()
    others = pl.ds(0, devices - 1)
    pltpu.make_async_copy(msg_s.at[others], got_ref.at[others], row_recv).wait()
    pltpu.make_async_copy(msg_s.at[others], got_ref.at[others], row_send).wait()
    for copy in id_copies + gates + mixes + list(pairs.values()) + hops + [go_pair] + gos + cols + blocks:
        copy.wait_send()


def grads(lens, acts, og, item_owner, seq_count, dp_count, capacity, maxlen):
    tokens = og.shape[0]
    devices = seq_count * dp_count
    lines = capacity * D // 128
    pos = tokens * seq_count
    hbm = pl.BlockSpec(memory_space=pl.ANY)
    block = D // dp_count
    bf = lambda *shape: pltpu.VMEM(shape, BF)
    f32 = lambda *shape: pltpu.VMEM(shape, F32)
    dma = lambda n: pltpu.SemaphoreType.DMA((n,))
    return pl.pallas_call(
        functools.partial(grads_kernel, tokens, maxlen, dp_count, capacity),
        out_shape=(
            jax.ShapeDtypeStruct((block, 6 * DH), F32),
            jax.ShapeDtypeStruct((block, 2 * DH), F32),
            jax.ShapeDtypeStruct((block, 2 * DH), F32),
            jax.ShapeDtypeStruct((devices, lines, 128), BF),
            jax.ShapeDtypeStruct((dp_count, seq_count, 2 * tokens), jnp.int32),
        ),
        in_specs=[pl.BlockSpec(memory_space=pltpu.SMEM)] + vmem(10) + [hbm] * 2 + vmem(4),
        out_specs=tuple(vmem(5)),
        scratch_shapes=[
            f32(6 * DH, pos), bf(pos, D), bf(2 * DH, pos), bf(2, DH, pos),
            f32(2, DH, pos), f32(2, DH, pos), f32(2, DH, pos), bf(8 * DH, pos), f32(6 * DH, D),
            bf(4, D, tokens), bf(4, D, tokens), bf(4, D, tokens), bf(2, D // 2, tokens), bf(2, D, tokens),
            bf(D, tokens), bf(dp_count, block, D), bf(dp_count, block // 2, D), bf(dp_count, block // 2, D),
            bf(dp_count, block // 2, D), bf(block // 2, D), bf(seq_count, block // 2, 2 * DH),
            bf(D, 6 * DH), bf(dp_count, block, 6 * DH), bf(D, 2 * DH), bf(dp_count, block, 2 * DH),
            bf(capacity, devices, tokens), f32(devices * lines, 128), bf(devices, lines, 128),
            pltpu.VMEM((seq_count, 2 * tokens), jnp.int32),
            dma(2), dma(seq_count), dma(seq_count), dma(4), dma(4), dma(6), dma(6),
            dma(1), dma(1), dma(dp_count), dma(dp_count), dma(seq_count), dma(seq_count), dma(dp_count), dma(dp_count), dma(dp_count), dma(dp_count), dma(dp_count), dma(dp_count),
            pltpu.SemaphoreType.DMA, pltpu.SemaphoreType.DMA,
        ],
        compiler_params=pltpu.CompilerParams(vmem_limit_bytes=VMEM_BYTES, collective_id=2, has_side_effects=True),
        name="grads",
    )(
        lens, acts["stats"], acts["h"], acts["gate"], acts["gsg"], acts["mg"], acts["q"], acts["kt"], acts["k"],
        acts["v"], acts["w"], acts["sg"], acts["x"].reshape(pos, D),
        og, acts["ids"], item_owner, item_owner.reshape(1, tokens),
    )


def update_kernel(
    capacity, devices,
    got_ref, ids_ref, me_ref, accum_ref, gattn_ref, ggate_ref, go_ref, tab_hbm,
    gattn_out, ggate_out, go_out, tab_out, accum_out,
    wide_s, rows_s, tab_ref, load_sem, keep_sem,
):
    lines = D // 128
    load = pltpu.make_async_copy(tab_hbm, tab_ref, load_sem)
    load.start()
    gattn_out[...] = gattn_ref[...]
    ggate_out[...] = ggate_ref[...]
    go_out[...] = go_ref[...]
    tokens = ids_ref.shape[1] // 2
    rows_own = tab_ref.shape[0]
    wide_s[...] = got_ref[...].astype(F32).reshape(wide_s.shape)
    hit = ids_ref[:, :tokens] == me_ref[0]
    hit_f = jnp.where(hit, 1.0, 0.0)
    before = lax.broadcasted_iota(jnp.int32, (tokens, tokens), 0) < lax.broadcasted_iota(jnp.int32, (tokens, tokens), 1)
    rank = mm(hit_f.astype(BF), jnp.where(before, 1.0, 0.0).astype(BF))
    row = (ids_ref[:, tokens:] + 1).astype(F32)
    eye = lax.broadcasted_iota(jnp.int32, (128, 128), 0) == lax.broadcasted_iota(jnp.int32, (128, 128), 1)
    names = []
    for slot in range(capacity):
        name = jnp.sum(jnp.where(hit & (rank == float(slot)), row, 0.0), axis=1, keepdims=True)
        names.append(jnp.sum(jnp.where(eye, name, 0.0), axis=0, keepdims=True) - 1.0)
        for line in range(lines):
            rows_s[slot * devices : (slot + 1) * devices, line * 128 : (line + 1) * 128] = wide_s[
                pl.ds(slot * lines + line, devices, stride=capacity * lines), :
            ].astype(BF)
    names = jnp.concatenate(names, axis=1)
    load.wait()
    keeps = []
    for part in range(rows_own // 128):
        at = slice(part * 128, (part + 1) * 128)
        own = (lax.broadcasted_iota(jnp.int32, (128, 1), 0) + part * 128).astype(F32)
        grad = mm(jnp.where(own == names, 1.0, 0.0).astype(BF), rows_s[...])
        square = jnp.sum(grad * grad, axis=1, keepdims=True) * (1.0 / D)
        old = jnp.sum(jnp.where(eye, accum_ref[part : part + 1, :], 0.0), axis=1, keepdims=True)
        new = old + square
        tab_ref[at, :] = tab_ref[at, :] - LEARN_RATE * grad * lax.rsqrt(new)
        keep = pltpu.make_async_copy(tab_ref.at[at], tab_out.at[at], keep_sem.at[part])
        keep.start()
        keeps.append(keep)
        accum_out[part : part + 1, :] = jnp.sum(jnp.where(eye, new, 0.0), axis=0, keepdims=True)
    for keep in keeps:
        keep.wait()


def update(got, ids, me, table, accum, gattn, ggate, go, capacity, devices):
    rows_own = table.shape[0]
    lines = capacity * D // 128
    like = lambda a: jax.ShapeDtypeStruct(a.shape, a.dtype)
    hbm = pl.BlockSpec(memory_space=pl.ANY)
    accum = accum.reshape(rows_own // 128, 128)
    gattn, ggate, go, table, accum = pl.pallas_call(
        functools.partial(update_kernel, capacity, devices),
        out_shape=(like(gattn), like(ggate), like(go), like(table), like(accum)),
        in_specs=vmem(2) + [pl.BlockSpec(memory_space=pltpu.SMEM)] + vmem(4) + [hbm],
        out_specs=tuple(vmem(3) + [hbm] + vmem(1)),
        scratch_shapes=[
            pltpu.VMEM((devices * lines, 128), F32),
            pltpu.VMEM((capacity * devices, D), BF),
            pltpu.VMEM((rows_own, D), F32),
            pltpu.SemaphoreType.DMA,
            pltpu.SemaphoreType.DMA((rows_own // 128,)),
        ],
        compiler_params=pltpu.CompilerParams(vmem_limit_bytes=VMEM_BYTES),
        name="update",
    )(got, ids, me.reshape(1), accum, gattn, ggate, go, table)
    return gattn, ggate, go, table, accum.reshape(rows_own)


def body(
    layer_input,
    out_grad,
    lengths,
    item_owner,
    item_row,
    w_attn,
    w_gate,
    w_out,
    emb_table,
    row_accum,
):
    seq_count = lax.axis_size("seq")
    dp_count = lax.axis_size("dp")
    devices = seq_count * dp_count
    tokens_dev = layer_input.shape[0]
    pos = tokens_dev * seq_count
    maxlen = 2 * pos // 3
    capacity = max(2, 2 * tokens_dev // devices)
    lens = lengths[0]
    acts = gather(lens, item_owner, item_row, layer_input, out_grad, w_attn, w_gate, w_out, tokens_dev, seq_count, maxlen)
    gattn, ggate, go, got, ids = grads(lens, acts, out_grad, item_owner, seq_count, dp_count, capacity, maxlen)
    me = lax.axis_index("seq") * dp_count + lax.axis_index("dp")
    ids = ids.reshape(devices, 2 * tokens_dev)
    return update(got, ids, me, emb_table, row_accum, gattn, ggate, go, capacity, devices)


def solution(mesh):
    placed = (
        P(("dp", "seq"), None),
        P(("dp", "seq"), None),
        P("dp", None),
        P(("dp", "seq"), None),
        P(("dp", "seq")),
        P(),
        P(),
        P(),
        P(("seq", "dp"), None),
        P(("seq", "dp")),
    )
    return jax.shard_map(
        body,
        mesh=mesh,
        in_specs=placed,
        out_specs=(
            P("dp", "seq"),
            P("dp", "seq"),
            P("dp", "seq"),
            P(("seq", "dp"), None),
            P(("seq", "dp")),
        ),
        check_vma=False,
    )
```
